32 devices in a mesh: grp: 8 (over y, x, core), shard: 4 (over z).
Axes of the slice: x: 2, y: 2, z: 4, core: 2. Of those that a mesh axis runs over, the one named last changes fastest.
Arguments:
- tokens: bfloat16 [2, 8, 512, 2048], P(None, 'grp', 'shard'), may hold values from -6 to 6
- cotangent: bfloat16 [2, 8, 512, 2048], P(None, 'grp', 'shard'), may hold values from -6 to 6
- sequence_lengths: int32 [2, 8, 4], P(None, 'grp'), may hold values from 1 to 448, as said below
- attention_norm_gain: bfloat16 [2048], P('shard'), may hold values from 0.5 to 1.5
- query_matrix: bfloat16 [2048, 2048], P('shard'), may hold values from -0.125 to 0.125
- key_value_matrix: bfloat16 [2048, 1024], P('shard'), may hold values from -0.125 to 0.125
- output_matrix: bfloat16 [2048, 2048], P('shard'), may hold values from -0.375 to 0.375
- adapter_down_maps: bfloat16 [2048, 24], P('shard'), may hold values from -0.125 to 0.125
- adapter_up_query: bfloat16 [8, 2048], P(None, 'shard'), may hold values from -1 to 1
- adapter_up_key_value: bfloat16 [2, 8, 512], P(None, None, 'shard'), may hold values from -1 to 1
- adapter_down_output: bfloat16 [2048, 8], P('shard'), may hold values from -0.125 to 0.125
- adapter_up_output: bfloat16 [8, 2048], P(None, 'shard'), may hold values from -1 to 1
- query_feature_matrices: bfloat16 [32, 64, 64], P('shard'), may hold values from -1.5 to 1.5
- key_feature_matrices: bfloat16 [8, 64, 64], P('shard'), may hold values from -1.5 to 1.5
- feedforward_norm_gain: bfloat16 [2048], P('shard'), may hold values from 0.5 to 1.5
- gate_matrix: bfloat16 [2048, 8192], P('shard'), may hold values from -0.125 to 0.125
- up_matrix: bfloat16 [2048, 8192], P('shard'), may hold values from -0.125 to 0.125
- down_matrix: bfloat16 [8192, 2048], P('shard'), may hold values from -0.125 to 0.125
Outputs:
- output: bfloat16 [2, 8, 512, 2048], P(None, 'grp', 'shard')
- grad_tokens: bfloat16 [2, 8, 512, 2048], P(None, 'grp', 'shard')
- grad_attn_gain: float32 [2048], P('shard')
- grad_query_weight: float32 [2048, 2048], P('shard', 'grp')
- grad_keyvalue_weight: float32 [2048, 1024], P('shard', 'grp')
- grad_output_weight: float32 [2048, 2048], P('shard', 'grp')
- adapter_down_gradient: float32 [2048, 24], P('shard')
- adapter_up_query_gradient: float32 [8, 2048], P(None, 'shard')
- adapter_up_key_value_gradient: float32 [2, 8, 512], P(None, None, 'shard')
- adapter_down_output_gradient: float32 [2048, 8], P('shard')
- adapter_up_output_gradient: float32 [8, 2048], P(None, 'shard')
- grad_feature_query: float32 [32, 64, 64], P('shard')
- grad_feature_key: float32 [8, 64, 64], P('shard')
- grad_ffn_gain: float32 [2048], P('shard')
- grad_gate_weight: float32 [2048, 8192], P('shard', 'grp')
- grad_up_weight: float32 [2048, 8192], P('shard', 'grp')
- grad_down_weight: float32 [8192, 2048], P('shard', 'grp')
The draws below stay inside these ranges and needn't reach their ends.
Inputs may be any that keep to these rules, and one draw needn't show every extreme that they name: `sequence_lengths`: each row lists 4 - 1 document lengths in order, then the padding slots at the stream's end (1 or more); the entries sum to 512, and one document of each row has exactly 448 tokens.
All inputs are finite; a program needn't handle non-finite values.
Results may differ from the reference program's by a relative error of at most 0.02.
Values may be sent and summed in bfloat16 or wider, within the bound.
No kernel may reach another device: no remote copies, remote signals or barrier semaphores. Data moves between devices by JAX's collectives and lax.ppermute only.
A program may use at most 768 MiB of HBM per device.

```python
import jax
import jax.numpy as jnp
from jax import lax

MODEL_WIDTH = 2048
H = 32
KEY_VALUE_HEADS = 8
HEAD_SIZE = 64
FF = 8192
ADAPTER_RANK = 8
WIN = 64
MB = 2
NSEQ = 4
KEY_FEATURES = 512
SEQ_TOK = 512
SHORT = 64
LONG = 448
N_GRP = 8


def draw_sequence_lengths(key, part):
    streams = MB * N_GRP

    def one_stream(stream_key):
        place_key, cut_key = jax.random.split(stream_key)
        long_place = jax.random.randint(place_key, (), 0, NSEQ - 1)
        cut_points = jnp.sort(jax.random.permutation(cut_key, SHORT - 1)[:NSEQ - 2] + 1).astype(jnp.int32)
        bounds = jnp.concatenate([jnp.zeros((1,), jnp.int32), cut_points, jnp.full((1,), SHORT, jnp.int32)])
        shorts = bounds[1:] - bounds[:-1]
        positions = jnp.arange(NSEQ - 1, dtype=jnp.int32)
        before_long = jnp.take(shorts, jnp.clip(positions, 0, NSEQ - 2))
        after_long = jnp.take(shorts, jnp.clip(positions - 1, 0, NSEQ - 2))
        doc_lengths = jnp.where(positions < long_place, before_long, jnp.where(positions == long_place, LONG, after_long))
        return jnp.concatenate([doc_lengths, shorts[NSEQ - 2:]]).astype(jnp.int32)
    stream_keys = jax.random.split(key, streams)
    return jax.vmap(one_stream)(stream_keys).reshape(MB, N_GRP, NSEQ)


def steps_of(own_key, extent, shards, least, top_value):
    loudness = 1.0
    for position, blocks in shards:
        steps = jax.random.uniform(jax.random.fold_in(jax.random.fold_in(own_key, 6), position), (blocks,), jnp.float32, least / len(shards), top_value / len(shards))
        loudness = loudness * jnp.repeat(jnp.exp(steps), extent[position] // blocks).reshape((-1,) + (1,) * (len(extent) - 1 - position))
    return loudness


def normal_values(key, extent, scale, reach, pieces=(), kind=jnp.bfloat16):
    values = scale * jax.random.normal(key, extent, jnp.float32)
    if pieces:
        values = values * steps_of(key, extent, pieces, -0.22, 0.18)
    return jnp.clip(values, -reach, reach).astype(kind)


def setup_inputs(seed: int = 0) -> dict:
    streams_of = jax.random.split(jax.random.key(seed), 19)
    tokens = normal_values(streams_of[0], (MB, N_GRP, SEQ_TOK, MODEL_WIDTH), 1.0, 6.0, ((1, 8), (2, 4)))
    cotangent = normal_values(streams_of[1], (MB, N_GRP, SEQ_TOK, MODEL_WIDTH), 1.0, 6.0, ((1, 8), (2, 4)))
    sequence_lengths = draw_sequence_lengths(jax.random.fold_in(streams_of[18], 71), 0)
    attention_norm_gain = jnp.clip(1.0 + 0.1 * jax.random.normal(streams_of[3], (MODEL_WIDTH,), jnp.float32), 0.5, 1.5).astype(jnp.bfloat16)
    query_matrix = normal_values(streams_of[4], (MODEL_WIDTH, MODEL_WIDTH), MODEL_WIDTH ** -0.5, 0.125, ((0, 4),))
    key_value_matrix = normal_values(streams_of[5], (MODEL_WIDTH, 2 * KEY_FEATURES), MODEL_WIDTH ** -0.5, 0.125, ((0, 4),))
    output_matrix = normal_values(streams_of[6], (MODEL_WIDTH, MODEL_WIDTH), (MODEL_WIDTH // 8) ** -0.5, 0.375, ((0, 4),))
    adapter_down_maps = normal_values(streams_of[7], (MODEL_WIDTH, 3 * ADAPTER_RANK), MODEL_WIDTH ** -0.5, 0.125, ((0, 4),))
    adapter_up_query = normal_values(streams_of[8], (ADAPTER_RANK, MODEL_WIDTH), (4 * ADAPTER_RANK) ** -0.5, 1.0, ((1, 4),))
    adapter_up_key_value = normal_values(streams_of[9], (2, ADAPTER_RANK, KEY_FEATURES), (4 * ADAPTER_RANK) ** -0.5, 1.0, ((2, 4),))
    adapter_down_output = normal_values(streams_of[10], (MODEL_WIDTH, ADAPTER_RANK), MODEL_WIDTH ** -0.5, 0.125, ((0, 4),))
    adapter_up_output = normal_values(streams_of[11], (ADAPTER_RANK, MODEL_WIDTH), (4 * ADAPTER_RANK) ** -0.5, 1.0, ((1, 4),))
    query_feature_matrices = normal_values(streams_of[12], (H, HEAD_SIZE, HEAD_SIZE), (HEAD_SIZE // 4) ** -0.5, 1.5, ((0, 4),))
    key_feature_matrices = normal_values(streams_of[13], (KEY_VALUE_HEADS, HEAD_SIZE, HEAD_SIZE), (HEAD_SIZE // 4) ** -0.5, 1.5, ((0, 4),))
    feedforward_norm_gain = jnp.clip(1.0 + 0.1 * jax.random.normal(streams_of[14], (MODEL_WIDTH,), jnp.float32), 0.5, 1.5).astype(jnp.bfloat16)
    gate_matrix = normal_values(streams_of[15], (MODEL_WIDTH, FF), MODEL_WIDTH ** -0.5, 0.125, ((0, 4),))
    up_matrix = normal_values(streams_of[16], (MODEL_WIDTH, FF), MODEL_WIDTH ** -0.5, 0.125, ((0, 4),))
    down_matrix = normal_values(streams_of[17], (FF, MODEL_WIDTH), (FF // 4) ** -0.5, 0.125, ((0, 4),))
    return dict(tokens=tokens, cotangent=cotangent, sequence_lengths=sequence_lengths, attention_norm_gain=attention_norm_gain, query_matrix=query_matrix, key_value_matrix=key_value_matrix, output_matrix=output_matrix, adapter_down_maps=adapter_down_maps, adapter_up_query=adapter_up_query, adapter_up_key_value=adapter_up_key_value, adapter_down_output=adapter_down_output, adapter_up_output=adapter_up_output, query_feature_matrices=query_feature_matrices, key_feature_matrices=key_feature_matrices, feedforward_norm_gain=feedforward_norm_gain, gate_matrix=gate_matrix, up_matrix=up_matrix, down_matrix=down_matrix)


EPS = 1e-05
ROPE_BASE = 500000.0
HIGH = lax.Precision.HIGHEST

@jax.custom_vjp
def low(v):
    return lax.optimization_barrier(v.astype(jnp.bfloat16)).astype(jnp.float32)

@jax.custom_vjp
def low_back(v):
    return v

def low_keep(v):
    return (low(v), None)

def low_pass(kept, grad):
    return (grad,)

def back_keep(v):
    return (v, None)

def back_low(kept, grad):
    return (low(grad),)
low.defvjp(low_keep, low_pass)
low_back.defvjp(back_keep, back_low)

def rms(vector, gain_vec):
    return vector * lax.rsqrt(lax.optimization_barrier(jnp.mean(vector * vector, axis=-1, keepdims=True)) + EPS) * gain_vec

def highest_product(left_side, right_side):
    return jnp.dot(left_side, right_side, precision=HIGH, preferred_element_type=jnp.float32)

def rotate(tensor, relative):
    half_dim = tensor.shape[-1] // 2
    frequency = ROPE_BASE ** (-jnp.arange(half_dim, dtype=jnp.float32) / half_dim)
    angles = relative.astype(jnp.float32)[:, None] * frequency[None, :]
    cosine = jnp.cos(angles)[:, None, :]
    sine_part = jnp.sin(angles)[:, None, :]
    first_half = tensor[..., :half_dim]
    second = tensor[..., half_dim:]
    return jnp.concatenate([first_half * cosine - second * sine_part, second * cosine + first_half * sine_part], axis=-1)

def locate(lengths_row, offset, amount):
    doc_ends = jnp.cumsum(lengths_row).astype(jnp.int32)
    begins = (doc_ends - lengths_row).astype(jnp.int32)
    positions = (offset + jnp.arange(amount, dtype=jnp.int32)).astype(jnp.int32)
    doc_ids = lax.optimization_barrier(jnp.sum((positions[:, None] >= doc_ends[None, :]).astype(jnp.int32), axis=1)).astype(jnp.int32)
    doc_ids = jnp.where(positions < 0, -1, doc_ids).astype(jnp.int32)
    doc_match = doc_ids[:, None] == jnp.arange(lengths_row.shape[0], dtype=jnp.int32)[None, :]
    relative = (positions - lax.optimization_barrier(jnp.sum(jnp.where(doc_match, begins[None, :], 0), axis=1))).astype(jnp.int32)
    return (positions, doc_ids, relative)

def feature_map(tensor, mixing):
    logits = jnp.einsum('lnd,nde->lne', tensor, mixing, precision=HIGH)
    return low(jnp.concatenate([jax.nn.softmax(logits, axis=-1), jax.nn.softmax(-logits, axis=-1)], axis=-1))

def mixer(queries, keys_all, values_all, carried, carried_total, query_maps, key_maps, window_mask, linear_mask, reuse_mask):
    row_count = queries.shape[0]
    kv_head_count = keys_all.shape[1]
    head_dim = queries.shape[2]
    groups = queries.shape[1] // kv_head_count
    grouped = queries.reshape(row_count, kv_head_count, groups, head_dim)
    phi_query = feature_map(queries, query_maps).reshape(row_count, kv_head_count, groups, 2 * head_dim)
    phi_key = feature_map(keys_all, key_maps)
    scores = jnp.einsum('qgjd,kgd->gjqk', grouped, keys_all, precision=HIGH) * head_dim ** (-0.5)
    row_max = lax.optimization_barrier(jnp.max(jnp.where(window_mask, scores, -1e+30), axis=-1))
    weights = jnp.where(window_mask, jnp.exp(jnp.where(window_mask, scores - row_max[..., None], -10000.0)), 0.0)
    rounded = low(weights)
    kernel = jnp.where(linear_mask, jnp.einsum('qgjf,kgf->gjqk', phi_query, phi_key, precision=HIGH), 0.0)
    damped = jnp.exp(-row_max)
    carried_num = jnp.einsum('qgjf,gfd->gjqd', phi_query, carried, precision=HIGH) * reuse_mask[None, None, :, None]
    carried_den = jnp.einsum('qgjf,gf->gjq', phi_query, carried_total, precision=HIGH) * reuse_mask[None, None, :]
    numerator = jnp.einsum('gjqk,kgd->gjqd', rounded, values_all, precision=HIGH) + damped[..., None] * (jnp.einsum('gjqk,kgd->gjqd', kernel, values_all, precision=HIGH) + carried_num)
    denominator = lax.optimization_barrier(jnp.sum(weights, axis=-1)) + damped * (lax.optimization_barrier(jnp.sum(kernel, axis=-1)) + carried_den)
    mixed = numerator / denominator[..., None]
    return jnp.transpose(mixed, (2, 0, 1, 3)).reshape(row_count, kv_head_count * groups * head_dim)

def stream_forward(token_floats, lengths_row, parameters):
    attention_norm_gain, query_matrix, key_value_matrix, output_matrix, adapter_down_maps, adapter_up_query, adapter_up_key_value, adapter_down_output, adapter_up_output, query_feature_matrices, key_feature_matrices, feedforward_norm_gain, gate_matrix, up_matrix, down_matrix = parameters
    length = token_floats.shape[0]
    adapter_rank_size = adapter_up_query.shape[0]
    key_value_width = adapter_up_key_value.shape[2]
    head_count = query_feature_matrices.shape[0]
    kv_head_count = key_feature_matrices.shape[0]
    head_dim = query_feature_matrices.shape[1]
    positions, doc_ids, relative = locate(lengths_row, 0, length)
    normalized_rows = low(rms(token_floats, attention_norm_gain))
    adapter_middle = low(highest_product(normalized_rows, adapter_down_maps))
    query_linear = low_back(highest_product(normalized_rows, query_matrix) + highest_product(adapter_middle[:, :adapter_rank_size], adapter_up_query))
    key_value_linear = low_back(highest_product(normalized_rows, key_value_matrix) + jnp.concatenate([highest_product(adapter_middle[:, adapter_rank_size:2 * adapter_rank_size], adapter_up_key_value[0]), highest_product(adapter_middle[:, 2 * adapter_rank_size:], adapter_up_key_value[1])], axis=1))
    queries = low(rotate(query_linear.reshape(length, head_count, head_dim), relative))
    keys_all = low(rotate(key_value_linear[:, :key_value_width].reshape(length, kv_head_count, head_dim), relative))
    values_all = low(key_value_linear[:, key_value_width:].reshape(length, kv_head_count, head_dim))
    block_rows = min(512, length)

    def one_block(block_index):
        block_start = (block_index * block_rows).astype(jnp.int32)
        query_block = lax.dynamic_slice_in_dim(queries, block_start, block_rows, 0)
        block_positions = lax.dynamic_slice_in_dim(positions, block_start, block_rows, 0)
        block_docs = lax.dynamic_slice_in_dim(doc_ids, block_start, block_rows, 0)
        same_doc = block_docs[:, None] == doc_ids[None, :]
        distance = block_positions[:, None] - positions[None, :]
        window_mask = same_doc & (distance >= 0) & (distance < WIN)
        linear_mask = same_doc & (distance >= WIN)
        return mixer(query_block, keys_all, values_all, jnp.zeros((kv_head_count, 2 * head_dim, head_dim), jnp.float32), jnp.zeros((kv_head_count, 2 * head_dim), jnp.float32), query_feature_matrices, key_feature_matrices, window_mask, linear_mask, jnp.zeros((block_rows,), jnp.float32))
    attended = lax.map(jax.checkpoint(one_block), jnp.arange(length // block_rows, dtype=jnp.int32))
    context_rows = low_back(low(attended.reshape(length, head_count * head_dim)))
    adapter_output = low(highest_product(context_rows, adapter_down_output))
    branch_output = low_back(highest_product(context_rows, output_matrix) + highest_product(adapter_output, adapter_up_output))
    hidden_rows = token_floats + branch_output
    normed_ffn = low(rms(hidden_rows, feedforward_norm_gain))
    gate_lin = low_back(highest_product(normed_ffn, gate_matrix))
    up_lin = low_back(highest_product(normed_ffn, up_matrix))
    product = low(jax.nn.silu(gate_lin) * up_lin)
    return hidden_rows + low_back(highest_product(product, down_matrix))

def reference(tokens, cotangent, sequence_lengths, attention_norm_gain, query_matrix, key_value_matrix, output_matrix, adapter_down_maps, adapter_up_query, adapter_up_key_value, adapter_down_output, adapter_up_output, query_feature_matrices, key_feature_matrices, feedforward_norm_gain, gate_matrix, up_matrix, down_matrix):
    parameters = tuple((weight_matrix.astype(jnp.float32) for weight_matrix in (attention_norm_gain, query_matrix, key_value_matrix, output_matrix, adapter_down_maps, adapter_up_query, adapter_up_key_value, adapter_down_output, adapter_up_output, query_feature_matrices, key_feature_matrices, feedforward_norm_gain, gate_matrix, up_matrix, down_matrix)))
    streams = MB * N_GRP
    flat_tokens = tokens.reshape(streams, SEQ_TOK, MODEL_WIDTH)
    flat_cot = cotangent.reshape(streams, SEQ_TOK, MODEL_WIDTH)
    flat_lengths = sequence_lengths.reshape(streams, NSEQ)

    def per_stream(totals, stream_item):
        stream_tokens, stream_cot, stream_lengths = stream_item

        def forward(token_floats, *weights):
            return stream_forward(token_floats, stream_lengths, weights)
        result, pullback = jax.vjp(forward, stream_tokens.astype(jnp.float32), *parameters)
        positions, doc_ids, relative = locate(stream_lengths, 0, SEQ_TOK)
        live_mask = (doc_ids < NSEQ - 1).astype(jnp.float32)
        gradients = pullback(stream_cot.astype(jnp.float32) * live_mask[:, None])
        totals = tuple((total + grad for total, grad in zip(totals, gradients[1:])))
        return (totals, (result.astype(jnp.bfloat16), gradients[0].astype(jnp.bfloat16)))
    zero_grads = tuple((jnp.zeros_like(weight_matrix) for weight_matrix in parameters))
    totals, (outputs, token_grads) = lax.scan(per_stream, zero_grads, (flat_tokens, flat_cot, flat_lengths))
    return (outputs.reshape(tokens.shape), token_grads.reshape(tokens.shape), totals[0], totals[1], totals[2], totals[3], totals[4], totals[5], totals[6], totals[7], totals[8], totals[9], totals[10], totals[11], totals[12], totals[13], totals[14])
```

```python
import functools
import jax
import jax.numpy as jnp
from jax import lax
from jax.experimental import pallas as pl
from jax.experimental.pallas import tpu as pltpu
from jax.sharding import PartitionSpec as P

WIN = 64
EPS = 1e-05
ROPE_BASE = 500000.0
BF = jnp.bfloat16
F32 = jnp.float32
QB = 128


def nn(a, b):
    return lax.dot_general(a, b, (((1,), (0,)), ((), ())), preferred_element_type=F32)


def nt(a, b):
    return lax.dot_general(a, b, (((1,), (1,)), ((), ())), preferred_element_type=F32)


def tn(a, b):
    return lax.dot_general(a, b, (((0,), (0,)), ((), ())), preferred_element_type=F32)


def turned(x, cos, sin):
    half = x.shape[0] // 2
    a, b = x[:half], x[half:]
    return jnp.concatenate([a * cos - b * sin, b * cos + a * sin], axis=0)


def features(z):
    half = z.shape[0] // 2

    def one(part):
        e = jnp.exp(part - jnp.max(part, axis=0, keepdims=True))
        return e / jnp.sum(e, axis=0, keepdims=True)

    return jnp.concatenate([one(z[:half]), one(z[half:])], axis=0)


def features_back(p, g):
    half = p.shape[0] // 2

    def one(pp, gg):
        return pp * (gg - jnp.sum(pp * gg, axis=0, keepdims=True))

    return one(p[:half], g[:half]) - one(p[half:], g[half:])


def masks(drow_ref, dcol_ref, q0, k0, count, heads):
    same = dcol_ref[k0 : k0 + count, :] == drow_ref[0:1, q0 : q0 + QB]
    dist = (
        lax.broadcasted_iota(jnp.int32, (count, QB), 1)
        - lax.broadcasted_iota(jnp.int32, (count, QB), 0)
        + (q0 - k0)
    )
    window = jnp.where(same & (dist >= 0) & (dist < WIN), 1.0, 0.0)
    linear = jnp.where(same & (dist >= WIN), 1.0, 0.0)
    return (
        jnp.concatenate([window] * heads, axis=1),
        jnp.concatenate([linear] * heads, axis=1),
    )


def side(parts):
    return jnp.concatenate(parts, axis=1)


def mixed_rows(win_part, lin_part, w0, l1, n):
    pieces = []
    if w0 > 0:
        pieces.append(lin_part[:w0])
    pieces.append(lin_part[w0:l1] + win_part[: l1 - w0])
    pieces.append(win_part[l1 - w0 :])
    return jnp.concatenate(pieces, axis=0)


def fwd_kernel(q_ref, k_ref, v_ref, cos_ref, sin_ref, drow_ref, dcol_ref, fq_ref, fk_ref,
               qo, ko, vo, pqo, pko, atto, ctxo, mo, deno):
    heads = fq_ref.shape[0]
    hd = k_ref.shape[0]
    length = k_ref.shape[1]
    cos, sin = cos_ref[...], sin_ref[...]
    kt = turned(k_ref[...], cos, sin).astype(BF)
    ko[...] = kt
    vt = v_ref[...].astype(BF)
    vo[...] = vt
    keys = jnp.transpose(kt.astype(F32)).astype(BF)
    pkt = features(nn(fk_ref[0], kt)).astype(BF)
    pko[...] = pkt
    pk = jnp.transpose(pkt.astype(F32)).astype(BF)
    for j in range(heads):
        qt = turned(q_ref[j * hd : (j + 1) * hd, :], cos, sin).astype(BF)
        qo[j * hd : (j + 1) * hd, :] = qt
        pqo[j * 2 * hd : (j + 1) * 2 * hd, :] = features(nn(fq_ref[j], qt)).astype(BF)
    for q0 in range(0, length, QB):
        n = q0 + QB
        w0 = max(q0 - WIN, 0)
        l1 = n - WIN
        qcat = side([qo[j * hd : (j + 1) * hd, q0:n] for j in range(heads)])
        pcat = side([pqo[j * 2 * hd : (j + 1) * 2 * hd, q0:n] for j in range(heads)])
        window, _ = masks(drow_ref, dcol_ref, q0, w0, n - w0, heads)
        _, linear = masks(drow_ref, dcol_ref, q0, 0, l1, heads)
        s = nn(keys[w0:n], qcat) * hd ** (-0.5)
        s = jnp.where(window > 0, s, -1e30)
        m = jnp.max(s, axis=0, keepdims=True)
        w = jnp.exp(s - m)
        kd = jnp.where(linear > 0, nn(pk[:l1], pcat) * jnp.exp(-m), 0.0)
        den = jnp.sum(w, axis=0, keepdims=True) + jnp.sum(kd, axis=0, keepdims=True)
        a = mixed_rows(w, kd, w0, l1, n).astype(BF)
        out = nn(vt[:, :n], a) / den
        for j in range(heads):
            cols = slice(j * QB, (j + 1) * QB)
            atto[j * hd : (j + 1) * hd, q0:n] = out[:, cols]
            ctxo[j * hd : (j + 1) * hd, q0:n] = out[:, cols].astype(BF)
            mo[0, j : j + 1, q0:n] = m[:, cols]
            deno[0, j : j + 1, q0:n] = den[:, cols]


def bwd_kernel(q_ref, k_ref, v_ref, pq_ref, pk_ref, att_ref, m_ref, den_ref, g_ref,
               cos_ref, sin_ref, drow_ref, dcol_ref, fq_ref, fk_ref,
               dqo, dko, dvo, dfqo, dfko,
               dq_s, dpq_s, dk_s, dv_s, dpk_s):
    heads = fq_ref.shape[0]
    hd = k_ref.shape[0]
    length = k_ref.shape[1]
    cos, sin = cos_ref[...], sin_ref[...]
    kt = k_ref[...]
    pkt = pk_ref[...]
    keys = jnp.transpose(kt.astype(F32)).astype(BF)
    vals = jnp.transpose(v_ref[...].astype(F32)).astype(BF)
    pk = jnp.transpose(pkt.astype(F32)).astype(BF)
    dk_s[...] = jnp.zeros_like(dk_s)
    dv_s[...] = jnp.zeros_like(dv_s)
    dpk_s[...] = jnp.zeros_like(dpk_s)
    scale = hd ** (-0.5)
    for q0 in range(0, length, QB):
        n = q0 + QB
        w0 = max(q0 - WIN, 0)
        l1 = n - WIN
        qcat = side([q_ref[j * hd : (j + 1) * hd, q0:n] for j in range(heads)])
        pcat = side([pq_ref[j * 2 * hd : (j + 1) * 2 * hd, q0:n] for j in range(heads)])
        gcat = side([g_ref[j * hd : (j + 1) * hd, q0:n] for j in range(heads)])
        acat = side([att_ref[j * hd : (j + 1) * hd, q0:n] for j in range(heads)])
        m = side([m_ref[0, j : j + 1, q0:n] for j in range(heads)])
        rden = 1.0 / side([den_ref[0, j : j + 1, q0:n] for j in range(heads)])
        gf = gcat.astype(F32)
        c = jnp.sum(gf * acat, axis=0, keepdims=True)
        window, _ = masks(drow_ref, dcol_ref, q0, w0, n - w0, heads)
        _, linear = masks(drow_ref, dcol_ref, q0, 0, l1, heads)
        db = (nn(vals[:n], gcat) - c) * rden
        s = nn(keys[w0:n], qcat) * scale
        s = jnp.where(window > 0, s, -1e30)
        w = jnp.exp(s - m)
        d = jnp.exp(-m)
        kd = jnp.where(linear > 0, nn(pk[:l1], pcat) * d, 0.0)
        b = mixed_rows(w, kd, w0, l1, n)
        dv_s[0:n, :] += nt(b.astype(BF), (gf * rden).astype(BF))
        dm = -jnp.sum(b * db, axis=0, keepdims=True)
        top = jnp.where(s == m, 1.0, 0.0)
        ties = jnp.sum(top, axis=0, keepdims=True)
        ds = ((w * db[w0:] + top * (dm / ties)) * scale).astype(BF)
        dqw = tn(keys[w0:n], ds)
        dk_s[w0:n, :] += nt(ds, qcat)
        dker = jnp.where(linear > 0, db[:l1] * d, 0.0).astype(BF)
        dpq = tn(pk[:l1], dker)
        dpk_s[0:l1, :] += nt(dker, pcat)
        for j in range(heads):
            cols = slice(j * QB, (j + 1) * QB)
            dq_s[j * hd : (j + 1) * hd, q0:n] = dqw[:, cols]
            dpq_s[j * 2 * hd : (j + 1) * 2 * hd, q0:n] = dpq[:, cols]
    for j in range(heads):
        rows = slice(j * hd, (j + 1) * hd)
        wide = slice(j * 2 * hd, (j + 1) * 2 * hd)
        dz = features_back(pq_ref[wide, :].astype(F32), dpq_s[wide, :]).astype(BF)
        dfqo[j] = nt(q_ref[rows, :], dz)
        dq = dq_s[rows, :] + nn(fq_ref[j], dz)
        dqo[rows, :] = turned(dq, cos, -sin).astype(BF)
    dz = features_back(pkt.astype(F32), jnp.transpose(dpk_s[...])).astype(BF)
    dfko[0] = nt(kt, dz)
    dk = jnp.transpose(dk_s[...]) + nn(fk_ref[0], dz)
    dko[...] = turned(dk, cos, -sin).astype(BF)
    dvo[...] = jnp.transpose(dv_s[...]).astype(BF)


def attn_specs(nq, nk, hd, length):
    heads = nq // nk
    whole = lambda shape: pl.BlockSpec(shape, lambda g: (0,) * len(shape))
    return dict(
        q=pl.BlockSpec((heads * hd, length), lambda g: (g, 0)),
        k=pl.BlockSpec((hd, length), lambda g: (g, 0)),
        kin=pl.BlockSpec((hd, length), lambda g: (nq + g, 0)),
        vin=pl.BlockSpec((hd, length), lambda g: (nq + nk + g, 0)),
        pq=pl.BlockSpec((2 * heads * hd, length), lambda g: (g, 0)),
        pk=pl.BlockSpec((2 * hd, length), lambda g: (g, 0)),
        row=pl.BlockSpec((1, heads, length), lambda g: (g, 0, 0)),
        angle=whole((hd // 2, length)),
        drow=whole((1, length)),
        dcol=whole((length, QB)),
        fq2=pl.BlockSpec((heads, 2 * hd, hd), lambda g: (g, 0, 0)),
        fk2=pl.BlockSpec((1, 2 * hd, hd), lambda g: (g, 0, 0)),
        fq=pl.BlockSpec((heads, hd, hd), lambda g: (g, 0, 0)),
        fk=pl.BlockSpec((1, hd, hd), lambda g: (g, 0, 0)),
    )


def attn_fwd(proj, cos, sin, drow, dcol, fq2, fk2):
    nq, nk, hd = fq2.shape[0], fk2.shape[0], fq2.shape[2]
    length = proj.shape[1]
    heads = nq // nk
    sp = attn_specs(nq, nk, hd, length)
    sds = jax.ShapeDtypeStruct
    pairs = length * length * nq
    return pl.pallas_call(
        fwd_kernel,
        grid=(nk,),
        in_specs=[sp["q"], sp["kin"], sp["vin"], sp["angle"], sp["angle"], sp["drow"], sp["dcol"],
                  sp["fq2"], sp["fk2"]],
        out_specs=[sp["q"], sp["k"], sp["k"], sp["pq"], sp["pk"], sp["q"], sp["q"], sp["row"], sp["row"]],
        out_shape=[
            sds((nq * hd, length), BF), sds((nk * hd, length), BF), sds((nk * hd, length), BF),
            sds((2 * nq * hd, length), BF), sds((2 * nk * hd, length), BF),
            sds((nq * hd, length), F32), sds((nq * hd, length), BF),
            sds((nk, heads, length), F32), sds((nk, heads, length), F32),
        ],
        cost_estimate=pl.CostEstimate(flops=8 * pairs * hd, bytes_accessed=8 << 20, transcendentals=pairs),
        compiler_params=pltpu.CompilerParams(vmem_limit_bytes=48 << 20),
        name="attn_fwd",
    )(proj, proj, proj, cos, sin, drow, dcol, fq2, fk2)


def attn_bwd(saved, g, cos, sin, drow, dcol, fq, fk):
    qt, kt, vt, pq, pk, att, m, den = saved
    nq, nk, hd = fq.shape[0], fk.shape[0], fq.shape[2]
    length = qt.shape[1]
    heads = nq // nk
    sp = attn_specs(nq, nk, hd, length)
    sds = jax.ShapeDtypeStruct
    pairs = length * length * nq
    return pl.pallas_call(
        bwd_kernel,
        grid=(nk,),
        in_specs=[sp["q"], sp["k"], sp["k"], sp["pq"], sp["pk"], sp["q"], sp["row"], sp["row"], sp["q"],
                  sp["angle"], sp["angle"], sp["drow"], sp["dcol"], sp["fq"], sp["fk"]],
        out_specs=[sp["q"], sp["k"], sp["k"], sp["fq"], sp["fk"]],
        out_shape=[
            sds((nq * hd, length), BF), sds((nk * hd, length), BF), sds((nk * hd, length), BF),
            sds((nq, hd, hd), F32), sds((nk, hd, hd), F32),
        ],
        scratch_shapes=[
            pltpu.VMEM((heads * hd, length), F32),
            pltpu.VMEM((2 * heads * hd, length), F32),
            pltpu.VMEM((length, hd), F32),
            pltpu.VMEM((length, hd), F32),
            pltpu.VMEM((length, 2 * hd), F32),
        ],
        cost_estimate=pl.CostEstimate(flops=20 * pairs * hd, bytes_accessed=8 << 20, transcendentals=pairs),
        compiler_params=pltpu.CompilerParams(vmem_limit_bytes=48 << 20),
        name="attn_bwd",
    )(qt, kt, vt, pq, pk, att, m, den, g, cos, sin, drow, dcol, fq, fk)


def gather_z(x):
    n, i = lax.axis_size("shard"), lax.axis_index("shard")
    ups, downs, up, down = [], [], x, x
    for t in range(1, n):
        up = lax.ppermute(up, "shard", [(k, k + 1) for k in range(t - 1, n - 1)])
        down = lax.ppermute(down, "shard", [(k, k - 1) for k in range(n - t, 0, -1)])
        ups.append(up)
        downs.append(down)
    out = jnp.zeros((n,) + x.shape, x.dtype)
    out = lax.dynamic_update_slice_in_dim(out, x[None], i, 0)
    for t in range(1, n):
        block = jnp.where(i >= t, ups[t - 1], downs[n - t - 1])
        out = lax.dynamic_update_slice_in_dim(out, block[None], (i - t) % n, 0)
    return out


def scatter_z(p):
    n, i = lax.axis_size("shard"), lax.axis_index("shard")
    total = lax.dynamic_index_in_dim(p, i, 0, False).astype(F32)
    for step in (1, -1):
        got = None
        for t in range(1, n):
            block = lax.dynamic_index_in_dim(p, jnp.clip(i + step * (n - t), 0, n - 1), 0, False)
            if got is not None:
                block = (block.astype(F32) + got.astype(F32)).astype(p.dtype)
            if step > 0:
                pairs = [(k, k + 1) for k in range(0, t)]
            else:
                pairs = [(k, k - 1) for k in range(n - 1, n - 1 - t, -1)]
            got = lax.ppermute(block, "shard", pairs)
        if got is not None:
            total = total + got.astype(F32)
    return total


def swap_z(parts):
    n, i = lax.axis_size("shard"), lax.axis_index("shard")
    own = lax.dynamic_index_in_dim(parts, i, 0, True)
    out = lax.dynamic_update_slice_in_dim(jnp.zeros(parts.shape, parts.dtype), own, i, 0)
    for t in range(1, n):
        block = lax.dynamic_index_in_dim(parts, (i + t) % n, 0, True)
        got = lax.ppermute(block, "shard", [(k, (k + t) % n) for k in range(n)])
        out = lax.dynamic_update_slice_in_dim(out, got, (i - t) % n, 0)
    return out


def scatter_small(p):
    return jnp.sum(swap_z(p).astype(F32), axis=0)


def column_weight(pieces):
    n, size, g = lax.axis_size("shard"), lax.axis_size("grp"), lax.axis_index("grp")
    rows = pieces[0].shape[0] // size
    mine = [lax.dynamic_slice_in_dim(w, g * rows, rows, 0) for w in pieces]
    mine = [jnp.swapaxes(w.reshape(rows, n, -1), 0, 1) for w in mine]
    mine = jnp.concatenate(mine, axis=2) if len(mine) > 1 else mine[0]
    swapped = swap_z(mine)
    full = lax.all_gather(swapped, "grp", axis=1)
    return full.reshape(n * size * rows, -1)


def column_grads(grad, widths):
    n, size = lax.axis_size("shard"), lax.axis_size("grp")
    rows = grad.shape[0] // (n * size)
    part = lax.psum_scatter(grad, "grp", scatter_dimension=0, tiled=True)
    part = swap_z(part.reshape(n, rows, grad.shape[1]))
    outs, start = [], 0
    whole = []
    for group in widths:
        cols = []
        for width in group:
            cols.append(jnp.swapaxes(part[:, :, start : start + width], 0, 1).reshape(rows, n * width))
            start += width
        whole.append(jnp.concatenate(cols, axis=1) if len(cols) > 1 else cols[0])
    for w in whole:
        moved = lax.all_to_all(w, "grp", 1, 0, tiled=True)
        outs.append(moved.astype(F32))
    return outs


def group_major(x):
    n, size = lax.axis_size("shard"), lax.axis_size("grp")
    return jnp.swapaxes(x.reshape(x.shape[0], n, size, -1), 1, 2).reshape(x.shape)


def norm_scale(h):
    return lax.rsqrt(jnp.mean(h * h, axis=-1, keepdims=True) + EPS)


def norm_back(h, gain, gn):
    r = norm_scale(h)
    g = gn * gain
    grad = r * g - h * (r * r * r) * jnp.mean(g * h, axis=-1, keepdims=True)
    return grad, jnp.sum(gn * h * r, axis=0)


def body(
    tokens,
    cotangent,
    sequence_lengths,
    attention_norm_gain,
    query_matrix,
    key_value_matrix,
    output_matrix,
    adapter_down_maps,
    adapter_up_query,
    adapter_up_key_value,
    adapter_down_output,
    adapter_up_output,
    query_feature_matrices,
    key_feature_matrices,
    feedforward_norm_gain,
    gate_matrix,
    up_matrix,
    down_matrix,
):
    n, shard, size = lax.axis_size("shard"), lax.axis_index("shard"), lax.axis_size("grp")
    batches, _, rows, width = tokens.shape
    length = n * rows
    share = width // n
    nq, hd = query_feature_matrices.shape[:2]
    nk = key_feature_matrices.shape[0]
    rank = adapter_up_query.shape[0]
    qw, kw = nq * hd, nk * hd
    ffq = down_matrix.shape[0]

    small = jnp.concatenate(
        [
            attention_norm_gain[None],
            feedforward_norm_gain[None],
            adapter_up_output,
            adapter_down_maps.T,
        ],
        axis=0,
    )
    small_full = jnp.swapaxes(gather_z(small), 0, 1).reshape(small.shape[0], width)
    gain_attn = small_full[0].astype(F32)
    gain_ffn = small_full[1].astype(F32)
    up_output = small_full[2 : 2 + rank]
    down_maps_t = small_full[2 + rank :]
    xs = [gather_z(tokens[b, 0]).reshape(length, width) for b in range(batches)]
    half_kv = key_value_matrix.shape[1] // 2
    w_qkv = column_weight(
        [query_matrix, key_value_matrix[:, :half_kv], key_value_matrix[:, half_kv:]]
    )
    w_gate = column_weight([gate_matrix])
    w_up = column_weight([up_matrix])
    cots = [gather_z(cotangent[b, 0]).reshape(length, width) for b in range(batches)]
    zero = jnp.zeros
    u_all = jnp.concatenate(
        [
            jnp.concatenate([adapter_up_query, zero((rank, 2 * kw), BF)], axis=1),
            jnp.concatenate([zero((rank, qw), BF), adapter_up_key_value[0], zero((rank, kw), BF)], axis=1),
            jnp.concatenate([zero((rank, qw + kw), BF), adapter_up_key_value[1]], axis=1),
        ],
        axis=0,
    )

    ends = jnp.cumsum(sequence_lengths[:, 0], axis=1)
    begins = ends - sequence_lengths[:, 0]
    where = jnp.arange(length, dtype=jnp.int32)
    docs = jnp.sum((where[None, :, None] >= ends[:, None, :]).astype(jnp.int32), axis=2)
    relative = where[None] - jnp.max(
        jnp.where(where[None, :, None] >= begins[:, None, :], begins[:, None, :], 0), axis=2
    )
    lives = docs < sequence_lengths.shape[2] - 1
    freq = ROPE_BASE ** (-jnp.arange(hd // 2, dtype=F32) / (hd // 2))
    angles = freq[None, :, None] * relative.astype(F32)[:, None, :]
    cos_all, sin_all = jnp.cos(angles), jnp.sin(angles)

    def doubled(f):
        return jnp.swapaxes(jnp.concatenate([f, -f], axis=2), 1, 2)

    fq2, fk2 = doubled(query_feature_matrices), doubled(key_feature_matrices)

    keep = []
    outputs = []
    for b in range(batches):
        x = xs[b].astype(F32)
        normed = (x * norm_scale(x) * gain_attn).astype(BF)
        mid = nt(normed, down_maps_t).astype(BF)
        proj = lax.dot_general(w_qkv, normed, (((0,), (1,)), ((), ())), preferred_element_type=F32)
        proj = proj + lax.dot_general(u_all, mid, (((0,), (1,)), ((), ())), preferred_element_type=F32)
        place = (
            cos_all[b],
            sin_all[b],
            docs[b][None],
            jnp.broadcast_to(docs[b][:, None], (length, QB)),
        )
        qt, kt, vt, pq, pk, att, ctx, m, den = attn_fwd(proj, *place, fq2, fk2)
        lora_own = scatter_small(tn(ctx, adapter_down_output).reshape(n, rows, rank)).astype(BF)
        branch = scatter_z(tn(ctx, output_matrix).astype(BF).reshape(n, rows, width))
        x_own = tokens[b, 0].astype(F32)
        hidden = x_own + branch + nn(lora_own, up_output)
        normed_own = (hidden * norm_scale(hidden) * gain_ffn).astype(BF)
        normed_ffn = gather_z(normed_own).reshape(length, width)
        gate = nn(normed_ffn, w_gate)
        up = nn(normed_ffn, w_up)
        product = (gate * jax.nn.sigmoid(gate) * up).astype(BF)
        ffn = scatter_z(nn(product, down_matrix).astype(BF).reshape(n, rows, width))
        outputs.append((hidden + ffn).astype(BF))
        keep.append(
            dict(normed=normed, mid=mid, saved=(qt, kt, vt, pq, pk, att, m, den), ctx=ctx, place=place,
                 lora=lora_own, x=x_own, hidden=hidden, nf=normed_ffn, gate=gate, up=up, product=product)
        )
    token_grads = []
    for b in range(batches):
        k = keep[b]
        live = lives[b]
        gm = jnp.where(live[:, None], cots[b], 0).astype(BF)
        live_own = lax.dynamic_slice_in_dim(live, shard * rows, rows, 0)
        grad_out = jnp.where(live_own[:, None], cotangent[b, 0], 0).astype(F32)
        gp = nt(gm, down_matrix)
        sg = jax.nn.sigmoid(k["gate"])
        dgate = (gp * k["up"] * (sg + k["gate"] * sg * (1.0 - sg))).astype(BF)
        dup = (gp * k["gate"] * sg).astype(BF)
        gnf = scatter_z((nt(dgate, w_gate) + nt(dup, w_up)).astype(BF).reshape(n, rows, width))
        back, ffn_gain = norm_back(k["hidden"], gain_ffn, gnf)
        grad_hidden = grad_out + back
        gb_own = grad_hidden.astype(BF)
        gb = gather_z(gb_own).reshape(length, width)
        glo = nt(gb, up_output)
        gctx = nt(output_matrix, gb) + nt(adapter_down_output.astype(F32), glo)
        dq, dk, dv, dfq, dfk = attn_bwd(
            k["saved"], gctx.astype(BF), *k["place"], query_feature_matrices, key_feature_matrices
        )
        dqkv = jnp.concatenate([dq, dk, dv], axis=0)
        glm = tn(dqkv, u_all.T)
        gn = lax.dot_general(dqkv, w_qkv, (((0,), (1,)), ((), ())), preferred_element_type=F32)
        gn = gn + nn(glm, down_maps_t.astype(F32))
        gn = scatter_z(gn.astype(BF).reshape(n, rows, width))
        back, attn_gain = norm_back(k["x"], gain_attn, gn)
        token_grads.append((grad_hidden + back).astype(BF))
        k.update(gm=gm, dgate=dgate, dup=dup, gb=gb, glo=glo, dqkv=dqkv, glm=glm, dfq=dfq, dfk=dfk,
                 ffn_gain=ffn_gain, attn_gain=attn_gain, up_out=tn(k["lora"], gb_own))

    def both(name, axis=0):
        return jnp.concatenate([k[name] for k in keep], axis=axis)

    def added(name):
        return functools.reduce(lambda a, c: a + c, [k[name] for k in keep])

    nf = group_major(both("nf"))
    (grad_gate,) = column_grads(tn(nf, both("dgate")).astype(BF), [[ffq]])
    (grad_up,) = column_grads(tn(nf, both("dup")).astype(BF), [[ffq]])
    grad_down = lax.psum_scatter(
        tn(both("product"), both("gm")).astype(BF), "grp", scatter_dimension=1, tiled=True
    ).astype(F32)
    ctx = both("ctx", 1)
    grad_output = lax.psum_scatter(
        nn(ctx, both("gb")).astype(BF), "grp", scatter_dimension=1, tiled=True
    ).astype(F32)
    normed = both("normed")
    dqkv = both("dqkv", 1)
    dw = lax.dot_general(group_major(normed), dqkv, (((0,), (1,)), ((), ())), preferred_element_type=F32)
    grad_query, grad_kv = column_grads(dw.astype(BF), [[qw], [kw, kw]])

    glm = both("glm")
    down_maps_grad = tn(normed.astype(F32), glm)
    ups = lax.dot_general(both("mid"), dqkv, (((0,), (1,)), ((), ())), preferred_element_type=F32)
    down_out_grad = nn(ctx.astype(F32), both("glo"))
    spread = [
        added("attn_gain").reshape(n, share),
        added("ffn_gain").reshape(n, share),
        down_maps_grad.reshape(n, share * 3 * rank),
        jnp.swapaxes(added("up_out").reshape(rank, n, share), 0, 1).reshape(n, rank * share),
    ]
    lined = scatter_small(jnp.concatenate(spread, axis=1).astype(BF))
    local = [
        ups[:rank, :qw].reshape(-1),
        ups[rank : 2 * rank, qw : qw + kw].reshape(-1),
        ups[2 * rank :, qw + kw :].reshape(-1),
        down_out_grad.reshape(-1),
        added("dfq").reshape(-1),
        added("dfk").reshape(-1),
    ]
    flat = lax.psum(jnp.concatenate([lined] + local).astype(BF), "grp").astype(F32)
    shapes = [
        (share,),
        (share,),
        (share, 3 * rank),
        (rank, share),
        (rank, qw),
        (rank, kw),
        (rank, kw),
        (qw, rank),
        (nq, hd, hd),
        (nk, hd, hd),
    ]
    got, start = [], 0
    for shape in shapes:
        count = 1
        for extent in shape:
            count *= extent
        got.append(flat[start : start + count].reshape(shape))
        start += count
    g_attn, g_ffn, g_down_maps, g_up_out, g_up_q, g_up_k, g_up_v, g_down_out, g_fq, g_fk = got
    return (
        jnp.stack(outputs)[:, None],
        jnp.stack(token_grads)[:, None],
        g_attn,
        grad_query,
        grad_kv,
        grad_output,
        g_down_maps,
        g_up_q,
        jnp.stack([g_up_k, g_up_v]),
        g_down_out,
        g_up_out,
        g_fq,
        g_fk,
        g_ffn,
        grad_gate,
        grad_up,
        grad_down,
    )


def solution(mesh):
    placed = (
        P(None, "grp", "shard", None),
        P(None, "grp", "shard", None),
        P(None, "grp", None),
        P("shard"),
        P("shard", None),
        P("shard", None),
        P("shard", None),
        P("shard", None),
        P(None, "shard"),
        P(None, None, "shard"),
        P("shard", None),
        P(None, "shard"),
        P("shard", None, None),
        P("shard", None, None),
        P("shard"),
        P("shard", None),
        P("shard", None),
        P("shard", None),
    )
    return jax.shard_map(
        body,
        mesh=mesh,
        in_specs=placed,
        out_specs=(
            P(None, "grp", "shard", None),
            P(None, "grp", "shard", None),
            P("shard"),
            P("shard", "grp"),
            P("shard", "grp"),
            P("shard", "grp"),
            P("shard", None),
            P(None, "shard"),
            P(None, None, "shard"),
            P("shard", None),
            P(None, "shard"),
            P("shard", None, None),
            P("shard", None, None),
            P("shard"),
            P("shard", "grp"),
            P("shard", "grp"),
            P("shard", "grp"),
        ),
        check_vma=False,
    )
```

```python
import functools
import jax
import jax.numpy as jnp
from jax import lax
from jax.experimental import pallas as pl
from jax.experimental.pallas import tpu as pltpu
from jax.sharding import PartitionSpec as P

WIN = 64
EPS = 1e-05
ROPE_BASE = 500000.0
BF = jnp.bfloat16
F32 = jnp.float32
QB = 128


def nn(a, b):
    return lax.dot_general(a, b, (((1,), (0,)), ((), ())), preferred_element_type=F32)


def nt(a, b):
    return lax.dot_general(a, b, (((1,), (1,)), ((), ())), preferred_element_type=F32)


def tn(a, b):
    return lax.dot_general(a, b, (((0,), (0,)), ((), ())), preferred_element_type=F32)


def turned(x, cos, sin):
    half = x.shape[0] // 2
    a, b = x[:half], x[half:]
    return jnp.concatenate([a * cos - b * sin, b * cos + a * sin], axis=0)


def features(z):
    half = z.shape[0] // 2

    def one(part):
        e = jnp.exp(part - jnp.max(part, axis=0, keepdims=True))
        return e / jnp.sum(e, axis=0, keepdims=True)

    return jnp.concatenate([one(z[:half]), one(z[half:])], axis=0)


def features_back(p, g):
    half = p.shape[0] // 2

    def one(pp, gg):
        return pp * (gg - jnp.sum(pp * gg, axis=0, keepdims=True))

    return one(p[:half], g[:half]) - one(p[half:], g[half:])


def masks(drow_ref, dcol_ref, q0, k0, count, heads):
    same = dcol_ref[k0 : k0 + count, :] == drow_ref[0:1, q0 : q0 + QB]
    dist = (
        lax.broadcasted_iota(jnp.int32, (count, QB), 1)
        - lax.broadcasted_iota(jnp.int32, (count, QB), 0)
        + (q0 - k0)
    )
    window = jnp.where(same & (dist >= 0) & (dist < WIN), 1.0, 0.0)
    linear = jnp.where(same & (dist >= WIN), 1.0, 0.0)
    return (
        jnp.concatenate([window] * heads, axis=1),
        jnp.concatenate([linear] * heads, axis=1),
    )


def side(parts):
    return jnp.concatenate(parts, axis=1)


def mixed_rows(win_part, lin_part, w0, l1, n):
    pieces = []
    if w0 > 0:
        pieces.append(lin_part[:w0])
    pieces.append(lin_part[w0:l1] + win_part[: l1 - w0])
    pieces.append(win_part[l1 - w0 :])
    return jnp.concatenate(pieces, axis=0)


def block_pick(me_ref, place, blocks):
    me, n, per = me_ref[0], me_ref[1], me_ref[2]
    source = lax.rem(me - place // per + n, n) * per + lax.rem(place, per)
    out = blocks[0]
    for m in range(1, len(blocks)):
        out = jnp.where(source == m, blocks[m], out)
    return out


def lanes(ref, rows=slice(None)):
    return [ref[rows, m * QB : (m + 1) * QB] for m in range(ref.shape[1] // QB)]


def fwd_kernel(me_ref, q_ref, k_ref, v_ref, cos_ref, sin_ref, drow_ref, dcol_ref, fq_ref, fk_ref,
               qo, ko, vo, pqo, pko, atto, ctxo, mo, deno):
    heads = fq_ref.shape[0]
    hd = k_ref.shape[0]
    length = k_ref.shape[1]
    for block in range(length // QB):
        cols = slice(block * QB, (block + 1) * QB)
        cos, sin = cos_ref[:, cols], sin_ref[:, cols]
        ko[:, cols] = turned(block_pick(me_ref, block, lanes(k_ref)), cos, sin).astype(BF)
        vo[:, cols] = block_pick(me_ref, block, lanes(v_ref)).astype(BF)
        for j in range(heads):
            rows = slice(j * hd, (j + 1) * hd)
            qo[rows, cols] = turned(block_pick(me_ref, block, lanes(q_ref, rows)), cos, sin).astype(BF)
    kt = ko[...]
    vt = vo[...]
    keys = jnp.transpose(kt.astype(F32)).astype(BF)
    pkt = features(nn(fk_ref[0], kt)).astype(BF)
    pko[...] = pkt
    pk = jnp.transpose(pkt.astype(F32)).astype(BF)
    for j in range(heads):
        qt = qo[j * hd : (j + 1) * hd, :]
        pqo[j * 2 * hd : (j + 1) * 2 * hd, :] = features(nn(fq_ref[j], qt)).astype(BF)
    for q0 in range(0, length, QB):
        n = q0 + QB
        w0 = max(q0 - WIN, 0)
        l1 = n - WIN
        qcat = side([qo[j * hd : (j + 1) * hd, q0:n] for j in range(heads)])
        pcat = side([pqo[j * 2 * hd : (j + 1) * 2 * hd, q0:n] for j in range(heads)])
        window, _ = masks(drow_ref, dcol_ref, q0, w0, n - w0, heads)
        _, linear = masks(drow_ref, dcol_ref, q0, 0, l1, heads)
        s = nn(keys[w0:n], qcat) * hd ** (-0.5)
        s = jnp.where(window > 0, s, -1e30)
        m = jnp.max(s, axis=0, keepdims=True)
        w = jnp.exp(s - m)
        kd = jnp.where(linear > 0, nn(pk[:l1], pcat) * jnp.exp(-m), 0.0)
        den = jnp.sum(w, axis=0, keepdims=True) + jnp.sum(kd, axis=0, keepdims=True)
        a = mixed_rows(w, kd, w0, l1, n).astype(BF)
        out = nn(vt[:, :n], a) / den
        for j in range(heads):
            cols = slice(j * QB, (j + 1) * QB)
            atto[j * hd : (j + 1) * hd, q0:n] = out[:, cols]
            mo[0, j : j + 1, q0:n] = m[:, cols]
            deno[0, j : j + 1, q0:n] = den[:, cols]
    for place in range(length // QB):
        ctxo[:, place * QB : (place + 1) * QB] = block_pick(me_ref, place, lanes(atto)).astype(BF)


def bwd_kernel(me_ref, q_ref, k_ref, v_ref, pq_ref, pk_ref, att_ref, m_ref, den_ref, g_ref,
               cos_ref, sin_ref, drow_ref, dcol_ref, fq_ref, fk_ref,
               dqo, dko, dvo, dfqo, dfko,
               dq_s, dpq_s, dk_s, dv_s, dpk_s):
    heads = fq_ref.shape[0]
    hd = k_ref.shape[0]
    length = k_ref.shape[1]
    cos, sin = cos_ref[...], sin_ref[...]
    kt = k_ref[...]
    pkt = pk_ref[...]
    keys = jnp.transpose(kt.astype(F32)).astype(BF)
    vals = jnp.transpose(v_ref[...].astype(F32)).astype(BF)
    pk = jnp.transpose(pkt.astype(F32)).astype(BF)

    def store(ref, rows, value):
        for place in range(length // QB):
            block = block_pick(me_ref, place, [value[:, p : p + QB] for p in range(0, length, QB)])
            ref[rows, place * QB : (place + 1) * QB] = block.astype(BF)

    dk_s[...] = jnp.zeros_like(dk_s)
    dv_s[...] = jnp.zeros_like(dv_s)
    dpk_s[...] = jnp.zeros_like(dpk_s)
    scale = hd ** (-0.5)
    for q0 in range(0, length, QB):
        n = q0 + QB
        w0 = max(q0 - WIN, 0)
        l1 = n - WIN
        qcat = side([q_ref[j * hd : (j + 1) * hd, q0:n] for j in range(heads)])
        pcat = side([pq_ref[j * 2 * hd : (j + 1) * 2 * hd, q0:n] for j in range(heads)])
        gcat = block_pick(
            me_ref, q0 // QB,
            [side([g_ref[j * hd : (j + 1) * hd, p : p + QB] for j in range(heads)]).astype(F32)
             for p in range(0, length, QB)],
        ).astype(BF)
        acat = side([att_ref[j * hd : (j + 1) * hd, q0:n] for j in range(heads)])
        m = side([m_ref[0, j : j + 1, q0:n] for j in range(heads)])
        rden = 1.0 / side([den_ref[0, j : j + 1, q0:n] for j in range(heads)])
        gf = gcat.astype(F32)
        c = jnp.sum(gf * acat, axis=0, keepdims=True)
        window, _ = masks(drow_ref, dcol_ref, q0, w0, n - w0, heads)
        _, linear = masks(drow_ref, dcol_ref, q0, 0, l1, heads)
        db = (nn(vals[:n], gcat) - c) * rden
        s = nn(keys[w0:n], qcat) * scale
        s = jnp.where(window > 0, s, -1e30)
        w = jnp.exp(s - m)
        d = jnp.exp(-m)
        kd = jnp.where(linear > 0, nn(pk[:l1], pcat) * d, 0.0)
        b = mixed_rows(w, kd, w0, l1, n)
        dv_s[0:n, :] += nt(b.astype(BF), (gf * rden).astype(BF))
        dm = -jnp.sum(b * db, axis=0, keepdims=True)
        top = jnp.where(s == m, 1.0, 0.0)
        ties = jnp.sum(top, axis=0, keepdims=True)
        ds = ((w * db[w0:] + top * (dm / ties)) * scale).astype(BF)
        dqw = tn(keys[w0:n], ds)
        dk_s[w0:n, :] += nt(ds, qcat)
        dker = jnp.where(linear > 0, db[:l1] * d, 0.0).astype(BF)
        dpq = tn(pk[:l1], dker)
        dpk_s[0:l1, :] += nt(dker, pcat)
        for j in range(heads):
            cols = slice(j * QB, (j + 1) * QB)
            dq_s[j * hd : (j + 1) * hd, q0:n] = dqw[:, cols]
            dpq_s[j * 2 * hd : (j + 1) * 2 * hd, q0:n] = dpq[:, cols]
    for j in range(heads):
        rows = slice(j * hd, (j + 1) * hd)
        wide = slice(j * 2 * hd, (j + 1) * 2 * hd)
        dz = features_back(pq_ref[wide, :].astype(F32), dpq_s[wide, :]).astype(BF)
        dfqo[j] = nt(q_ref[rows, :], dz)
        store(dqo, rows, turned(dq_s[rows, :] + nn(fq_ref[j], dz), cos, -sin))
    dz = features_back(pkt.astype(F32), jnp.transpose(dpk_s[...])).astype(BF)
    dfko[0] = nt(kt, dz)
    dk = jnp.transpose(dk_s[...]) + nn(fk_ref[0], dz)
    store(dko, slice(None), turned(dk, cos, -sin))
    store(dvo, slice(None), jnp.transpose(dv_s[...]))


def attn_specs(nq, nk, hd, length):
    heads = nq // nk
    whole = lambda shape: pl.BlockSpec(shape, lambda g: (0,) * len(shape))
    return dict(
        me=pl.BlockSpec(memory_space=pltpu.SMEM),
        q=pl.BlockSpec((heads * hd, length), lambda g: (g, 0)),
        k=pl.BlockSpec((hd, length), lambda g: (g, 0)),
        kin=pl.BlockSpec((hd, length), lambda g: (nq + g, 0)),
        vin=pl.BlockSpec((hd, length), lambda g: (nq + nk + g, 0)),
        pq=pl.BlockSpec((2 * heads * hd, length), lambda g: (g, 0)),
        pk=pl.BlockSpec((2 * hd, length), lambda g: (g, 0)),
        row=pl.BlockSpec((1, heads, length), lambda g: (g, 0, 0)),
        angle=whole((hd // 2, length)),
        drow=whole((1, length)),
        dcol=whole((length, QB)),
        fq2=pl.BlockSpec((heads, 2 * hd, hd), lambda g: (g, 0, 0)),
        fk2=pl.BlockSpec((1, 2 * hd, hd), lambda g: (g, 0, 0)),
        fq=pl.BlockSpec((heads, hd, hd), lambda g: (g, 0, 0)),
        fk=pl.BlockSpec((1, hd, hd), lambda g: (g, 0, 0)),
    )


def attn_fwd(me, proj, cos, sin, drow, dcol, fq2, fk2):
    nq, nk, hd = fq2.shape[0], fk2.shape[0], fq2.shape[2]
    length = proj.shape[1]
    heads = nq // nk
    sp = attn_specs(nq, nk, hd, length)
    sds = jax.ShapeDtypeStruct
    pairs = length * length * nq
    return pl.pallas_call(
        fwd_kernel,
        grid=(nk,),
        in_specs=[sp["me"], sp["q"], sp["kin"], sp["vin"], sp["angle"], sp["angle"], sp["drow"], sp["dcol"],
                  sp["fq2"], sp["fk2"]],
        out_specs=[sp["q"], sp["k"], sp["k"], sp["pq"], sp["pk"], sp["q"], sp["q"], sp["row"], sp["row"]],
        out_shape=[
            sds((nq * hd, length), BF), sds((nk * hd, length), BF), sds((nk * hd, length), BF),
            sds((2 * nq * hd, length), BF), sds((2 * nk * hd, length), BF),
            sds((nq * hd, length), F32), sds((nq * hd, length), BF),
            sds((nk, heads, length), F32), sds((nk, heads, length), F32),
        ],
        cost_estimate=pl.CostEstimate(flops=8 * pairs * hd, bytes_accessed=8 << 20, transcendentals=pairs),
        compiler_params=pltpu.CompilerParams(vmem_limit_bytes=48 << 20),
        name="attn_fwd",
    )(me, proj, proj, proj, cos, sin, drow, dcol, fq2, fk2)


def attn_bwd(me, saved, g, cos, sin, drow, dcol, fq, fk):
    qt, kt, vt, pq, pk, att, m, den = saved
    nq, nk, hd = fq.shape[0], fk.shape[0], fq.shape[2]
    length = qt.shape[1]
    heads = nq // nk
    sp = attn_specs(nq, nk, hd, length)
    sds = jax.ShapeDtypeStruct
    pairs = length * length * nq
    return pl.pallas_call(
        bwd_kernel,
        grid=(nk,),
        in_specs=[sp["me"], sp["q"], sp["k"], sp["k"], sp["pq"], sp["pk"], sp["q"], sp["row"], sp["row"], sp["q"],
                  sp["angle"], sp["angle"], sp["drow"], sp["dcol"], sp["fq"], sp["fk"]],
        out_specs=[sp["q"], sp["k"], sp["k"], sp["fq"], sp["fk"]],
        out_shape=[
            sds((nq * hd, length), BF), sds((nk * hd, length), BF), sds((nk * hd, length), BF),
            sds((nq, hd, hd), F32), sds((nk, hd, hd), F32),
        ],
        scratch_shapes=[
            pltpu.VMEM((heads * hd, length), F32),
            pltpu.VMEM((2 * heads * hd, length), F32),
            pltpu.VMEM((length, hd), F32),
            pltpu.VMEM((length, hd), F32),
            pltpu.VMEM((length, 2 * hd), F32),
        ],
        cost_estimate=pl.CostEstimate(flops=20 * pairs * hd, bytes_accessed=8 << 20, transcendentals=pairs),
        compiler_params=pltpu.CompilerParams(vmem_limit_bytes=48 << 20),
        name="attn_bwd",
    )(me, qt, kt, vt, pq, pk, att, m, den, g, cos, sin, drow, dcol, fq, fk)


def ffn_kernel(x_ref, g_ref, wg_ref, wu_ref, wd_ref, out_ref, back_ref, prod_ref, dgate_ref, dup_ref,
               out_acc, back_acc):
    step = pl.program_id(1)
    x = x_ref[...]
    gate = nn(x, wg_ref[...])
    up = nn(x, wu_ref[...])
    sg = jax.nn.sigmoid(gate)
    act = gate * sg
    prod = (act * up).astype(BF)
    prod_ref[...] = prod
    gp = nt(g_ref[...], wd_ref[...])
    dgate = (gp * up * (sg + act * (1.0 - sg))).astype(BF)
    dup = (gp * act).astype(BF)
    dgate_ref[...] = dgate
    dup_ref[...] = dup
    out = nn(prod, wd_ref[...])
    back = nt(dgate, wg_ref[...]) + nt(dup, wu_ref[...])

    @pl.when(step == 0)
    def _():
        out_acc[...] = out
        back_acc[...] = back

    @pl.when(step > 0)
    def _():
        out_acc[...] += out
        back_acc[...] += back

    @pl.when(step == pl.num_programs(1) - 1)
    def _():
        out_ref[...] = out_acc[...].astype(BF)
        back_ref[...] = back_acc[...].astype(BF)


def ffn_both(x, g, w_both, wd):
    length, width = x.shape
    ff = wd.shape[0]
    tm, tf = min(512, length), min(512, ff)
    rows = pl.BlockSpec((tm, width), lambda i, j: (i, 0))
    cols = pl.BlockSpec((width, tf), lambda i, j: (0, j))
    tile = pl.BlockSpec((tm, tf), lambda i, j: (i, j))
    more = pl.BlockSpec((width, tf), lambda i, j: (0, ff // tf + j))
    sds = jax.ShapeDtypeStruct
    return pl.pallas_call(
        ffn_kernel,
        grid=(length // tm, ff // tf),
        in_specs=[rows, rows, cols, more, pl.BlockSpec((tf, width), lambda i, j: (j, 0))],
        out_specs=[rows, rows, tile, tile, tile],
        out_shape=[sds((length, width), BF)] * 2 + [sds((length, ff), BF)] * 3,
        scratch_shapes=[pltpu.VMEM((tm, width), F32)] * 2,
        cost_estimate=pl.CostEstimate(
            flops=12 * length * width * ff, bytes_accessed=6 * width * ff, transcendentals=length * ff
        ),
        compiler_params=pltpu.CompilerParams(vmem_limit_bytes=56 << 20),
        name="ffn_both",
    )(x, g, w_both, w_both, wd)


def weight_grad(pairs, x_dim, y_dim, by_rows, side_index, others=None, add=None):
    x0, y0 = pairs[0]
    tokens, rows, cols = x0.shape[x_dim], x0.shape[1 - x_dim], y0.shape[1 - y_dim]
    groups = lax.axis_size("grp")
    half = groups // 2
    count = len(pairs)
    extra = 0 if add is None else 1

    def kernel(side_ref, *refs):
        out = refs[-1]

        def cut(ref, dim, size, which):
            place = slice(which * size, (which + 1) * size)
            return ref[:, place] if dim == 0 else ref[place, :]

        for which in range(2):

            @pl.when(side_ref[0] == which)
            def _(which=which):
                total = None
                for k in range(count):
                    x, y = refs[2 * k], refs[2 * k + 1]
                    x = cut(x, x_dim, tm, which) if by_rows else x[...]
                    y = y[...] if by_rows else cut(y, y_dim, tn, which)
                    part = lax.dot_general(x, y, (((x_dim,), (y_dim,)), ((), ())), preferred_element_type=F32)
                    total = part if total is None else total + part
                total = total.reshape(out.shape)
                if extra:
                    total = total + refs[2 * count][...].astype(F32)
                out[...] = total.astype(BF)

    def spec(dim, size, where):
        if dim == 0:
            return pl.BlockSpec((tokens, size), lambda i, j: (0, where(i, j)))
        return pl.BlockSpec((size, tokens), lambda i, j: (where(i, j), 0))

    if by_rows:
        shards = lax.axis_size("shard")
        part = rows // shards // groups
        tm, tn = half * part, cols
        grid = (shards, 1)
        xs = spec(x_dim, 2 * tm, lambda i, j: i)
        ys = spec(y_dim, tn, lambda i, j: j)
        shape = (half, shards, part, cols)
        block = pl.BlockSpec((half, 1, part, tn), lambda i, j: (0, i, 0, j))
    else:
        tm, tn = min(1024, rows), cols // groups
        grid = (rows // tm, half)
        xs = spec(x_dim, tm, lambda i, j: i)
        ys = spec(y_dim, 2 * tn, lambda i, j: j)
        shape = (half, rows, tn)
        block = pl.BlockSpec((1, tm, tn), lambda i, j: (j, i, 0))
    return pl.pallas_call(
        kernel,
        grid=grid,
        in_specs=[pl.BlockSpec(memory_space=pltpu.SMEM)] + [xs, ys] * count + [block] * extra,
        out_specs=block,
        out_shape=jax.ShapeDtypeStruct(shape, BF),
        cost_estimate=pl.CostEstimate(
            flops=count * tokens * rows * cols, bytes_accessed=rows * cols, transcendentals=0
        ),
        compiler_params=pltpu.CompilerParams(vmem_limit_bytes=48 << 20),
        name="weight_grad",
    )(side_index, *[a for pair in pairs for a in pair], *([add] if extra else []))


def tie(x, *others):
    return lax.optimization_barrier((x,) + others)[0] if others else x


def gather_small(x):
    SCOPE[0] = "small"
    n = lax.axis_size("shard")
    x = now(x)
    return [x] + [permute(x, "shard", [(k, (k + t) % n) for k in range(n)]) for t in range(1, n)]


SCOPE = ["start"]


def permute(x, axis, pairs):
    with jax.named_scope(SCOPE[0]):
        return lax.ppermute(x, axis, pairs)


class Clock:
    before, here = [], []


def now(x):
    return tie(x, *Clock.before)


def put(*values):
    Clock.here.extend(values)


def tick():
    Clock.before, Clock.here = Clock.here, []


class Gather:
    def __init__(self, x, name="gather"):
        self.name = name
        self.x, self.up, self.down = x, x, x
        self.ups, self.downs = [], []

    def step(self):
        n, t = lax.axis_size("shard"), len(self.ups) + 1
        if t >= n:
            return
        SCOPE[0] = self.name + str(t)
        self.up = permute(now(self.up), "shard", [(k, k + 1) for k in range(t - 1, n - 1)])
        self.down = permute(now(self.down), "shard", [(k, k - 1) for k in range(n - t, 0, -1)])
        self.ups.append(self.up)
        self.downs.append(self.down)
        put(self.up, self.down)

    def last(self):
        while len(self.ups) + 1 < lax.axis_size("shard"):
            self.step()

    def result(self):
        n, i = lax.axis_size("shard"), lax.axis_index("shard")
        blocks = [jnp.where(i >= t, self.ups[t - 1], self.downs[n - t - 1]) for t in range(1, n)]
        return jnp.concatenate([self.x] + blocks)


class Scatter:
    def __init__(self, x, name="scatter"):
        self.name = name
        n = lax.axis_size("shard")
        rows = x.shape[0] // n
        self.parts = [x[k * rows : (k + 1) * rows] for k in range(n)]
        self.got, self.t = {1: None, -1: None}, 0

    def step(self):
        n, t = len(self.parts), self.t + 1
        if t >= n:
            return
        SCOPE[0] = self.name + str(t)
        self.t = t
        for way in (1, -1):
            block = now(self.parts[t if way > 0 else n - t])
            if self.got[way] is not None:
                block = (block.astype(F32) + self.got[way].astype(F32)).astype(block.dtype)
            if way > 0:
                pairs = [(k, k + 1) for k in range(0, t)]
            else:
                pairs = [(k, k - 1) for k in range(n - 1, n - 1 - t, -1)]
            self.got[way] = permute(block, "shard", pairs)
            put(self.got[way])

    def last(self):
        while self.t + 1 < len(self.parts):
            self.step()

    def result(self):
        total = self.parts[0].astype(F32)
        for way in (1, -1):
            if self.got[way] is not None:
                total = total + self.got[way].astype(F32)
        return total


def gather_direct(x, name):
    SCOPE[0] = name
    n = lax.axis_size("shard")
    x = now(x)
    got = [permute(x, "shard", [(k, (k + t) % n) for k in range(n)]) for t in range(1, n)]
    put(*got)
    return jnp.concatenate([x] + got)


def scatter_direct(x, name):
    SCOPE[0] = name
    n = lax.axis_size("shard")
    rows = x.shape[0] // n
    x = now(x)
    got = [
        permute(x[t * rows : (t + 1) * rows], "shard", [(k, (k - t) % n) for k in range(n)]) for t in range(1, n)
    ]
    put(*got)
    return functools.reduce(lambda a, c: a + c.astype(F32), got, x[:rows].astype(F32))


def in_order(blocks):
    n, i = lax.axis_size("shard"), lax.axis_index("shard")
    return [pick(i, [blocks[(m - j) % n] for m in range(n)]) for j in range(n)]


def pick(i, cases):
    out = cases[0]
    for m in range(1, len(cases)):
        out = jnp.where(i == m, cases[m], out)
    return out


def swap_z(parts, name="swap"):
    n, i = lax.axis_size("shard"), lax.axis_index("shard")
    SCOPE[0] = name
    parts = now(parts)
    out = [lax.dynamic_index_in_dim(parts, i, 0, False)]
    for t in range(1, n):
        block = lax.dynamic_index_in_dim(parts, (i + t) % n, 0, False)
        out.append(permute(block, "shard", [(k, (k + t) % n) for k in range(n)]))
    put(*out[1:])
    return out


def scatter_small(p):
    return functools.reduce(lambda a, c: a + c, [part.astype(F32) for part in swap_z(p)])


def swapped_rows(name, pieces, hold):
    n, i = lax.axis_size("shard"), lax.axis_index("shard")
    size, g = lax.axis_size("grp"), lax.axis_index("grp")
    rows = pieces[0].shape[0] // size
    SCOPE[0] = name

    def part(d):
        cut = []
        for w in pieces:
            cols = w.shape[1] // n
            cut.append(lax.dynamic_slice(w, (g * rows, d * cols), (rows, cols)))
        return jnp.concatenate(cut, axis=1) if len(cut) > 1 else cut[0]

    blocks = [part(i)]
    for t in range(1, n):
        block = now(part((i + t) % n))
        blocks.append(permute(block, "shard", [(k, (k + t) % n) for k in range(n)]))
    if hold:
        put(*blocks[1:])
    return jnp.stack(in_order(blocks))


def all_rows(part):
    n, rows, cols = part.shape
    return lax.all_gather(part, "grp", axis=1).reshape(n * lax.axis_size("grp") * rows, cols)


class Halves:
    def __init__(self, name, pairs, x_dim, y_dim, by_rows):
        self.name = name
        self.args = (pairs, x_dim, y_dim, by_rows)

    def half(self, which, **more):
        (x, y), *rest = self.args[0]
        which = jnp.stack([which]).astype(jnp.int32)
        return weight_grad([(now(x), y)] + rest, *self.args[1:], which, **more)

    def send(self):
        self.sent = self.half(1 - lax.axis_index("grp") % 2)
        put(self.sent)

    def core(self):
        SCOPE[0] = self.name + "core"
        size = lax.axis_size("grp")
        self.come = permute(now(self.sent), "grp", [(k, k ^ 1) for k in range(size)])
        put(self.come)

    def keep(self):
        self.value = self.half(lax.axis_index("grp") % 2, add=self.come)
        put(self.value)

    def finish(self):
        size = lax.axis_size("grp")
        flat = self.value.reshape((-1,) + self.value.shape[2:])
        alike = [[k for k in range(size) if k % 2 == c] for c in range(2)]
        return lax.psum_scatter(flat, "grp", scatter_dimension=0, axis_index_groups=alike, tiled=True)


def column_grads(part, widths):
    n, size = lax.axis_size("shard"), lax.axis_size("grp")
    rows = part.shape[1]
    outs, start = [], 0
    for group in widths:
        cols = []
        for width in group:
            cols.append(jnp.swapaxes(part[:, :, start : start + width], 0, 1).reshape(rows, n * width))
            start += width
        whole = jnp.concatenate(cols, axis=1) if len(cols) > 1 else cols[0]
        moved = lax.all_to_all(whole, "grp", 1, 0, tiled=True)
        moved = jnp.swapaxes(moved.reshape(size // 2, 2, rows, -1), 0, 1).reshape(size * rows, -1)
        outs.append(moved.astype(F32))
    return outs


def group_sum(x):
    SCOPE[0] = "groupsum"
    size = lax.axis_size("grp")
    step = 1
    while step < size:
        got = lax.ppermute(x, "grp", [(k, k ^ step) for k in range(size)])
        x = (x.astype(F32) + got.astype(F32)).astype(BF)
        step *= 2
    return x.astype(F32)


def norm_scale(h):
    return lax.rsqrt(jnp.mean(h * h, axis=-1, keepdims=True) + EPS)


def norm_back(h, gain, gn):
    r = norm_scale(h)
    g = gn * gain
    grad = r * g - h * (r * r * r) * jnp.mean(g * h, axis=-1, keepdims=True)
    return grad, jnp.sum(gn * h * r, axis=0)


def body(
    tokens,
    cotangent,
    sequence_lengths,
    attention_norm_gain,
    query_matrix,
    key_value_matrix,
    output_matrix,
    adapter_down_maps,
    adapter_up_query,
    adapter_up_key_value,
    adapter_down_output,
    adapter_up_output,
    query_feature_matrices,
    key_feature_matrices,
    feedforward_norm_gain,
    gate_matrix,
    up_matrix,
    down_matrix,
):
    n, shard, size = lax.axis_size("shard"), lax.axis_index("shard"), lax.axis_size("grp")
    batches, _, rows, width = tokens.shape
    length = n * rows
    share = width // n
    nq, hd = query_feature_matrices.shape[:2]
    nk = key_feature_matrices.shape[0]
    rank = adapter_up_query.shape[0]
    qw, kw = nq * hd, nk * hd
    ffq = down_matrix.shape[0]

    small = jnp.concatenate(
        [
            attention_norm_gain[None],
            feedforward_norm_gain[None],
            adapter_up_output,
            adapter_down_maps.T,
        ],
        axis=0,
    )
    half_kv = key_value_matrix.shape[1] // 2
    ends = jnp.cumsum(sequence_lengths[:, 0], axis=1)
    last = sequence_lengths.shape[2] - 2
    own = shard * rows + jnp.arange(rows, dtype=jnp.int32)
    gm_own = [jnp.where((own < ends[b, last])[:, None], cotangent[b, 0], 0) for b in range(batches)]
    me = jnp.stack([shard, jnp.int32(n), jnp.int32(rows // QB)]).astype(jnp.int32)
    Clock.before, Clock.here = [], []
    tok = [Gather(tokens[b, 0], f"tok{b}x") for b in range(batches)]
    cot0 = Gather(gm_own[0], "cot0x")
    s_qkv = swapped_rows("sqkv", [query_matrix, key_value_matrix[:, :half_kv], key_value_matrix[:, half_kv:]], True)
    tok[0].step()
    tick()
    w_qkv = all_rows(s_qkv)
    small_full = jnp.concatenate(in_order(gather_small(small)), axis=1)
    gain_attn = small_full[0].astype(F32)
    gain_ffn = small_full[1].astype(F32)
    up_output = small_full[2 : 2 + rank]
    down_maps_t = small_full[2 + rank :]
    tok[0].step()
    tick()
    tok[0].last()
    tick()
    tok[1].step()
    s_both = swapped_rows("sgu", [gate_matrix, up_matrix], False)
    pad = jnp.zeros((qw, -rank % 128), BF)
    out_wide = jnp.concatenate([output_matrix, adapter_down_output, pad], axis=1)
    zero = jnp.zeros
    u_all = jnp.concatenate(
        [
            jnp.concatenate([adapter_up_query, zero((rank, 2 * kw), BF)], axis=1),
            jnp.concatenate([zero((rank, qw), BF), adapter_up_key_value[0], zero((rank, kw), BF)], axis=1),
            jnp.concatenate([zero((rank, qw + kw), BF), adapter_up_key_value[1]], axis=1),
        ],
        axis=0,
    )

    begins = ends - sequence_lengths[:, 0]
    where = jnp.arange(length, dtype=jnp.int32)
    docs = jnp.sum((where[None, :, None] >= ends[:, None, :]).astype(jnp.int32), axis=2)
    relative = where[None] - jnp.max(
        jnp.where(where[None, :, None] >= begins[:, None, :], begins[:, None, :], 0), axis=2
    )
    freq = ROPE_BASE ** (-jnp.arange(hd // 2, dtype=F32) / (hd // 2))
    angles = freq[None, :, None] * relative.astype(F32)[:, None, :]
    cos_all, sin_all = jnp.cos(angles), jnp.sin(angles)

    def doubled(f):
        return jnp.swapaxes(jnp.concatenate([f, -f], axis=2), 1, 2)

    fq2, fk2 = doubled(query_feature_matrices), doubled(key_feature_matrices)

    def attention(b):
        x = now(tok[b].result()).astype(F32)
        normed = (x * norm_scale(x) * gain_attn).astype(BF)
        mid = nt(normed, down_maps_t).astype(BF)
        proj = lax.dot_general(w_qkv, normed, (((0,), (1,)), ((), ())), preferred_element_type=F32)
        proj = proj + lax.dot_general(u_all, mid, (((0,), (1,)), ((), ())), preferred_element_type=F32)
        place = (
            cos_all[b],
            sin_all[b],
            docs[b][None],
            jnp.broadcast_to(docs[b][:, None], (length, QB)),
        )
        qt, kt, vt, pq, pk, att, ctx, m, den = attn_fwd(me, proj, *place, fq2, fk2)
        branch = tn(ctx, out_wide).astype(BF)
        put(branch)
        return dict(normed=normed, mid=mid, saved=(qt, kt, vt, pq, pk, att, m, den), ctx=ctx, place=place,
                    branch=Scatter(branch, f"br{b}x"))

    def after_attention(b):
        k = keep[b]
        branch = k["branch"].result()
        lora_own = branch[:, width : width + rank].astype(BF)
        x_own = tokens[b, 0].astype(F32)
        hidden = x_own + branch[:, :width] + nn(lora_own, up_output)
        normed_own = (hidden * norm_scale(hidden) * gain_ffn).astype(BF)
        k.update(lora=lora_own, x=x_own, hidden=hidden, send=Gather(normed_own, f"nf{b}x"))

    def ffn(b, cot):
        k = keep[b]
        nf = k["send"].result()
        out, back, product, dgate, dup = ffn_both(now(nf), cot, w_both, down_matrix)
        put(dup)
        k.update(nf=nf, gm=cot, out=out, back=back, product=product, dgate=dgate, dup=dup)

    def after_ffn(b, gnf):
        k = keep[b]
        back, ffn_gain = norm_back(k["hidden"], gain_ffn, gnf)
        grad_hidden = gm_own[b].astype(F32) + back
        gb_own = grad_hidden.astype(BF)
        k.update(grad_hidden=grad_hidden, gb_own=gb_own, send=Gather(gb_own, f"gb{b}x"), ffn_gain=ffn_gain)

    def attention_back(b):
        k = keep[b]
        gb = now(k["send"].result())
        glo = nt(gb, up_output)
        gctx = nt(output_matrix, gb) + nt(adapter_down_output.astype(F32), glo)
        dq, dk, dv, dfq, dfk = attn_bwd(
            me, k["saved"], gctx.astype(BF), *k["place"], query_feature_matrices, key_feature_matrices
        )
        dqkv = jnp.concatenate([dq, dk, dv], axis=0)
        glm = tn(dqkv, u_all.T)
        gn = lax.dot_general(dqkv, w_qkv, (((0,), (1,)), ((), ())), preferred_element_type=F32)
        gn = (gn + nn(glm, down_maps_t.astype(F32))).astype(BF)
        put(gn)
        both = jnp.concatenate([gn, k["out"]], axis=1)
        k.update(gb=gb, glo=glo, dqkv=dqkv, glm=glm, dfq=dfq, dfk=dfk, gn=Scatter(both, f"gn{b}x"))

    def pairs(one, two):
        return [(k[one], k[two]) for k in keep]

    tick()
    keep = [attention(0)]
    tok[1].step()
    tick()
    w_both = all_rows(now(s_both))
    keep[0]["branch"].step()
    tok[1].last()
    keep[0]["branch"].step()
    tick()
    keep.append(attention(1))
    keep[0]["branch"].last()
    tick()
    after_attention(0)
    keep[0]["send"].step()
    tick()
    keep[0]["send"].step()
    keep[1]["branch"].step()
    tick()
    keep[0]["send"].last()
    keep[1]["branch"].step()
    tick()
    keep[1]["branch"].last()
    cot0.step()
    tick()
    after_attention(1)
    keep[1]["send"].step()
    cot0.step()
    tick()
    keep[1]["send"].step()
    cot0.last()
    tick()
    keep[1]["send"].last()
    tick()
    ffn(0, cot0.result())
    cot1 = gather_direct(gm_own[1], "cot1x")
    tick()
    ffn(1, cot1)
    gnf0 = scatter_direct(keep[0]["back"], "gnf0x")
    tick()
    w_g = Halves("Wg", pairs("nf", "dgate"), 0, 0, True)
    w_u = Halves("Wu", pairs("nf", "dup"), 0, 0, True)
    w_d = Halves("Wd", pairs("product", "gm"), 0, 0, False)
    gnf1 = Scatter(keep[1]["back"], "gnf1x")
    after_ffn(0, gnf0)
    keep[0]["send"].step()
    w_g.send()
    w_u.send()
    tick()
    keep[0]["send"].step()
    gnf1.step()
    w_g.core()
    w_d.send()
    tick()
    keep[0]["send"].last()
    gnf1.step()
    w_u.core()
    w_g.keep()
    r_g = w_g.finish()
    tick()
    gnf1.last()
    w_d.core()
    attention_back(0)
    w_u.keep()
    r_u = w_u.finish()
    tick()
    after_ffn(1, gnf1.result())
    keep[1]["send"].step()
    w_d.keep()
    r_d = w_d.finish()
    tick()
    keep[1]["send"].step()
    keep[0]["gn"].step()
    tick()
    keep[1]["send"].last()
    keep[0]["gn"].step()
    put(r_g)
    tick()
    attention_back(1)
    keep[0]["gn"].last()
    t_g = swap_z(r_g.reshape(n, -1, ffq), "swapg")
    tick()
    w_q = Halves("Wq", pairs("normed", "dqkv"), 0, 1, True)
    w_o = Halves("Wo", pairs("ctx", "gb"), 1, 0, False)
    w_q.send()
    w_o.send()
    keep[1]["gn"].step()
    put(r_u)
    tick()
    keep[1]["gn"].step()
    w_q.core()
    w_o.core()
    put(r_d)
    tick()
    keep[1]["gn"].last()
    t_u = swap_z(r_u.reshape(n, -1, ffq), "swapu")
    w_q.keep()
    r_q = w_q.finish()
    w_o.keep()
    r_o = w_o.finish()
    (grad_gate,) = column_grads(jnp.stack(in_order(t_g)), [[ffq]])
    tick()
    (grad_up,) = column_grads(jnp.stack(in_order(t_u)), [[ffq]])
    t_q = jnp.stack(in_order(swap_z(r_q.reshape(n, -1, qw + 2 * kw), "swapq")))
    grad_query, grad_kv = column_grads(t_q, [[qw], [kw, kw]])
    grad_down = r_d.astype(F32)
    grad_output = r_o.astype(F32)
    for k in keep:
        k["up_out"] = tn(k["lora"], k["gb_own"])
    output = []
    token_grads = []
    for k in keep:
        summed = k["gn"].result()
        output.append((k["hidden"] + summed[:, width:]).astype(BF))
        back, attn_gain = norm_back(k["x"], gain_attn, summed[:, :width])
        token_grads.append((k["grad_hidden"] + back).astype(BF))
        k.update(attn_gain=attn_gain)

    def both(name, axis=0):
        return jnp.concatenate([k[name] for k in keep], axis=axis)

    def added(name):
        return functools.reduce(lambda a, c: a + c, [k[name] for k in keep])

    normed = both("normed")
    ctx = both("ctx", 1)
    dqkv = both("dqkv", 1)
    glm = both("glm")
    down_maps_grad = tn(normed.astype(F32), glm)
    ups = lax.dot_general(both("mid"), dqkv, (((0,), (1,)), ((), ())), preferred_element_type=F32)
    down_out_grad = nn(ctx.astype(F32), both("glo"))
    spread = [
        added("attn_gain").reshape(n, share),
        added("ffn_gain").reshape(n, share),
        down_maps_grad.reshape(n, share * 3 * rank),
        jnp.swapaxes(added("up_out").reshape(rank, n, share), 0, 1).reshape(n, rank * share),
    ]
    lined = scatter_small(jnp.concatenate(spread, axis=1).astype(BF))
    local = [
        ups[:rank, :qw].reshape(-1),
        ups[rank : 2 * rank, qw : qw + kw].reshape(-1),
        ups[2 * rank :, qw + kw :].reshape(-1),
        down_out_grad.reshape(-1),
        added("dfq").reshape(-1),
        added("dfk").reshape(-1),
    ]
    flat = group_sum(jnp.concatenate([lined] + local).astype(BF))
    shapes = [
        (share,),
        (share,),
        (share, 3 * rank),
        (rank, share),
        (rank, qw),
        (rank, kw),
        (rank, kw),
        (qw, rank),
        (nq, hd, hd),
        (nk, hd, hd),
    ]
    got, start = [], 0
    for shape in shapes:
        count = 1
        for extent in shape:
            count *= extent
        got.append(flat[start : start + count].reshape(shape))
        start += count
    g_attn, g_ffn, g_down_maps, g_up_out, g_up_q, g_up_k, g_up_v, g_down_out, g_fq, g_fk = got
    return (
        jnp.stack(output)[:, None],
        jnp.stack(token_grads)[:, None],
        g_attn,
        grad_query,
        grad_kv,
        grad_output,
        g_down_maps,
        g_up_q,
        jnp.stack([g_up_k, g_up_v]),
        g_down_out,
        g_up_out,
        g_fq,
        g_fk,
        g_ffn,
        grad_gate,
        grad_up,
        grad_down,
    )


def solution(mesh):
    placed = (
        P(None, "grp", "shard", None),
        P(None, "grp", "shard", None),
        P(None, "grp", None),
        P("shard"),
        P("shard", None),
        P("shard", None),
        P("shard", None),
        P("shard", None),
        P(None, "shard"),
        P(None, None, "shard"),
        P("shard", None),
        P(None, "shard"),
        P("shard", None, None),
        P("shard", None, None),
        P("shard"),
        P("shard", None),
        P("shard", None),
        P("shard", None),
    )
    return jax.shard_map(
        body,
        mesh=mesh,
        in_specs=placed,
        out_specs=(
            P(None, "grp", "shard", None),
            P(None, "grp", "shard", None),
            P("shard"),
            P("shard", "grp"),
            P("shard", "grp"),
            P("shard", "grp"),
            P("shard", None),
            P(None, "shard"),
            P(None, None, "shard"),
            P("shard", None),
            P(None, "shard"),
            P("shard", None, None),
            P("shard", None, None),
            P("shard"),
            P("shard", "grp"),
            P("shard", "grp"),
            P("shard", "grp"),
        ),
        check_vma=False,
    )
```

```python
import functools
import jax
import jax.numpy as jnp
from jax import lax
from jax.experimental import pallas as pl
from jax.experimental.pallas import tpu as pltpu
from jax.sharding import PartitionSpec as P

WIN = 64
EPS = 1e-05
ROPE_BASE = 500000.0
BF = jnp.bfloat16
F32 = jnp.float32
QB = 128


def nn(a, b):
    return lax.dot_general(a, b, (((1,), (0,)), ((), ())), preferred_element_type=F32)


def nt(a, b):
    return lax.dot_general(a, b, (((1,), (1,)), ((), ())), preferred_element_type=F32)


def tn(a, b):
    return lax.dot_general(a, b, (((0,), (0,)), ((), ())), preferred_element_type=F32)


def turned(x, cos, sin):
    half = x.shape[0] // 2
    a, b = x[:half], x[half:]
    return jnp.concatenate([a * cos - b * sin, b * cos + a * sin], axis=0)


def features(z):
    half = z.shape[0] // 2

    def one(part):
        e = jnp.exp(part - jnp.max(part, axis=0, keepdims=True))
        return e / jnp.sum(e, axis=0, keepdims=True)

    return jnp.concatenate([one(z[:half]), one(z[half:])], axis=0)


def features_back(p, g):
    half = p.shape[0] // 2

    def one(pp, gg):
        return pp * (gg - jnp.sum(pp * gg, axis=0, keepdims=True))

    return one(p[:half], g[:half]) - one(p[half:], g[half:])


def masks(drow_ref, dcol_ref, q0, k0, count, heads):
    same = dcol_ref[k0 : k0 + count, :] == drow_ref[0:1, q0 : q0 + QB]
    dist = (
        lax.broadcasted_iota(jnp.int32, (count, QB), 1)
        - lax.broadcasted_iota(jnp.int32, (count, QB), 0)
        + (q0 - k0)
    )
    window = jnp.where(same & (dist >= 0) & (dist < WIN), 1.0, 0.0)
    linear = jnp.where(same & (dist >= WIN), 1.0, 0.0)
    return (
        jnp.concatenate([window] * heads, axis=1),
        jnp.concatenate([linear] * heads, axis=1),
    )


def side(parts):
    return jnp.concatenate(parts, axis=1)


def mixed_rows(win_part, lin_part, w0, l1, n):
    pieces = []
    if w0 > 0:
        pieces.append(lin_part[:w0])
    pieces.append(lin_part[w0:l1] + win_part[: l1 - w0])
    pieces.append(win_part[l1 - w0 :])
    return jnp.concatenate(pieces, axis=0)


def block_pick(me_ref, place, blocks):
    me, n, per = me_ref[0], me_ref[1], me_ref[2]
    source = lax.rem(me - place // per + n, n) * per + lax.rem(place, per)
    out = blocks[0]
    for m in range(1, len(blocks)):
        out = jnp.where(source == m, blocks[m], out)
    return out


def lanes(ref, rows=slice(None)):
    return [ref[rows, m * QB : (m + 1) * QB] for m in range(ref.shape[1] // QB)]


def fwd_kernel(me_ref, q_ref, k_ref, v_ref, cos_ref, sin_ref, drow_ref, dcol_ref, fq_ref, fk_ref,
               qo, ko, vo, pqo, pko, atto, ctxo, mo, deno):
    heads = fq_ref.shape[0]
    hd = k_ref.shape[0]
    length = k_ref.shape[1]
    for block in range(length // QB):
        cols = slice(block * QB, (block + 1) * QB)
        cos, sin = cos_ref[:, cols], sin_ref[:, cols]
        ko[:, cols] = turned(block_pick(me_ref, block, lanes(k_ref)), cos, sin).astype(BF)
        vo[:, cols] = block_pick(me_ref, block, lanes(v_ref)).astype(BF)
        for j in range(heads):
            rows = slice(j * hd, (j + 1) * hd)
            qo[rows, cols] = turned(block_pick(me_ref, block, lanes(q_ref, rows)), cos, sin).astype(BF)
    kt = ko[...]
    vt = vo[...]
    keys = jnp.transpose(kt.astype(F32)).astype(BF)
    pkt = features(nn(fk_ref[0], kt)).astype(BF)
    pko[...] = pkt
    pk = jnp.transpose(pkt.astype(F32)).astype(BF)
    for j in range(heads):
        qt = qo[j * hd : (j + 1) * hd, :]
        pqo[j * 2 * hd : (j + 1) * 2 * hd, :] = features(nn(fq_ref[j], qt)).astype(BF)
    for q0 in range(0, length, QB):
        n = q0 + QB
        w0 = max(q0 - WIN, 0)
        l1 = n - WIN
        qcat = side([qo[j * hd : (j + 1) * hd, q0:n] for j in range(heads)])
        pcat = side([pqo[j * 2 * hd : (j + 1) * 2 * hd, q0:n] for j in range(heads)])
        window, _ = masks(drow_ref, dcol_ref, q0, w0, n - w0, heads)
        _, linear = masks(drow_ref, dcol_ref, q0, 0, l1, heads)
        s = nn(keys[w0:n], qcat) * hd ** (-0.5)
        s = jnp.where(window > 0, s, -1e30)
        m = jnp.max(s, axis=0, keepdims=True)
        w = jnp.exp(s - m)
        kd = jnp.where(linear > 0, nn(pk[:l1], pcat) * jnp.exp(-m), 0.0)
        den = jnp.sum(w, axis=0, keepdims=True) + jnp.sum(kd, axis=0, keepdims=True)
        a = mixed_rows(w, kd, w0, l1, n).astype(BF)
        out = nn(vt[:, :n], a) / den
        for j in range(heads):
            cols = slice(j * QB, (j + 1) * QB)
            atto[j * hd : (j + 1) * hd, q0:n] = out[:, cols]
            mo[0, j : j + 1, q0:n] = m[:, cols]
            deno[0, j : j + 1, q0:n] = den[:, cols]
    for place in range(length // QB):
        ctxo[:, place * QB : (place + 1) * QB] = block_pick(me_ref, place, lanes(atto)).astype(BF)


def bwd_kernel(me_ref, q_ref, k_ref, v_ref, pq_ref, pk_ref, att_ref, m_ref, den_ref, g_ref,
               cos_ref, sin_ref, drow_ref, dcol_ref, fq_ref, fk_ref,
               dqo, dko, dvo, dfqo, dfko,
               dq_s, dpq_s, dk_s, dv_s, dpk_s):
    heads = fq_ref.shape[0]
    hd = k_ref.shape[0]
    length = k_ref.shape[1]
    cos, sin = cos_ref[...], sin_ref[...]
    kt = k_ref[...]
    pkt = pk_ref[...]
    keys = jnp.transpose(kt.astype(F32)).astype(BF)
    vals = jnp.transpose(v_ref[...].astype(F32)).astype(BF)
    pk = jnp.transpose(pkt.astype(F32)).astype(BF)

    def store(ref, rows, value):
        for place in range(length // QB):
            block = block_pick(me_ref, place, [value[:, p : p + QB] for p in range(0, length, QB)])
            ref[rows, place * QB : (place + 1) * QB] = block.astype(BF)

    dk_s[...] = jnp.zeros_like(dk_s)
    dv_s[...] = jnp.zeros_like(dv_s)
    dpk_s[...] = jnp.zeros_like(dpk_s)
    scale = hd ** (-0.5)
    for q0 in range(0, length, QB):
        n = q0 + QB
        w0 = max(q0 - WIN, 0)
        l1 = n - WIN
        qcat = side([q_ref[j * hd : (j + 1) * hd, q0:n] for j in range(heads)])
        pcat = side([pq_ref[j * 2 * hd : (j + 1) * 2 * hd, q0:n] for j in range(heads)])
        gcat = block_pick(
            me_ref, q0 // QB,
            [side([g_ref[j * hd : (j + 1) * hd, p : p + QB] for j in range(heads)]).astype(F32)
             for p in range(0, length, QB)],
        ).astype(BF)
        acat = side([att_ref[j * hd : (j + 1) * hd, q0:n] for j in range(heads)])
        m = side([m_ref[0, j : j + 1, q0:n] for j in range(heads)])
        rden = 1.0 / side([den_ref[0, j : j + 1, q0:n] for j in range(heads)])
        gf = gcat.astype(F32)
        c = jnp.sum(gf * acat, axis=0, keepdims=True)
        window, _ = masks(drow_ref, dcol_ref, q0, w0, n - w0, heads)
        _, linear = masks(drow_ref, dcol_ref, q0, 0, l1, heads)
        db = (nn(vals[:n], gcat) - c) * rden
        s = nn(keys[w0:n], qcat) * scale
        s = jnp.where(window > 0, s, -1e30)
        w = jnp.exp(s - m)
        d = jnp.exp(-m)
        kd = jnp.where(linear > 0, nn(pk[:l1], pcat) * d, 0.0)
        b = mixed_rows(w, kd, w0, l1, n)
        dv_s[0:n, :] += nt(b.astype(BF), (gf * rden).astype(BF))
        dm = -jnp.sum(b * db, axis=0, keepdims=True)
        top = jnp.where(s == m, 1.0, 0.0)
        ties = jnp.sum(top, axis=0, keepdims=True)
        ds = ((w * db[w0:] + top * (dm / ties)) * scale).astype(BF)
        dqw = tn(keys[w0:n], ds)
        dk_s[w0:n, :] += nt(ds, qcat)
        dker = jnp.where(linear > 0, db[:l1] * d, 0.0).astype(BF)
        dpq = tn(pk[:l1], dker)
        dpk_s[0:l1, :] += nt(dker, pcat)
        for j in range(heads):
            cols = slice(j * QB, (j + 1) * QB)
            dq_s[j * hd : (j + 1) * hd, q0:n] = dqw[:, cols]
            dpq_s[j * 2 * hd : (j + 1) * 2 * hd, q0:n] = dpq[:, cols]
    for j in range(heads):
        rows = slice(j * hd, (j + 1) * hd)
        wide = slice(j * 2 * hd, (j + 1) * 2 * hd)
        dz = features_back(pq_ref[wide, :].astype(F32), dpq_s[wide, :]).astype(BF)
        dfqo[j] = nt(q_ref[rows, :], dz)
        store(dqo, rows, turned(dq_s[rows, :] + nn(fq_ref[j], dz), cos, -sin))
    dz = features_back(pkt.astype(F32), jnp.transpose(dpk_s[...])).astype(BF)
    dfko[0] = nt(kt, dz)
    dk = jnp.transpose(dk_s[...]) + nn(fk_ref[0], dz)
    store(dko, slice(None), turned(dk, cos, -sin))
    store(dvo, slice(None), jnp.transpose(dv_s[...]))


def attn_specs(nq, nk, hd, length):
    heads = nq // nk
    whole = lambda shape: pl.BlockSpec(shape, lambda g: (0,) * len(shape))
    return dict(
        me=pl.BlockSpec(memory_space=pltpu.SMEM),
        q=pl.BlockSpec((heads * hd, length), lambda g: (g, 0)),
        k=pl.BlockSpec((hd, length), lambda g: (g, 0)),
        kin=pl.BlockSpec((hd, length), lambda g: (nq + g, 0)),
        vin=pl.BlockSpec((hd, length), lambda g: (nq + nk + g, 0)),
        pq=pl.BlockSpec((2 * heads * hd, length), lambda g: (g, 0)),
        pk=pl.BlockSpec((2 * hd, length), lambda g: (g, 0)),
        row=pl.BlockSpec((1, heads, length), lambda g: (g, 0, 0)),
        angle=whole((hd // 2, length)),
        drow=whole((1, length)),
        dcol=whole((length, QB)),
        fq2=pl.BlockSpec((heads, 2 * hd, hd), lambda g: (g, 0, 0)),
        fk2=pl.BlockSpec((1, 2 * hd, hd), lambda g: (g, 0, 0)),
        fq=pl.BlockSpec((heads, hd, hd), lambda g: (g, 0, 0)),
        fk=pl.BlockSpec((1, hd, hd), lambda g: (g, 0, 0)),
    )


def attn_fwd(me, proj, cos, sin, drow, dcol, fq2, fk2):
    nq, nk, hd = fq2.shape[0], fk2.shape[0], fq2.shape[2]
    length = proj.shape[1]
    heads = nq // nk
    sp = attn_specs(nq, nk, hd, length)
    sds = jax.ShapeDtypeStruct
    pairs = length * length * nq
    return pl.pallas_call(
        fwd_kernel,
        grid=(nk,),
        in_specs=[sp["me"], sp["q"], sp["kin"], sp["vin"], sp["angle"], sp["angle"], sp["drow"], sp["dcol"],
                  sp["fq2"], sp["fk2"]],
        out_specs=[sp["q"], sp["k"], sp["k"], sp["pq"], sp["pk"], sp["q"], sp["q"], sp["row"], sp["row"]],
        out_shape=[
            sds((nq * hd, length), BF), sds((nk * hd, length), BF), sds((nk * hd, length), BF),
            sds((2 * nq * hd, length), BF), sds((2 * nk * hd, length), BF),
            sds((nq * hd, length), F32), sds((nq * hd, length), BF),
            sds((nk, heads, length), F32), sds((nk, heads, length), F32),
        ],
        cost_estimate=pl.CostEstimate(flops=8 * pairs * hd, bytes_accessed=8 << 20, transcendentals=pairs),
        compiler_params=pltpu.CompilerParams(vmem_limit_bytes=48 << 20),
        name="attn_fwd",
    )(me, proj, proj, proj, cos, sin, drow, dcol, fq2, fk2)


def attn_bwd(me, saved, g, cos, sin, drow, dcol, fq, fk):
    qt, kt, vt, pq, pk, att, m, den = saved
    nq, nk, hd = fq.shape[0], fk.shape[0], fq.shape[2]
    length = qt.shape[1]
    heads = nq // nk
    sp = attn_specs(nq, nk, hd, length)
    sds = jax.ShapeDtypeStruct
    pairs = length * length * nq
    return pl.pallas_call(
        bwd_kernel,
        grid=(nk,),
        in_specs=[sp["me"], sp["q"], sp["k"], sp["k"], sp["pq"], sp["pk"], sp["q"], sp["row"], sp["row"], sp["q"],
                  sp["angle"], sp["angle"], sp["drow"], sp["dcol"], sp["fq"], sp["fk"]],
        out_specs=[sp["q"], sp["k"], sp["k"], sp["fq"], sp["fk"]],
        out_shape=[
            sds((nq * hd, length), BF), sds((nk * hd, length), BF), sds((nk * hd, length), BF),
            sds((nq, hd, hd), F32), sds((nk, hd, hd), F32),
        ],
        scratch_shapes=[
            pltpu.VMEM((heads * hd, length), F32),
            pltpu.VMEM((2 * heads * hd, length), F32),
            pltpu.VMEM((length, hd), F32),
            pltpu.VMEM((length, hd), F32),
            pltpu.VMEM((length, 2 * hd), F32),
        ],
        cost_estimate=pl.CostEstimate(flops=20 * pairs * hd, bytes_accessed=8 << 20, transcendentals=pairs),
        compiler_params=pltpu.CompilerParams(vmem_limit_bytes=48 << 20),
        name="attn_bwd",
    )(me, qt, kt, vt, pq, pk, att, m, den, g, cos, sin, drow, dcol, fq, fk)


def ffn_kernel(x_ref, g_ref, wg_ref, wu_ref, wd_ref, out_ref, back_ref, prod_ref, dgate_ref, dup_ref,
               out_acc, back_acc):
    step = pl.program_id(1)
    x = x_ref[...]
    gate = nn(x, wg_ref[...])
    up = nn(x, wu_ref[...])
    sg = jax.nn.sigmoid(gate)
    act = gate * sg
    prod = (act * up).astype(BF)
    prod_ref[...] = prod
    gp = nt(g_ref[...], wd_ref[...])
    dgate = (gp * up * (sg + act * (1.0 - sg))).astype(BF)
    dup = (gp * act).astype(BF)
    dgate_ref[...] = dgate
    dup_ref[...] = dup
    out = nn(prod, wd_ref[...])
    back = nt(dgate, wg_ref[...]) + nt(dup, wu_ref[...])

    @pl.when(step == 0)
    def _():
        out_acc[...] = out
        back_acc[...] = back

    @pl.when(step > 0)
    def _():
        out_acc[...] += out
        back_acc[...] += back

    @pl.when(step == pl.num_programs(1) - 1)
    def _():
        out_ref[...] = out_acc[...].astype(BF)
        back_ref[...] = back_acc[...].astype(BF)


def ffn_both(x, g, w_both, wd):
    length, width = x.shape
    ff = wd.shape[0]
    tm, tf = min(512, length), min(512, ff)
    rows = pl.BlockSpec((tm, width), lambda i, j: (i, 0))
    cols = pl.BlockSpec((width, tf), lambda i, j: (0, j))
    tile = pl.BlockSpec((tm, tf), lambda i, j: (i, j))
    more = pl.BlockSpec((width, tf), lambda i, j: (0, ff // tf + j))
    sds = jax.ShapeDtypeStruct
    return pl.pallas_call(
        ffn_kernel,
        grid=(length // tm, ff // tf),
        in_specs=[rows, rows, cols, more, pl.BlockSpec((tf, width), lambda i, j: (j, 0))],
        out_specs=[rows, rows, tile, tile, tile],
        out_shape=[sds((length, width), BF)] * 2 + [sds((length, ff), BF)] * 3,
        scratch_shapes=[pltpu.VMEM((tm, width), F32)] * 2,
        cost_estimate=pl.CostEstimate(
            flops=12 * length * width * ff, bytes_accessed=6 * width * ff, transcendentals=length * ff
        ),
        compiler_params=pltpu.CompilerParams(vmem_limit_bytes=56 << 20),
        name="ffn_both",
    )(x, g, w_both, w_both, wd)


def weight_grad(pairs, x_dim, y_dim, by_rows, side_index, others=None, add=None):
    x0, y0 = pairs[0]
    tokens, rows, cols = x0.shape[x_dim], x0.shape[1 - x_dim], y0.shape[1 - y_dim]
    groups = lax.axis_size("grp")
    half = groups // 2
    count = len(pairs)
    extra = 0 if add is None else 1

    def kernel(side_ref, *refs):
        out = refs[-1]

        def cut(ref, dim, size, which):
            place = slice(which * size, (which + 1) * size)
            return ref[:, place] if dim == 0 else ref[place, :]

        for which in range(2):

            @pl.when(side_ref[0] == which)
            def _(which=which):
                total = None
                for k in range(count):
                    x, y = refs[2 * k], refs[2 * k + 1]
                    x = cut(x, x_dim, tm, which) if by_rows else x[...]
                    y = y[...] if by_rows else cut(y, y_dim, tn, which)
                    part = lax.dot_general(x, y, (((x_dim,), (y_dim,)), ((), ())), preferred_element_type=F32)
                    total = part if total is None else total + part
                total = total.reshape(out.shape)
                if extra:
                    total = total + refs[2 * count][...].astype(F32)
                out[...] = total.astype(BF)

    def spec(dim, size, where):
        if dim == 0:
            return pl.BlockSpec((tokens, size), lambda i, j: (0, where(i, j)))
        return pl.BlockSpec((size, tokens), lambda i, j: (where(i, j), 0))

    if by_rows:
        shards = lax.axis_size("shard")
        part = rows // shards // groups
        tm, tn = half * part, cols
        grid = (shards, 1)
        xs = spec(x_dim, 2 * tm, lambda i, j: i)
        ys = spec(y_dim, tn, lambda i, j: j)
        shape = (half, shards, part, cols)
        block = pl.BlockSpec((half, 1, part, tn), lambda i, j: (0, i, 0, j))
    else:
        tm, tn = min(1024, rows), cols // groups
        grid = (rows // tm, half)
        xs = spec(x_dim, tm, lambda i, j: i)
        ys = spec(y_dim, 2 * tn, lambda i, j: j)
        shape = (half, rows, tn)
        block = pl.BlockSpec((1, tm, tn), lambda i, j: (j, i, 0))
    return pl.pallas_call(
        kernel,
        grid=grid,
        in_specs=[pl.BlockSpec(memory_space=pltpu.SMEM)] + [xs, ys] * count + [block] * extra,
        out_specs=block,
        out_shape=jax.ShapeDtypeStruct(shape, BF),
        cost_estimate=pl.CostEstimate(
            flops=count * tokens * rows * cols, bytes_accessed=rows * cols, transcendentals=0
        ),
        compiler_params=pltpu.CompilerParams(vmem_limit_bytes=48 << 20),
        name="weight_grad",
    )(side_index, *[a for pair in pairs for a in pair], *([add] if extra else []))


def tie(x, *others):
    return lax.optimization_barrier((x,) + others)[0] if others else x


def gather_small(x):
    SCOPE[0] = "small"
    n = lax.axis_size("shard")
    x = now(x)
    return [x] + [permute(x, "shard", [(k, (k + t) % n) for k in range(n)]) for t in range(1, n)]


SCOPE = ["start"]


def permute(x, axis, pairs):
    Clock.sent.append(x)
    with jax.named_scope(SCOPE[0]):
        return lax.ppermute(x, axis, pairs)


class Clock:
    before, here, sent = [], [], []


def now(x):
    return tie(x, *Clock.before)


def beside(x):
    return tie(x, *Clock.before, *Clock.sent)


def put(*values):
    Clock.here.extend(values)


def tick():
    Clock.before, Clock.here, Clock.sent = Clock.here, [], []


class Gather:
    def __init__(self, x, name="gather"):
        self.name = name
        self.x, self.up, self.down = x, x, x
        self.ups, self.downs = [], []

    def step(self):
        n, t = lax.axis_size("shard"), len(self.ups) + 1
        if t >= n:
            return
        SCOPE[0] = self.name + str(t)
        self.up = permute(now(self.up), "shard", [(k, k + 1) for k in range(t - 1, n - 1)])
        self.down = permute(now(self.down), "shard", [(k, k - 1) for k in range(n - t, 0, -1)])
        self.ups.append(self.up)
        self.downs.append(self.down)
        put(self.up, self.down)

    def last(self):
        while len(self.ups) + 1 < lax.axis_size("shard"):
            self.step()

    def result(self):
        n, i = lax.axis_size("shard"), lax.axis_index("shard")
        blocks = [jnp.where(i >= t, self.ups[t - 1], self.downs[n - t - 1]) for t in range(1, n)]
        return jnp.concatenate([self.x] + blocks)


class Scatter:
    def __init__(self, x, name="scatter"):
        self.name = name
        n = lax.axis_size("shard")
        rows = x.shape[0] // n
        self.parts = [x[k * rows : (k + 1) * rows] for k in range(n)]
        self.got, self.t = {1: None, -1: None}, 0

    def step(self):
        n, t = len(self.parts), self.t + 1
        if t >= n:
            return
        SCOPE[0] = self.name + str(t)
        self.t = t
        for way in (1, -1):
            block = now(self.parts[t if way > 0 else n - t])
            if self.got[way] is not None:
                block = (block.astype(F32) + self.got[way].astype(F32)).astype(block.dtype)
            if way > 0:
                pairs = [(k, k + 1) for k in range(0, t)]
            else:
                pairs = [(k, k - 1) for k in range(n - 1, n - 1 - t, -1)]
            self.got[way] = permute(block, "shard", pairs)
            put(self.got[way])

    def last(self):
        while self.t + 1 < len(self.parts):
            self.step()

    def result(self):
        total = self.parts[0].astype(F32)
        for way in (1, -1):
            if self.got[way] is not None:
                total = total + self.got[way].astype(F32)
        return total


def gather_direct(x, name):
    SCOPE[0] = name
    n = lax.axis_size("shard")
    x = now(x)
    got = [permute(x, "shard", [(k, (k + t) % n) for k in range(n)]) for t in range(1, n)]
    put(*got)
    return [x] + got


def scatter_direct(x, name):
    SCOPE[0] = name
    n = lax.axis_size("shard")
    rows = x.shape[0] // n
    x = now(x)
    got = [
        permute(x[t * rows : (t + 1) * rows], "shard", [(k, (k - t) % n) for k in range(n)]) for t in range(1, n)
    ]
    put(*got)
    return functools.reduce(lambda a, c: a + c.astype(F32), got, x[:rows].astype(F32))


def in_order(blocks):
    n, i = lax.axis_size("shard"), lax.axis_index("shard")
    return [pick(i, [blocks[(m - j) % n] for m in range(n)]) for j in range(n)]


def pick(i, cases):
    out = cases[0]
    for m in range(1, len(cases)):
        out = jnp.where(i == m, cases[m], out)
    return out


def swap_z(parts, name="swap"):
    n, i = lax.axis_size("shard"), lax.axis_index("shard")
    SCOPE[0] = name
    parts = now(parts)
    out = [lax.dynamic_index_in_dim(parts, i, 0, False)]
    for t in range(1, n):
        block = lax.dynamic_index_in_dim(parts, (i + t) % n, 0, False)
        out.append(permute(block, "shard", [(k, (k + t) % n) for k in range(n)]))
    put(*out[1:])
    return out


def scatter_small(p):
    return functools.reduce(lambda a, c: a + c, [part.astype(F32) for part in swap_z(p)])


class SwappedRows:
    def __init__(self, name, pieces):
        self.name, self.pieces = name, pieces
        self.blocks = {0: self.part(lax.axis_index("shard"))}

    def part(self, d):
        n, size, g = lax.axis_size("shard"), lax.axis_size("grp"), lax.axis_index("grp")
        rows = self.pieces[0].shape[0] // size
        cut = []
        for w in self.pieces:
            cols = w.shape[1] // n
            cut.append(lax.dynamic_slice(w, (g * rows, d * cols), (rows, cols)))
        return jnp.concatenate(cut, axis=1) if len(cut) > 1 else cut[0]

    def step(self, *distances):
        SCOPE[0] = self.name
        n, i = lax.axis_size("shard"), lax.axis_index("shard")
        for t in distances:
            if 0 < t < n:
                block = now(self.part((i + t) % n))
                self.blocks[t] = permute(block, "shard", [(k, (k + t) % n) for k in range(n)])
                put(self.blocks[t])

    def result(self):
        n = lax.axis_size("shard")
        self.step(*[t for t in range(1, n) if t not in self.blocks])
        return jnp.stack(in_order([now(self.blocks[t]) for t in range(n)]))


def all_rows(part):
    n, rows, cols = part.shape
    return lax.all_gather(part, "grp", axis=1).reshape(n * lax.axis_size("grp") * rows, cols)


class Halves:
    def __init__(self, name, pairs, x_dim, y_dim, by_rows):
        self.name = name
        self.args = (pairs, x_dim, y_dim, by_rows)

    def half(self, which, **more):
        (x, y), *rest = self.args[0]
        which = jnp.stack([which]).astype(jnp.int32)
        return weight_grad([(beside(x), y)] + rest, *self.args[1:], which, **more)

    def send(self):
        self.sent = self.half(1 - lax.axis_index("grp") % 2)
        put(self.sent)

    def core(self):
        SCOPE[0] = self.name + "core"
        size = lax.axis_size("grp")
        self.come = permute(now(self.sent), "grp", [(k, k ^ 1) for k in range(size)])
        put(self.come)

    def keep(self):
        self.value = self.half(lax.axis_index("grp") % 2, add=self.come)
        put(self.value)

    def finish(self):
        size = lax.axis_size("grp")
        flat = self.value.reshape((-1,) + self.value.shape[2:])
        alike = [[k for k in range(size) if k % 2 == c] for c in range(2)]
        return lax.psum_scatter(flat, "grp", scatter_dimension=0, axis_index_groups=alike, tiled=True)


def column_grads(part, widths):
    n, size = lax.axis_size("shard"), lax.axis_size("grp")
    rows = part.shape[1]
    pieces, start = [], 0
    for group in widths:
        cols = []
        for width in group:
            cols.append(jnp.swapaxes(part[:, :, start : start + width], 0, 1).reshape(rows, n * width))
            start += width
        whole = jnp.concatenate(cols, axis=1) if len(cols) > 1 else cols[0]
        pieces.append(whole.reshape(rows, size, -1))
    moved = jnp.concatenate(pieces, axis=2) if len(pieces) > 1 else pieces[0]
    moved = lax.all_to_all(moved.reshape(rows, -1), "grp", 1, 0, tiled=True)
    moved = jnp.swapaxes(moved.reshape(size // 2, 2, rows, -1), 0, 1).reshape(size * rows, -1)
    outs, start = [], 0
    for piece in pieces:
        outs.append(moved[:, start : start + piece.shape[2]].astype(F32))
        start += piece.shape[2]
    return outs


def group_sum(x):
    SCOPE[0] = "groupsum"
    size = lax.axis_size("grp")
    step = 1
    while step < size:
        got = lax.ppermute(x, "grp", [(k, k ^ step) for k in range(size)])
        x = (x.astype(F32) + got.astype(F32)).astype(BF)
        step *= 2
    return x.astype(F32)


def norm_scale(h):
    return lax.rsqrt(jnp.mean(h * h, axis=-1, keepdims=True) + EPS)


def norm_back(h, gain, gn):
    r = norm_scale(h)
    g = gn * gain
    grad = r * g - h * (r * r * r) * jnp.mean(g * h, axis=-1, keepdims=True)
    return grad, jnp.sum(gn * h * r, axis=0)


def body(
    tokens,
    cotangent,
    sequence_lengths,
    attention_norm_gain,
    query_matrix,
    key_value_matrix,
    output_matrix,
    adapter_down_maps,
    adapter_up_query,
    adapter_up_key_value,
    adapter_down_output,
    adapter_up_output,
    query_feature_matrices,
    key_feature_matrices,
    feedforward_norm_gain,
    gate_matrix,
    up_matrix,
    down_matrix,
):
    n, shard, size = lax.axis_size("shard"), lax.axis_index("shard"), lax.axis_size("grp")
    batches, _, rows, width = tokens.shape
    length = n * rows
    share = width // n
    nq, hd = query_feature_matrices.shape[:2]
    nk = key_feature_matrices.shape[0]
    rank = adapter_up_query.shape[0]
    qw, kw = nq * hd, nk * hd
    ffq = down_matrix.shape[0]

    small = jnp.concatenate(
        [
            attention_norm_gain[None],
            feedforward_norm_gain[None],
            adapter_up_output,
            adapter_down_maps.T,
        ],
        axis=0,
    )
    half_kv = key_value_matrix.shape[1] // 2
    ends = jnp.cumsum(sequence_lengths[:, 0], axis=1)
    last = sequence_lengths.shape[2] - 2
    own = shard * rows + jnp.arange(rows, dtype=jnp.int32)
    gm_own = [jnp.where((own < ends[b, last])[:, None], cotangent[b, 0], 0) for b in range(batches)]
    me = jnp.stack([shard, jnp.int32(n), jnp.int32(rows // QB)]).astype(jnp.int32)
    Clock.before, Clock.here, Clock.sent = [], [], []
    tok = [Gather(tokens[b, 0], f"tok{b}x") for b in range(batches)]
    cot0 = Gather(gm_own[0], "cot0x")
    s_qkv = SwappedRows("sqkv", [query_matrix, key_value_matrix[:, :half_kv], key_value_matrix[:, half_kv:]])
    s_qkv.step(*range(1, n))
    tok[0].step()
    tick()
    w_qkv = all_rows(s_qkv.result())
    small_full = jnp.concatenate(in_order(gather_small(small)), axis=1)
    gain_attn = small_full[0].astype(F32)
    gain_ffn = small_full[1].astype(F32)
    up_output = small_full[2 : 2 + rank]
    down_maps_t = small_full[2 + rank :]
    tok[0].step()
    tick()
    tok[0].last()
    tick()
    tok[1].step()
    s_both = SwappedRows("sgu", [gate_matrix, up_matrix])
    s_both.step(1)
    pad = jnp.zeros((qw, -rank % 128), BF)
    out_wide = jnp.concatenate([output_matrix, adapter_down_output, pad], axis=1)
    zero = jnp.zeros
    u_all = jnp.concatenate(
        [
            jnp.concatenate([adapter_up_query, zero((rank, 2 * kw), BF)], axis=1),
            jnp.concatenate([zero((rank, qw), BF), adapter_up_key_value[0], zero((rank, kw), BF)], axis=1),
            jnp.concatenate([zero((rank, qw + kw), BF), adapter_up_key_value[1]], axis=1),
        ],
        axis=0,
    )

    begins = ends - sequence_lengths[:, 0]
    where = jnp.arange(length, dtype=jnp.int32)
    docs = jnp.sum((where[None, :, None] >= ends[:, None, :]).astype(jnp.int32), axis=2)
    relative = where[None] - jnp.max(
        jnp.where(where[None, :, None] >= begins[:, None, :], begins[:, None, :], 0), axis=2
    )
    freq = ROPE_BASE ** (-jnp.arange(hd // 2, dtype=F32) / (hd // 2))
    angles = freq[None, :, None] * relative.astype(F32)[:, None, :]
    cos_all, sin_all = jnp.cos(angles), jnp.sin(angles)

    def doubled(f):
        return jnp.swapaxes(jnp.concatenate([f, -f], axis=2), 1, 2)

    fq2, fk2 = doubled(query_feature_matrices), doubled(key_feature_matrices)

    def attention(b):
        x = beside(tok[b].result()).astype(F32)
        normed = (x * norm_scale(x) * gain_attn).astype(BF)
        mid = nt(normed, down_maps_t).astype(BF)
        proj = lax.dot_general(w_qkv, normed, (((0,), (1,)), ((), ())), preferred_element_type=F32)
        proj = proj + lax.dot_general(u_all, mid, (((0,), (1,)), ((), ())), preferred_element_type=F32)
        place = (
            cos_all[b],
            sin_all[b],
            docs[b][None],
            jnp.broadcast_to(docs[b][:, None], (length, QB)),
        )
        qt, kt, vt, pq, pk, att, ctx, m, den = attn_fwd(me, proj, *place, fq2, fk2)
        branch = tn(ctx, out_wide).astype(BF)
        put(branch)
        return dict(normed=normed, mid=mid, saved=(qt, kt, vt, pq, pk, att, m, den), ctx=ctx, place=place,
                    branch=Scatter(branch, f"br{b}x"))

    def after_attention(b):
        k = keep[b]
        branch = k["branch"].result()
        lora_own = branch[:, width : width + rank].astype(BF)
        x_own = tokens[b, 0].astype(F32)
        hidden = x_own + branch[:, :width] + nn(lora_own, up_output)
        normed_own = (hidden * norm_scale(hidden) * gain_ffn).astype(BF)
        k.update(lora=lora_own, x=x_own, hidden=hidden, send=Gather(normed_own, f"nf{b}x"))

    def ffn(b, cot):
        k = keep[b]
        nf = k["send"].result()
        out, back, product, dgate, dup = ffn_both(beside(nf), cot, w_both, down_matrix)
        put(dup)
        k.update(nf=nf, gm=cot, out=out, back=back, product=product, dgate=dgate, dup=dup)

    def after_ffn(b, gnf):
        k = keep[b]
        back, ffn_gain = norm_back(k["hidden"], gain_ffn, gnf)
        grad_hidden = gm_own[b].astype(F32) + back
        gb_own = grad_hidden.astype(BF)
        k.update(grad_hidden=grad_hidden, gb_own=gb_own, send=Gather(gb_own, f"gb{b}x"), ffn_gain=ffn_gain)

    def attention_back(b):
        k = keep[b]
        gb = beside(k["send"].result())
        glo = nt(gb, up_output)
        gctx = nt(output_matrix, gb) + nt(adapter_down_output.astype(F32), glo)
        dq, dk, dv, dfq, dfk = attn_bwd(
            me, k["saved"], gctx.astype(BF), *k["place"], query_feature_matrices, key_feature_matrices
        )
        dqkv = jnp.concatenate([dq, dk, dv], axis=0)
        glm = tn(dqkv, u_all.T)
        gn = lax.dot_general(dqkv, w_qkv, (((0,), (1,)), ((), ())), preferred_element_type=F32)
        gn = (gn + nn(glm, down_maps_t.astype(F32))).astype(BF)
        put(gn)
        k.update(gb=gb, glo=glo, dqkv=dqkv, glm=glm, dfq=dfq, dfk=dfk, gn=Scatter(gn, f"gn{b}x"))

    def pairs(one, two):
        return [(k[one], k[two]) for k in keep]

    tick()
    tok[1].step()
    s_both.step(n - 1)
    keep = [attention(0)]
    tick()
    s_both.step(*range(2, n - 1))
    keep[0]["branch"].step()
    tok[1].last()
    tick()
    w_both = all_rows(s_both.result())
    keep[0]["branch"].step()
    tick()
    keep[0]["branch"].last()
    keep.append(attention(1))
    tick()
    after_attention(0)
    keep[0]["send"].step()
    tick()
    keep[0]["send"].step()
    keep[1]["branch"].step()
    tick()
    keep[0]["send"].last()
    keep[1]["branch"].step()
    tick()
    keep[1]["branch"].last()
    cot0.step()
    tick()
    after_attention(1)
    keep[1]["send"].step()
    cot0.step()
    tick()
    keep[1]["send"].step()
    cot0.last()
    tick()
    keep[1]["send"].last()
    tick()
    cot1 = gather_direct(gm_own[1], "cot1x")
    ffn(0, cot0.result())
    tick()
    gnf0 = scatter_direct(keep[0]["back"], "gnf0x")
    ffn(1, jnp.concatenate([now(c) for c in cot1]))
    tick()
    w_g = Halves("Wg", pairs("nf", "dgate"), 0, 0, True)
    w_u = Halves("Wu", pairs("nf", "dup"), 0, 0, True)
    w_d = Halves("Wd", pairs("product", "gm"), 0, 0, False)
    gnf1 = Scatter(keep[1]["back"], "gnf1x")
    out = [Scatter(k["out"], f"out{b}x") for b, k in enumerate(keep)]
    after_ffn(0, gnf0)
    keep[0]["send"].step()
    out[0].step()
    w_g.send()
    w_u.send()
    tick()
    keep[0]["send"].step()
    gnf1.step()
    w_g.core()
    w_d.send()
    tick()
    keep[0]["send"].last()
    gnf1.step()
    w_u.core()
    w_g.keep()
    r_g = w_g.finish()
    tick()
    gnf1.last()
    out[0].step()
    w_d.core()
    attention_back(0)
    tick()
    after_ffn(1, gnf1.result())
    keep[1]["send"].step()
    out[0].last()
    w_u.keep()
    r_u = w_u.finish()
    tick()
    keep[1]["send"].step()
    keep[0]["gn"].step()
    w_d.keep()
    r_d = w_d.finish()
    tick()
    keep[1]["send"].last()
    keep[0]["gn"].step()
    put(r_g)
    tick()
    keep[0]["gn"].last()
    t_g = swap_z(r_g.reshape(n, -1, ffq), "swapg")
    attention_back(1)
    w_q = Halves("Wq", pairs("normed", "dqkv"), 0, 1, True)
    w_o = Halves("Wo", pairs("ctx", "gb"), 1, 0, False)
    w_q.send()
    w_o.send()
    tick()
    keep[1]["gn"].step()
    out[1].step()
    w_q.core()
    w_o.core()
    put(r_u)
    tick()
    keep[1]["gn"].step()
    out[1].step()
    w_q.keep()
    r_q = w_q.finish()
    w_o.keep()
    r_o = w_o.finish()
    put(r_d)
    tick()
    keep[1]["gn"].last()
    t_u = swap_z(r_u.reshape(n, -1, ffq), "swapu")
    (grad_gate,) = column_grads(jnp.stack(in_order([beside(t) for t in t_g])), [[ffq]])
    tick()
    out[1].last()
    for k in keep:
        k["gn_sum"] = now(k["gn"].result())
    for k in keep:
        k["up_out"] = tn(k["lora"], k["gb_own"])
    token_grads = []
    for k in keep:
        back, attn_gain = norm_back(k["x"], gain_attn, k["gn_sum"])
        token_grads.append((k["grad_hidden"] + back).astype(BF))
        k.update(attn_gain=attn_gain)

    def both(name, axis=0):
        return jnp.concatenate([k[name] for k in keep], axis=axis)

    def added(name):
        return functools.reduce(lambda a, c: a + c, [k[name] for k in keep])

    normed = both("normed")
    ctx = both("ctx", 1)
    dqkv = both("dqkv", 1)
    glm = both("glm")
    down_maps_grad = tn(normed.astype(F32), glm)
    ups = lax.dot_general(both("mid"), dqkv, (((0,), (1,)), ((), ())), preferred_element_type=F32)
    down_out_grad = nn(ctx.astype(F32), both("glo"))
    spread = [
        added("attn_gain").reshape(n, share),
        added("ffn_gain").reshape(n, share),
        down_maps_grad.reshape(n, share * 3 * rank),
        jnp.swapaxes(added("up_out").reshape(rank, n, share), 0, 1).reshape(n, rank * share),
    ]
    lined = scatter_small(jnp.concatenate(spread, axis=1).astype(BF))
    local = [
        ups[:rank, :qw].reshape(-1),
        ups[rank : 2 * rank, qw : qw + kw].reshape(-1),
        ups[2 * rank :, qw + kw :].reshape(-1),
        down_out_grad.reshape(-1),
        added("dfq").reshape(-1),
        added("dfk").reshape(-1),
    ]
    (grad_up,) = column_grads(jnp.stack(in_order([beside(t) for t in t_u])), [[ffq]])
    tick()
    t_q = jnp.stack(in_order(swap_z(r_q.reshape(n, -1, qw + 2 * kw), "swapq")))
    grad_query, grad_kv = column_grads(t_q, [[qw], [kw, kw]])
    grad_down = r_d.astype(F32)
    grad_output = r_o.astype(F32)
    output = [(k["hidden"] + o.result()).astype(BF) for k, o in zip(keep, out)]
    flat = group_sum(jnp.concatenate([lined] + local).astype(BF))
    shapes = [
        (share,),
        (share,),
        (share, 3 * rank),
        (rank, share),
        (rank, qw),
        (rank, kw),
        (rank, kw),
        (qw, rank),
        (nq, hd, hd),
        (nk, hd, hd),
    ]
    got, start = [], 0
    for shape in shapes:
        count = 1
        for extent in shape:
            count *= extent
        got.append(flat[start : start + count].reshape(shape))
        start += count
    g_attn, g_ffn, g_down_maps, g_up_out, g_up_q, g_up_k, g_up_v, g_down_out, g_fq, g_fk = got
    return (
        jnp.stack(output)[:, None],
        jnp.stack(token_grads)[:, None],
        g_attn,
        grad_query,
        grad_kv,
        grad_output,
        g_down_maps,
        g_up_q,
        jnp.stack([g_up_k, g_up_v]),
        g_down_out,
        g_up_out,
        g_fq,
        g_fk,
        g_ffn,
        grad_gate,
        grad_up,
        grad_down,
    )


def solution(mesh):
    placed = (
        P(None, "grp", "shard", None),
        P(None, "grp", "shard", None),
        P(None, "grp", None),
        P("shard"),
        P("shard", None),
        P("shard", None),
        P("shard", None),
        P("shard", None),
        P(None, "shard"),
        P(None, None, "shard"),
        P("shard", None),
        P(None, "shard"),
        P("shard", None, None),
        P("shard", None, None),
        P("shard"),
        P("shard", None),
        P("shard", None),
        P("shard", None),
    )
    return jax.shard_map(
        body,
        mesh=mesh,
        in_specs=placed,
        out_specs=(
            P(None, "grp", "shard", None),
            P(None, "grp", "shard", None),
            P("shard"),
            P("shard", "grp"),
            P("shard", "grp"),
            P("shard", "grp"),
            P("shard", None),
            P(None, "shard"),
            P(None, None, "shard"),
            P("shard", None),
            P(None, "shard"),
            P("shard", None, None),
            P("shard", None, None),
            P("shard"),
            P("shard", "grp"),
            P("shard", "grp"),
            P("shard", "grp"),
        ),
        check_vma=False,
    )
```

```python
import functools
import jax
import jax.numpy as jnp
from jax import lax
from jax.experimental import pallas as pl
from jax.experimental.pallas import tpu as pltpu
from jax.sharding import PartitionSpec as P

WIN = 64
EPS = 1e-05
ROPE_BASE = 500000.0
BF = jnp.bfloat16
F32 = jnp.float32
QB = 128


def nn(a, b):
    return lax.dot_general(a, b, (((1,), (0,)), ((), ())), preferred_element_type=F32)


def nt(a, b):
    return lax.dot_general(a, b, (((1,), (1,)), ((), ())), preferred_element_type=F32)


def tn(a, b):
    return lax.dot_general(a, b, (((0,), (0,)), ((), ())), preferred_element_type=F32)


def turned(x, cos, sin):
    half = x.shape[0] // 2
    a, b = x[:half], x[half:]
    return jnp.concatenate([a * cos - b * sin, b * cos + a * sin], axis=0)


def features(z):
    half = z.shape[0] // 2

    def one(part):
        e = jnp.exp(part - jnp.max(part, axis=0, keepdims=True))
        return e / jnp.sum(e, axis=0, keepdims=True)

    return jnp.concatenate([one(z[:half]), one(z[half:])], axis=0)


def features_back(p, g):
    half = p.shape[0] // 2

    def one(pp, gg):
        return pp * (gg - jnp.sum(pp * gg, axis=0, keepdims=True))

    return one(p[:half], g[:half]) - one(p[half:], g[half:])


def masks(drow_ref, dcol_ref, q0, k0, count, heads):
    same = dcol_ref[k0 : k0 + count, :] == drow_ref[0:1, q0 : q0 + QB]
    dist = (
        lax.broadcasted_iota(jnp.int32, (count, QB), 1)
        - lax.broadcasted_iota(jnp.int32, (count, QB), 0)
        + (q0 - k0)
    )
    window = jnp.where(same & (dist >= 0) & (dist < WIN), 1.0, 0.0)
    linear = jnp.where(same & (dist >= WIN), 1.0, 0.0)
    return (
        jnp.concatenate([window] * heads, axis=1),
        jnp.concatenate([linear] * heads, axis=1),
    )


def side(parts):
    return jnp.concatenate(parts, axis=1)


def mixed_rows(win_part, lin_part, w0, l1, n):
    pieces = []
    if w0 > 0:
        pieces.append(lin_part[:w0])
    pieces.append(lin_part[w0:l1] + win_part[: l1 - w0])
    pieces.append(win_part[l1 - w0 :])
    return jnp.concatenate(pieces, axis=0)


def block_pick(me_ref, place, blocks):
    me, n, per = me_ref[0], me_ref[1], me_ref[2]
    source = lax.rem(me - place // per + n, n) * per + lax.rem(place, per)
    out = blocks[0]
    for m in range(1, len(blocks)):
        out = jnp.where(source == m, blocks[m], out)
    return out


def lanes(ref, rows=slice(None)):
    return [ref[rows, m * QB : (m + 1) * QB] for m in range(ref.shape[1] // QB)]


def fwd_kernel(me_ref, q_ref, k_ref, v_ref, cos_ref, sin_ref, drow_ref, dcol_ref, fq_ref, fk_ref,
               qo, ko, vo, pqo, pko, atto, ctxo, mo, deno):
    heads = fq_ref.shape[0]
    hd = k_ref.shape[0]
    length = k_ref.shape[1]
    for block in range(length // QB):
        cols = slice(block * QB, (block + 1) * QB)
        cos, sin = cos_ref[:, cols], sin_ref[:, cols]
        ko[:, cols] = turned(block_pick(me_ref, block, lanes(k_ref)), cos, sin).astype(BF)
        vo[:, cols] = block_pick(me_ref, block, lanes(v_ref)).astype(BF)
        for j in range(heads):
            rows = slice(j * hd, (j + 1) * hd)
            qo[rows, cols] = turned(block_pick(me_ref, block, lanes(q_ref, rows)), cos, sin).astype(BF)
    kt = ko[...]
    vt = vo[...]
    keys = jnp.transpose(kt.astype(F32)).astype(BF)
    pkt = features(nn(fk_ref[0], kt)).astype(BF)
    pko[...] = pkt
    pk = jnp.transpose(pkt.astype(F32)).astype(BF)
    for j in range(heads):
        qt = qo[j * hd : (j + 1) * hd, :]
        pqo[j * 2 * hd : (j + 1) * 2 * hd, :] = features(nn(fq_ref[j], qt)).astype(BF)
    for q0 in range(0, length, QB):
        n = q0 + QB
        w0 = max(q0 - WIN, 0)
        l1 = n - WIN
        qcat = side([qo[j * hd : (j + 1) * hd, q0:n] for j in range(heads)])
        pcat = side([pqo[j * 2 * hd : (j + 1) * 2 * hd, q0:n] for j in range(heads)])
        window, _ = masks(drow_ref, dcol_ref, q0, w0, n - w0, heads)
        _, linear = masks(drow_ref, dcol_ref, q0, 0, l1, heads)
        s = nn(keys[w0:n], qcat) * hd ** (-0.5)
        s = jnp.where(window > 0, s, -1e30)
        m = jnp.max(s, axis=0, keepdims=True)
        w = jnp.exp(s - m)
        kd = jnp.where(linear > 0, nn(pk[:l1], pcat) * jnp.exp(-m), 0.0)
        den = jnp.sum(w, axis=0, keepdims=True) + jnp.sum(kd, axis=0, keepdims=True)
        a = mixed_rows(w, kd, w0, l1, n).astype(BF)
        out = nn(vt[:, :n], a) / den
        for j in range(heads):
            cols = slice(j * QB, (j + 1) * QB)
            atto[j * hd : (j + 1) * hd, q0:n] = out[:, cols]
            mo[0, j : j + 1, q0:n] = m[:, cols]
            deno[0, j : j + 1, q0:n] = den[:, cols]
    for place in range(length // QB):
        ctxo[:, place * QB : (place + 1) * QB] = block_pick(me_ref, place, lanes(atto)).astype(BF)


def bwd_kernel(me_ref, q_ref, k_ref, v_ref, pq_ref, pk_ref, att_ref, m_ref, den_ref, g_ref,
               cos_ref, sin_ref, drow_ref, dcol_ref, fq_ref, fk_ref,
               dqo, dko, dvo, dfqo, dfko,
               dq_s, dpq_s, dk_s, dv_s, dpk_s):
    heads = fq_ref.shape[0]
    hd = k_ref.shape[0]
    length = k_ref.shape[1]
    cos, sin = cos_ref[...], sin_ref[...]
    kt = k_ref[...]
    pkt = pk_ref[...]
    keys = jnp.transpose(kt.astype(F32)).astype(BF)
    vals = jnp.transpose(v_ref[...].astype(F32)).astype(BF)
    pk = jnp.transpose(pkt.astype(F32)).astype(BF)

    def store(ref, rows, value):
        for place in range(length // QB):
            block = block_pick(me_ref, place, [value[:, p : p + QB] for p in range(0, length, QB)])
            ref[rows, place * QB : (place + 1) * QB] = block.astype(BF)

    dk_s[...] = jnp.zeros_like(dk_s)
    dv_s[...] = jnp.zeros_like(dv_s)
    dpk_s[...] = jnp.zeros_like(dpk_s)
    scale = hd ** (-0.5)
    for q0 in range(0, length, QB):
        n = q0 + QB
        w0 = max(q0 - WIN, 0)
        l1 = n - WIN
        qcat = side([q_ref[j * hd : (j + 1) * hd, q0:n] for j in range(heads)])
        pcat = side([pq_ref[j * 2 * hd : (j + 1) * 2 * hd, q0:n] for j in range(heads)])
        gcat = block_pick(
            me_ref, q0 // QB,
            [side([g_ref[j * hd : (j + 1) * hd, p : p + QB] for j in range(heads)]).astype(F32)
             for p in range(0, length, QB)],
        ).astype(BF)
        acat = side([att_ref[j * hd : (j + 1) * hd, q0:n] for j in range(heads)])
        m = side([m_ref[0, j : j + 1, q0:n] for j in range(heads)])
        rden = 1.0 / side([den_ref[0, j : j + 1, q0:n] for j in range(heads)])
        gf = gcat.astype(F32)
        c = jnp.sum(gf * acat, axis=0, keepdims=True)
        window, _ = masks(drow_ref, dcol_ref, q0, w0, n - w0, heads)
        _, linear = masks(drow_ref, dcol_ref, q0, 0, l1, heads)
        db = (nn(vals[:n], gcat) - c) * rden
        s = nn(keys[w0:n], qcat) * scale
        s = jnp.where(window > 0, s, -1e30)
        w = jnp.exp(s - m)
        d = jnp.exp(-m)
        kd = jnp.where(linear > 0, nn(pk[:l1], pcat) * d, 0.0)
        b = mixed_rows(w, kd, w0, l1, n)
        dv_s[0:n, :] += nt(b.astype(BF), (gf * rden).astype(BF))
        dm = -jnp.sum(b * db, axis=0, keepdims=True)
        top = jnp.where(s == m, 1.0, 0.0)
        ties = jnp.sum(top, axis=0, keepdims=True)
        ds = ((w * db[w0:] + top * (dm / ties)) * scale).astype(BF)
        dqw = tn(keys[w0:n], ds)
        dk_s[w0:n, :] += nt(ds, qcat)
        dker = jnp.where(linear > 0, db[:l1] * d, 0.0).astype(BF)
        dpq = tn(pk[:l1], dker)
        dpk_s[0:l1, :] += nt(dker, pcat)
        for j in range(heads):
            cols = slice(j * QB, (j + 1) * QB)
            dq_s[j * hd : (j + 1) * hd, q0:n] = dqw[:, cols]
            dpq_s[j * 2 * hd : (j + 1) * 2 * hd, q0:n] = dpq[:, cols]
    for j in range(heads):
        rows = slice(j * hd, (j + 1) * hd)
        wide = slice(j * 2 * hd, (j + 1) * 2 * hd)
        dz = features_back(pq_ref[wide, :].astype(F32), dpq_s[wide, :]).astype(BF)
        dfqo[j] = nt(q_ref[rows, :], dz)
        store(dqo, rows, turned(dq_s[rows, :] + nn(fq_ref[j], dz), cos, -sin))
    dz = features_back(pkt.astype(F32), jnp.transpose(dpk_s[...])).astype(BF)
    dfko[0] = nt(kt, dz)
    dk = jnp.transpose(dk_s[...]) + nn(fk_ref[0], dz)
    store(dko, slice(None), turned(dk, cos, -sin))
    store(dvo, slice(None), jnp.transpose(dv_s[...]))


def attn_specs(nq, nk, hd, length):
    heads = nq // nk
    whole = lambda shape: pl.BlockSpec(shape, lambda g: (0,) * len(shape))
    return dict(
        me=pl.BlockSpec(memory_space=pltpu.SMEM),
        q=pl.BlockSpec((heads * hd, length), lambda g: (g, 0)),
        k=pl.BlockSpec((hd, length), lambda g: (g, 0)),
        kin=pl.BlockSpec((hd, length), lambda g: (nq + g, 0)),
        vin=pl.BlockSpec((hd, length), lambda g: (nq + nk + g, 0)),
        pq=pl.BlockSpec((2 * heads * hd, length), lambda g: (g, 0)),
        pk=pl.BlockSpec((2 * hd, length), lambda g: (g, 0)),
        row=pl.BlockSpec((1, heads, length), lambda g: (g, 0, 0)),
        angle=whole((hd // 2, length)),
        drow=whole((1, length)),
        dcol=whole((length, QB)),
        fq2=pl.BlockSpec((heads, 2 * hd, hd), lambda g: (g, 0, 0)),
        fk2=pl.BlockSpec((1, 2 * hd, hd), lambda g: (g, 0, 0)),
        fq=pl.BlockSpec((heads, hd, hd), lambda g: (g, 0, 0)),
        fk=pl.BlockSpec((1, hd, hd), lambda g: (g, 0, 0)),
    )


def attn_fwd(me, proj, cos, sin, drow, dcol, fq2, fk2):
    nq, nk, hd = fq2.shape[0], fk2.shape[0], fq2.shape[2]
    length = proj.shape[1]
    heads = nq // nk
    sp = attn_specs(nq, nk, hd, length)
    sds = jax.ShapeDtypeStruct
    pairs = length * length * nq
    return pl.pallas_call(
        fwd_kernel,
        grid=(nk,),
        in_specs=[sp["me"], sp["q"], sp["kin"], sp["vin"], sp["angle"], sp["angle"], sp["drow"], sp["dcol"],
                  sp["fq2"], sp["fk2"]],
        out_specs=[sp["q"], sp["k"], sp["k"], sp["pq"], sp["pk"], sp["q"], sp["q"], sp["row"], sp["row"]],
        out_shape=[
            sds((nq * hd, length), BF), sds((nk * hd, length), BF), sds((nk * hd, length), BF),
            sds((2 * nq * hd, length), BF), sds((2 * nk * hd, length), BF),
            sds((nq * hd, length), F32), sds((nq * hd, length), BF),
            sds((nk, heads, length), F32), sds((nk, heads, length), F32),
        ],
        cost_estimate=pl.CostEstimate(flops=8 * pairs * hd, bytes_accessed=8 << 20, transcendentals=pairs),
        compiler_params=pltpu.CompilerParams(vmem_limit_bytes=48 << 20),
        name="attn_fwd",
    )(me, proj, proj, proj, cos, sin, drow, dcol, fq2, fk2)


def attn_bwd(me, saved, g, cos, sin, drow, dcol, fq, fk):
    qt, kt, vt, pq, pk, att, m, den = saved
    nq, nk, hd = fq.shape[0], fk.shape[0], fq.shape[2]
    length = qt.shape[1]
    heads = nq // nk
    sp = attn_specs(nq, nk, hd, length)
    sds = jax.ShapeDtypeStruct
    pairs = length * length * nq
    return pl.pallas_call(
        bwd_kernel,
        grid=(nk,),
        in_specs=[sp["me"], sp["q"], sp["k"], sp["k"], sp["pq"], sp["pk"], sp["q"], sp["row"], sp["row"], sp["q"],
                  sp["angle"], sp["angle"], sp["drow"], sp["dcol"], sp["fq"], sp["fk"]],
        out_specs=[sp["q"], sp["k"], sp["k"], sp["fq"], sp["fk"]],
        out_shape=[
            sds((nq * hd, length), BF), sds((nk * hd, length), BF), sds((nk * hd, length), BF),
            sds((nq, hd, hd), F32), sds((nk, hd, hd), F32),
        ],
        scratch_shapes=[
            pltpu.VMEM((heads * hd, length), F32),
            pltpu.VMEM((2 * heads * hd, length), F32),
            pltpu.VMEM((length, hd), F32),
            pltpu.VMEM((length, hd), F32),
            pltpu.VMEM((length, 2 * hd), F32),
        ],
        cost_estimate=pl.CostEstimate(flops=20 * pairs * hd, bytes_accessed=8 << 20, transcendentals=pairs),
        compiler_params=pltpu.CompilerParams(vmem_limit_bytes=48 << 20),
        name="attn_bwd",
    )(me, qt, kt, vt, pq, pk, att, m, den, g, cos, sin, drow, dcol, fq, fk)


def ffn_kernel(x_ref, g_ref, wg_ref, wu_ref, wd_ref, out_ref, back_ref, prod_ref, dgate_ref, dup_ref,
               out_acc, back_acc):
    step = pl.program_id(1)
    x = x_ref[...]
    gate = nn(x, wg_ref[...])
    up = nn(x, wu_ref[...])
    sg = jax.nn.sigmoid(gate)
    act = gate * sg
    prod = (act * up).astype(BF)
    prod_ref[...] = prod
    gp = nt(g_ref[...], wd_ref[...])
    dgate = (gp * up * (sg + act * (1.0 - sg))).astype(BF)
    dup = (gp * act).astype(BF)
    dgate_ref[...] = dgate
    dup_ref[...] = dup
    out = nn(prod, wd_ref[...])
    back = nt(dgate, wg_ref[...]) + nt(dup, wu_ref[...])

    @pl.when(step == 0)
    def _():
        out_acc[...] = out
        back_acc[...] = back

    @pl.when(step > 0)
    def _():
        out_acc[...] += out
        back_acc[...] += back

    @pl.when(step == pl.num_programs(1) - 1)
    def _():
        out_ref[...] = out_acc[...].astype(BF)
        back_ref[...] = back_acc[...].astype(BF)


def ffn_both(x, g, w_both, wd):
    length, width = x.shape
    ff = wd.shape[0]
    tm, tf = min(512, length), min(512, ff)
    rows = pl.BlockSpec((tm, width), lambda i, j: (i, 0))
    cols = pl.BlockSpec((width, tf), lambda i, j: (0, j))
    tile = pl.BlockSpec((tm, tf), lambda i, j: (i, j))
    more = pl.BlockSpec((width, tf), lambda i, j: (0, ff // tf + j))
    sds = jax.ShapeDtypeStruct
    return pl.pallas_call(
        ffn_kernel,
        grid=(length // tm, ff // tf),
        in_specs=[rows, rows, cols, more, pl.BlockSpec((tf, width), lambda i, j: (j, 0))],
        out_specs=[rows, rows, tile, tile, tile],
        out_shape=[sds((length, width), BF)] * 2 + [sds((length, ff), BF)] * 3,
        scratch_shapes=[pltpu.VMEM((tm, width), F32)] * 2,
        cost_estimate=pl.CostEstimate(
            flops=12 * length * width * ff, bytes_accessed=6 * width * ff, transcendentals=length * ff
        ),
        compiler_params=pltpu.CompilerParams(vmem_limit_bytes=56 << 20),
        name="ffn_both",
    )(x, g, w_both, w_both, wd)


def weight_grad(pairs, x_dim, y_dim, by_rows, side_index, others=None, add=None):
    x0, y0 = pairs[0]
    tokens, rows, cols = x0.shape[x_dim], x0.shape[1 - x_dim], y0.shape[1 - y_dim]
    groups = lax.axis_size("grp")
    half = groups // 2
    count = len(pairs)
    extra = 0 if add is None else 1

    def kernel(side_ref, *refs):
        out = refs[-1]

        def cut(ref, dim, size, which):
            place = slice(which * size, (which + 1) * size)
            return ref[:, place] if dim == 0 else ref[place, :]

        for which in range(2):

            @pl.when(side_ref[0] == which)
            def _(which=which):
                total = None
                for k in range(count):
                    x, y = refs[2 * k], refs[2 * k + 1]
                    x = cut(x, x_dim, tm, which) if by_rows else x[...]
                    y = y[...] if by_rows else cut(y, y_dim, tn, which)
                    part = lax.dot_general(x, y, (((x_dim,), (y_dim,)), ((), ())), preferred_element_type=F32)
                    total = part if total is None else total + part
                total = total.reshape(out.shape)
                if extra:
                    total = total + refs[2 * count][...].astype(F32)
                out[...] = total.astype(BF)

    def spec(dim, size, where):
        if dim == 0:
            return pl.BlockSpec((tokens, size), lambda i, j: (0, where(i, j)))
        return pl.BlockSpec((size, tokens), lambda i, j: (where(i, j), 0))

    if by_rows:
        shards = lax.axis_size("shard")
        part = rows // shards // groups
        tm, tn = half * part, cols
        grid = (shards, 1)
        xs = spec(x_dim, 2 * tm, lambda i, j: i)
        ys = spec(y_dim, tn, lambda i, j: j)
        shape = (half, shards, part, cols)
        block = pl.BlockSpec((half, 1, part, tn), lambda i, j: (0, i, 0, j))
    else:
        tm, tn = min(1024, rows), cols // groups
        grid = (rows // tm, half)
        xs = spec(x_dim, tm, lambda i, j: i)
        ys = spec(y_dim, 2 * tn, lambda i, j: j)
        shape = (half, rows, tn)
        block = pl.BlockSpec((1, tm, tn), lambda i, j: (j, i, 0))
    return pl.pallas_call(
        kernel,
        grid=grid,
        in_specs=[pl.BlockSpec(memory_space=pltpu.SMEM)] + [xs, ys] * count + [block] * extra,
        out_specs=block,
        out_shape=jax.ShapeDtypeStruct(shape, BF),
        cost_estimate=pl.CostEstimate(
            flops=count * tokens * rows * cols, bytes_accessed=rows * cols, transcendentals=0
        ),
        compiler_params=pltpu.CompilerParams(vmem_limit_bytes=48 << 20),
        name="weight_grad",
    )(side_index, *[a for pair in pairs for a in pair], *([add] if extra else []))


def tie(x, *others):
    return lax.optimization_barrier((x,) + others)[0] if others else x


def gather_small(x):
    SCOPE[0] = "small"
    n = lax.axis_size("shard")
    x = now(x)
    return [x] + [permute(x, "shard", [(k, (k + t) % n) for k in range(n)]) for t in range(1, n)]


SCOPE = ["start"]


def permute(x, axis, pairs):
    Clock.sent.append(x)
    with jax.named_scope(SCOPE[0]):
        return lax.ppermute(x, axis, pairs)


class Clock:
    before, here, sent = [], [], []


def now(x):
    return tie(x, *Clock.before)


def beside(x):
    return tie(x, *Clock.before, *Clock.sent)


def put(*values):
    Clock.here.extend(values)


def tick():
    Clock.before, Clock.here, Clock.sent = Clock.here, [], []


class Gather:
    def __init__(self, x, name="gather"):
        self.name = name
        self.x, self.up, self.down = x, x, x
        self.ups, self.downs = [], []

    def step(self):
        n, t = lax.axis_size("shard"), len(self.ups) + 1
        if t >= n:
            return
        SCOPE[0] = self.name + str(t)
        self.up = permute(now(self.up), "shard", [(k, k + 1) for k in range(t - 1, n - 1)])
        self.down = permute(now(self.down), "shard", [(k, k - 1) for k in range(n - t, 0, -1)])
        self.ups.append(self.up)
        self.downs.append(self.down)
        put(self.up, self.down)

    def last(self):
        while len(self.ups) + 1 < lax.axis_size("shard"):
            self.step()

    def result(self):
        n, i = lax.axis_size("shard"), lax.axis_index("shard")
        blocks = [jnp.where(i >= t, now(self.ups[t - 1]), now(self.downs[n - t - 1])) for t in range(1, n)]
        return jnp.concatenate([self.x] + blocks)


class Scatter:
    def __init__(self, x, name="scatter"):
        self.name = name
        n = lax.axis_size("shard")
        rows = x.shape[0] // n
        self.parts = [x[k * rows : (k + 1) * rows] for k in range(n)]
        self.got, self.t = {1: None, -1: None}, 0

    def step(self):
        n, t = len(self.parts), self.t + 1
        if t >= n:
            return
        SCOPE[0] = self.name + str(t)
        self.t = t
        for way in (1, -1):
            block = now(self.parts[t if way > 0 else n - t])
            if self.got[way] is not None:
                block = (block.astype(F32) + self.got[way].astype(F32)).astype(block.dtype)
            if way > 0:
                pairs = [(k, k + 1) for k in range(0, t)]
            else:
                pairs = [(k, k - 1) for k in range(n - 1, n - 1 - t, -1)]
            self.got[way] = permute(block, "shard", pairs)
            put(self.got[way])

    def last(self):
        while self.t + 1 < len(self.parts):
            self.step()

    def result(self):
        total = self.parts[0].astype(F32)
        for way in (1, -1):
            if self.got[way] is not None:
                total = total + self.got[way].astype(F32)
        return total


def gather_direct(x, name):
    SCOPE[0] = name
    n = lax.axis_size("shard")
    x = now(x)
    got = [permute(x, "shard", [(k, (k + t) % n) for k in range(n)]) for t in range(1, n)]
    put(*got)
    return [x] + got


def scatter_direct(x, name):
    SCOPE[0] = name
    n = lax.axis_size("shard")
    rows = x.shape[0] // n
    x = now(x)
    got = [
        permute(x[t * rows : (t + 1) * rows], "shard", [(k, (k - t) % n) for k in range(n)]) for t in range(1, n)
    ]
    put(*got)
    return functools.reduce(lambda a, c: a + c.astype(F32), got, x[:rows].astype(F32))


def in_order(blocks):
    n, i = lax.axis_size("shard"), lax.axis_index("shard")
    return [pick(i, [blocks[(m - j) % n] for m in range(n)]) for j in range(n)]


def pick(i, cases):
    out = cases[0]
    for m in range(1, len(cases)):
        out = jnp.where(i == m, cases[m], out)
    return out


def swap_z(parts, name="swap"):
    n, i = lax.axis_size("shard"), lax.axis_index("shard")
    SCOPE[0] = name
    parts = now(parts)
    out = [lax.dynamic_index_in_dim(parts, i, 0, False)]
    for t in range(1, n):
        block = lax.dynamic_index_in_dim(parts, (i + t) % n, 0, False)
        out.append(permute(block, "shard", [(k, (k + t) % n) for k in range(n)]))
    put(*out[1:])
    return out


def scatter_small(p):
    return functools.reduce(lambda a, c: a + c, [part.astype(F32) for part in swap_z(p)])


class SwappedRows:
    def __init__(self, name, pieces):
        self.name, self.pieces = name, pieces
        self.blocks = {0: self.part(lax.axis_index("shard"))}

    def part(self, d):
        n, size, g = lax.axis_size("shard"), lax.axis_size("grp"), lax.axis_index("grp")
        rows = self.pieces[0].shape[0] // size
        cut = []
        for w in self.pieces:
            cols = w.shape[1] // n
            cut.append(lax.dynamic_slice(w, (g * rows, d * cols), (rows, cols)))
        return jnp.concatenate(cut, axis=1) if len(cut) > 1 else cut[0]

    def step(self, *distances):
        SCOPE[0] = self.name
        n, i = lax.axis_size("shard"), lax.axis_index("shard")
        for t in distances:
            if 0 < t < n:
                block = now(self.part((i + t) % n))
                self.blocks[t] = permute(block, "shard", [(k, (k + t) % n) for k in range(n)])
                put(self.blocks[t])

    def result(self):
        n = lax.axis_size("shard")
        self.step(*[t for t in range(1, n) if t not in self.blocks])
        return jnp.stack(in_order([now(self.blocks[t]) for t in range(n)]))


def all_rows(part):
    n, rows, cols = part.shape
    return lax.all_gather(part, "grp", axis=1).reshape(n * lax.axis_size("grp") * rows, cols)


class Halves:
    def __init__(self, name, pairs, x_dim, y_dim, by_rows):
        self.name = name
        self.args = (pairs, x_dim, y_dim, by_rows)

    def half(self, which, **more):
        (x, y), *rest = self.args[0]
        which = jnp.stack([which]).astype(jnp.int32)
        return weight_grad([(beside(x), y)] + rest, *self.args[1:], which, **more)

    def send(self):
        self.sent = self.half(1 - lax.axis_index("grp") % 2)
        put(self.sent)

    def core(self):
        SCOPE[0] = self.name + "core"
        size = lax.axis_size("grp")
        self.come = permute(now(self.sent), "grp", [(k, k ^ 1) for k in range(size)])
        put(self.come)

    def keep(self):
        self.value = self.half(lax.axis_index("grp") % 2, add=self.come)
        put(self.value)

    def finish(self):
        size = lax.axis_size("grp")
        flat = now(self.value).reshape((-1,) + self.value.shape[2:])
        alike = [[k for k in range(size) if k % 2 == c] for c in range(2)]
        return lax.psum_scatter(flat, "grp", scatter_dimension=0, axis_index_groups=alike, tiled=True)


def column_grads(part, widths):
    n, size = lax.axis_size("shard"), lax.axis_size("grp")
    rows = part.shape[1]
    pieces, start = [], 0
    for group in widths:
        cols = []
        for width in group:
            cols.append(jnp.swapaxes(part[:, :, start : start + width], 0, 1).reshape(rows, n * width))
            start += width
        whole = jnp.concatenate(cols, axis=1) if len(cols) > 1 else cols[0]
        pieces.append(whole.reshape(rows, size, -1))
    moved = jnp.concatenate(pieces, axis=2) if len(pieces) > 1 else pieces[0]
    moved = lax.all_to_all(moved.reshape(rows, -1), "grp", 1, 0, tiled=True)
    moved = jnp.swapaxes(moved.reshape(size // 2, 2, rows, -1), 0, 1).reshape(size * rows, -1)
    outs, start = [], 0
    for piece in pieces:
        outs.append(moved[:, start : start + piece.shape[2]].astype(F32))
        start += piece.shape[2]
    return outs


def group_sum(x):
    SCOPE[0] = "groupsum"
    size = lax.axis_size("grp")
    step = 1
    while step < size:
        got = lax.ppermute(x, "grp", [(k, k ^ step) for k in range(size)])
        x = (x.astype(F32) + got.astype(F32)).astype(BF)
        step *= 2
    return x.astype(F32)


def norm_scale(h):
    return lax.rsqrt(jnp.mean(h * h, axis=-1, keepdims=True) + EPS)


def norm_back(h, gain, gn):
    r = norm_scale(h)
    g = gn * gain
    grad = r * g - h * (r * r * r) * jnp.mean(g * h, axis=-1, keepdims=True)
    return grad, jnp.sum(gn * h * r, axis=0)


def body(
    tokens,
    cotangent,
    sequence_lengths,
    attention_norm_gain,
    query_matrix,
    key_value_matrix,
    output_matrix,
    adapter_down_maps,
    adapter_up_query,
    adapter_up_key_value,
    adapter_down_output,
    adapter_up_output,
    query_feature_matrices,
    key_feature_matrices,
    feedforward_norm_gain,
    gate_matrix,
    up_matrix,
    down_matrix,
):
    n, shard, size = lax.axis_size("shard"), lax.axis_index("shard"), lax.axis_size("grp")
    batches, _, rows, width = tokens.shape
    length = n * rows
    share = width // n
    nq, hd = query_feature_matrices.shape[:2]
    nk = key_feature_matrices.shape[0]
    rank = adapter_up_query.shape[0]
    qw, kw = nq * hd, nk * hd
    ffq = down_matrix.shape[0]

    small = jnp.concatenate(
        [
            attention_norm_gain[None],
            feedforward_norm_gain[None],
            adapter_up_output,
            adapter_down_maps.T,
        ],
        axis=0,
    )
    half_kv = key_value_matrix.shape[1] // 2
    ends = jnp.cumsum(sequence_lengths[:, 0], axis=1)
    last = sequence_lengths.shape[2] - 2
    own = shard * rows + jnp.arange(rows, dtype=jnp.int32)
    gm_own = [jnp.where((own < ends[b, last])[:, None], cotangent[b, 0], 0) for b in range(batches)]
    me = jnp.stack([shard, jnp.int32(n), jnp.int32(rows // QB)]).astype(jnp.int32)
    Clock.before, Clock.here, Clock.sent = [], [], []
    tok = [Gather(tokens[b, 0], f"tok{b}x") for b in range(batches)]
    cot0 = Gather(gm_own[0], "cot0x")
    s_qkv = SwappedRows("sqkv", [query_matrix, key_value_matrix[:, :half_kv], key_value_matrix[:, half_kv:]])
    s_qkv.step(*range(1, n))
    tok[0].step()
    tick()
    w_qkv = all_rows(s_qkv.result())
    small_full = jnp.concatenate(in_order(gather_small(small)), axis=1)
    gain_attn = small_full[0].astype(F32)
    gain_ffn = small_full[1].astype(F32)
    up_output = small_full[2 : 2 + rank]
    down_maps_t = small_full[2 + rank :]
    tok[0].step()
    tick()
    tok[0].last()
    tick()
    tok[1].step()
    s_both = SwappedRows("sgu", [gate_matrix, up_matrix])
    s_both.step(1)
    pad = jnp.zeros((qw, -rank % 128), BF)
    out_wide = jnp.concatenate([output_matrix, adapter_down_output, pad], axis=1)
    zero = jnp.zeros
    u_all = jnp.concatenate(
        [
            jnp.concatenate([adapter_up_query, zero((rank, 2 * kw), BF)], axis=1),
            jnp.concatenate([zero((rank, qw), BF), adapter_up_key_value[0], zero((rank, kw), BF)], axis=1),
            jnp.concatenate([zero((rank, qw + kw), BF), adapter_up_key_value[1]], axis=1),
        ],
        axis=0,
    )

    begins = ends - sequence_lengths[:, 0]
    where = jnp.arange(length, dtype=jnp.int32)
    docs = jnp.sum((where[None, :, None] >= ends[:, None, :]).astype(jnp.int32), axis=2)
    relative = where[None] - jnp.max(
        jnp.where(where[None, :, None] >= begins[:, None, :], begins[:, None, :], 0), axis=2
    )
    freq = ROPE_BASE ** (-jnp.arange(hd // 2, dtype=F32) / (hd // 2))
    angles = freq[None, :, None] * relative.astype(F32)[:, None, :]
    cos_all, sin_all = jnp.cos(angles), jnp.sin(angles)

    def doubled(f):
        return jnp.swapaxes(jnp.concatenate([f, -f], axis=2), 1, 2)

    fq2, fk2 = doubled(query_feature_matrices), doubled(key_feature_matrices)

    def attention(b):
        x = beside(tok[b].result()).astype(F32)
        normed = (x * norm_scale(x) * gain_attn).astype(BF)
        mid = nt(normed, down_maps_t).astype(BF)
        proj = lax.dot_general(w_qkv, normed, (((0,), (1,)), ((), ())), preferred_element_type=F32)
        proj = proj + lax.dot_general(u_all, mid, (((0,), (1,)), ((), ())), preferred_element_type=F32)
        place = (
            cos_all[b],
            sin_all[b],
            docs[b][None],
            jnp.broadcast_to(docs[b][:, None], (length, QB)),
        )
        qt, kt, vt, pq, pk, att, ctx, m, den = attn_fwd(me, proj, *place, fq2, fk2)
        branch = tn(ctx, out_wide).astype(BF)
        put(branch)
        return dict(normed=normed, mid=mid, saved=(qt, kt, vt, pq, pk, att, m, den), ctx=ctx, place=place,
                    branch=Scatter(branch, f"br{b}x"))

    def after_attention(b):
        k = keep[b]
        branch = k["branch"].result()
        lora_own = branch[:, width : width + rank].astype(BF)
        x_own = tokens[b, 0].astype(F32)
        hidden = x_own + branch[:, :width] + nn(lora_own, up_output)
        normed_own = (hidden * norm_scale(hidden) * gain_ffn).astype(BF)
        k.update(lora=lora_own, x=x_own, hidden=hidden, send=Gather(normed_own, f"nf{b}x"))

    def ffn(b, cot):
        k = keep[b]
        nf = k["send"].result()
        out, back, product, dgate, dup = ffn_both(beside(nf), cot, w_both, down_matrix)
        put(dup)
        k.update(nf=nf, gm=cot, out=out, back=back, product=product, dgate=dgate, dup=dup)

    def after_ffn(b, gnf):
        k = keep[b]
        back, ffn_gain = norm_back(k["hidden"], gain_ffn, gnf)
        grad_hidden = gm_own[b].astype(F32) + back
        gb_own = grad_hidden.astype(BF)
        k.update(grad_hidden=grad_hidden, gb_own=gb_own, send=Gather(gb_own, f"gb{b}x"), ffn_gain=ffn_gain)

    def attention_back(b):
        k = keep[b]
        gb = beside(k["send"].result())
        glo = nt(gb, up_output)
        gctx = nt(output_matrix, gb) + nt(adapter_down_output.astype(F32), glo)
        dq, dk, dv, dfq, dfk = attn_bwd(
            me, k["saved"], gctx.astype(BF), *k["place"], query_feature_matrices, key_feature_matrices
        )
        dqkv = jnp.concatenate([dq, dk, dv], axis=0)
        glm = tn(dqkv, u_all.T)
        gn = lax.dot_general(dqkv, w_qkv, (((0,), (1,)), ((), ())), preferred_element_type=F32)
        gn = (gn + nn(glm, down_maps_t.astype(F32))).astype(BF)
        put(gn)
        k.update(gb=gb, glo=glo, dqkv=dqkv, glm=glm, dfq=dfq, dfk=dfk, gn=Scatter(gn, f"gn{b}x"))

    def pairs(one, two):
        return [(k[one], k[two]) for k in keep]

    tick()
    tok[1].step()
    s_both.step(n - 1)
    keep = [attention(0)]
    tick()
    s_both.step(*range(2, n - 1))
    keep[0]["branch"].step()
    tok[1].last()
    tick()
    w_both = all_rows(s_both.result())
    keep[0]["branch"].step()
    tick()
    keep[0]["branch"].last()
    keep.append(attention(1))
    tick()
    after_attention(0)
    keep[0]["send"].step()
    tick()
    keep[0]["send"].step()
    keep[1]["branch"].step()
    tick()
    keep[0]["send"].last()
    keep[1]["branch"].step()
    tick()
    keep[1]["branch"].last()
    cot0.step()
    tick()
    after_attention(1)
    keep[1]["send"].step()
    cot0.step()
    tick()
    keep[1]["send"].step()
    cot0.last()
    tick()
    keep[1]["send"].last()
    cot1 = gather_direct(gm_own[1], "cot1x")
    ffn(0, cot0.result())
    tick()
    gnf0 = scatter_direct(keep[0]["back"], "gnf0x")
    ffn(1, jnp.concatenate([now(c) for c in cot1]))
    tick()
    w_g = Halves("Wg", pairs("nf", "dgate"), 0, 0, True)
    w_u = Halves("Wu", pairs("nf", "dup"), 0, 0, True)
    w_d = Halves("Wd", pairs("product", "gm"), 0, 0, False)
    gnf1 = Scatter(keep[1]["back"], "gnf1x")
    out = [Scatter(k["out"], f"out{b}x") for b, k in enumerate(keep)]
    after_ffn(0, gnf0)
    keep[0]["send"].step()
    out[0].step()
    w_g.send()
    w_u.send()
    tick()
    keep[0]["send"].step()
    gnf1.step()
    w_g.core()
    w_d.send()
    tick()
    keep[0]["send"].last()
    gnf1.step()
    w_u.core()
    w_g.keep()
    tick()
    r_g = w_g.finish()
    gnf1.last()
    out[0].step()
    w_d.core()
    attention_back(0)
    tick()
    after_ffn(1, gnf1.result())
    keep[1]["send"].step()
    out[0].last()
    w_u.keep()
    tick()
    r_u = w_u.finish()
    keep[1]["send"].step()
    keep[0]["gn"].step()
    w_d.keep()
    tick()
    r_d = w_d.finish()
    keep[1]["send"].last()
    keep[0]["gn"].step()
    put(r_g)
    tick()
    keep[0]["gn"].last()
    t_g = swap_z(r_g.reshape(n, -1, ffq), "swapg")
    attention_back(1)
    w_q = Halves("Wq", pairs("normed", "dqkv"), 0, 1, True)
    w_o = Halves("Wo", pairs("ctx", "gb"), 1, 0, False)
    w_q.send()
    w_o.send()
    tick()
    keep[1]["gn"].step()
    out[1].step()
    w_q.core()
    w_o.core()
    put(r_u)
    tick()
    keep[1]["gn"].step()
    out[1].step()
    w_q.keep()
    w_o.keep()
    put(r_d)
    tick()
    r_q = w_q.finish()
    r_o = w_o.finish()
    keep[1]["gn"].last()
    t_u = swap_z(r_u.reshape(n, -1, ffq), "swapu")
    (grad_gate,) = column_grads(jnp.stack(in_order([now(t) for t in t_g])), [[ffq]])
    tick()
    (grad_up,) = column_grads(jnp.stack(in_order([now(t) for t in t_u])), [[ffq]])
    out[1].last()
    for k in keep:
        k["gn_sum"] = now(k["gn"].result())
    for k in keep:
        k["up_out"] = tn(k["lora"], k["gb_own"])
    token_grads = []
    for k in keep:
        back, attn_gain = norm_back(k["x"], gain_attn, k["gn_sum"])
        token_grads.append((k["grad_hidden"] + back).astype(BF))
        k.update(attn_gain=attn_gain)

    def both(name, axis=0):
        return jnp.concatenate([k[name] for k in keep], axis=axis)

    def added(name):
        return functools.reduce(lambda a, c: a + c, [k[name] for k in keep])

    normed = both("normed")
    ctx = both("ctx", 1)
    dqkv = both("dqkv", 1)
    glm = both("glm")
    down_maps_grad = tn(normed.astype(F32), glm)
    ups = lax.dot_general(both("mid"), dqkv, (((0,), (1,)), ((), ())), preferred_element_type=F32)
    down_out_grad = nn(ctx.astype(F32), both("glo"))
    spread = [
        added("attn_gain").reshape(n, share),
        added("ffn_gain").reshape(n, share),
        down_maps_grad.reshape(n, share * 3 * rank),
        jnp.swapaxes(added("up_out").reshape(rank, n, share), 0, 1).reshape(n, rank * share),
    ]
    lined = scatter_small(jnp.concatenate(spread, axis=1).astype(BF))
    local = [
        ups[:rank, :qw].reshape(-1),
        ups[rank : 2 * rank, qw : qw + kw].reshape(-1),
        ups[2 * rank :, qw + kw :].reshape(-1),
        down_out_grad.reshape(-1),
        added("dfq").reshape(-1),
        added("dfk").reshape(-1),
    ]
    t_q = jnp.stack(in_order(swap_z(r_q.reshape(n, -1, qw + 2 * kw), "swapq")))
    grad_query, grad_kv = column_grads(t_q, [[qw], [kw, kw]])
    grad_down = r_d.astype(F32)
    grad_output = r_o.astype(F32)
    output = [(k["hidden"] + o.result()).astype(BF) for k, o in zip(keep, out)]
    flat = group_sum(jnp.concatenate([lined] + local).astype(BF))
    shapes = [
        (share,),
        (share,),
        (share, 3 * rank),
        (rank, share),
        (rank, qw),
        (rank, kw),
        (rank, kw),
        (qw, rank),
        (nq, hd, hd),
        (nk, hd, hd),
    ]
    got, start = [], 0
    for shape in shapes:
        count = 1
        for extent in shape:
            count *= extent
        got.append(flat[start : start + count].reshape(shape))
        start += count
    g_attn, g_ffn, g_down_maps, g_up_out, g_up_q, g_up_k, g_up_v, g_down_out, g_fq, g_fk = got
    return (
        jnp.stack(output)[:, None],
        jnp.stack(token_grads)[:, None],
        g_attn,
        grad_query,
        grad_kv,
        grad_output,
        g_down_maps,
        g_up_q,
        jnp.stack([g_up_k, g_up_v]),
        g_down_out,
        g_up_out,
        g_fq,
        g_fk,
        g_ffn,
        grad_gate,
        grad_up,
        grad_down,
    )


def solution(mesh):
    placed = (
        P(None, "grp", "shard", None),
        P(None, "grp", "shard", None),
        P(None, "grp", None),
        P("shard"),
        P("shard", None),
        P("shard", None),
        P("shard", None),
        P("shard", None),
        P(None, "shard"),
        P(None, None, "shard"),
        P("shard", None),
        P(None, "shard"),
        P("shard", None, None),
        P("shard", None, None),
        P("shard"),
        P("shard", None),
        P("shard", None),
        P("shard", None),
    )
    return jax.shard_map(
        body,
        mesh=mesh,
        in_specs=placed,
        out_specs=(
            P(None, "grp", "shard", None),
            P(None, "grp", "shard", None),
            P("shard"),
            P("shard", "grp"),
            P("shard", "grp"),
            P("shard", "grp"),
            P("shard", None),
            P(None, "shard"),
            P(None, None, "shard"),
            P("shard", None),
            P(None, "shard"),
            P("shard", None, None),
            P("shard", None, None),
            P("shard"),
            P("shard", "grp"),
            P("shard", "grp"),
            P("shard", "grp"),
        ),
        check_vma=False,
    )
```

```python
import functools
import jax
import jax.numpy as jnp
from jax import lax
from jax.experimental import pallas as pl
from jax.experimental.pallas import tpu as pltpu
from jax.sharding import PartitionSpec as P

WIN = 64
EPS = 1e-05
ROPE_BASE = 500000.0
BF = jnp.bfloat16
F32 = jnp.float32
QB = 128


def nn(a, b):
    return lax.dot_general(a, b, (((1,), (0,)), ((), ())), preferred_element_type=F32)


def nt(a, b):
    return lax.dot_general(a, b, (((1,), (1,)), ((), ())), preferred_element_type=F32)


def tn(a, b):
    return lax.dot_general(a, b, (((0,), (0,)), ((), ())), preferred_element_type=F32)


def turned(x, cos, sin):
    half = x.shape[0] // 2
    a, b = x[:half], x[half:]
    return jnp.concatenate([a * cos - b * sin, b * cos + a * sin], axis=0)


def features(z):
    half = z.shape[0] // 2

    def one(part):
        e = jnp.exp(part - jnp.max(part, axis=0, keepdims=True))
        return e / jnp.sum(e, axis=0, keepdims=True)

    return jnp.concatenate([one(z[:half]), one(z[half:])], axis=0)


def features_back(p, g):
    half = p.shape[0] // 2

    def one(pp, gg):
        return pp * (gg - jnp.sum(pp * gg, axis=0, keepdims=True))

    return one(p[:half], g[:half]) - one(p[half:], g[half:])


def masks(drow_ref, dcol_ref, q0, k0, count, heads):
    same = dcol_ref[k0 : k0 + count, :] == drow_ref[0:1, q0 : q0 + QB]
    dist = (
        lax.broadcasted_iota(jnp.int32, (count, QB), 1)
        - lax.broadcasted_iota(jnp.int32, (count, QB), 0)
        + (q0 - k0)
    )
    window = jnp.where(same & (dist >= 0) & (dist < WIN), 1.0, 0.0)
    linear = jnp.where(same & (dist >= WIN), 1.0, 0.0)
    return (
        jnp.concatenate([window] * heads, axis=1),
        jnp.concatenate([linear] * heads, axis=1),
    )


def side(parts):
    return jnp.concatenate(parts, axis=1)


def mixed_rows(win_part, lin_part, w0, l1, n):
    pieces = []
    if w0 > 0:
        pieces.append(lin_part[:w0])
    pieces.append(lin_part[w0:l1] + win_part[: l1 - w0])
    pieces.append(win_part[l1 - w0 :])
    return jnp.concatenate(pieces, axis=0)


def block_pick(me_ref, place, blocks):
    me, n, per = me_ref[0], me_ref[1], me_ref[2]
    source = lax.rem(me - place // per + n, n) * per + lax.rem(place, per)
    out = blocks[0]
    for m in range(1, len(blocks)):
        out = jnp.where(source == m, blocks[m], out)
    return out


def lanes(ref, rows=slice(None)):
    return [ref[rows, m * QB : (m + 1) * QB] for m in range(ref.shape[1] // QB)]


def fwd_kernel(me_ref, q_ref, k_ref, v_ref, cos_ref, sin_ref, drow_ref, dcol_ref, fq_ref, fk_ref,
               qo, ko, vo, pqo, pko, atto, ctxo, mo, deno):
    heads = fq_ref.shape[0]
    hd = k_ref.shape[0]
    length = k_ref.shape[1]
    for block in range(length // QB):
        cols = slice(block * QB, (block + 1) * QB)
        cos, sin = cos_ref[:, cols], sin_ref[:, cols]
        ko[:, cols] = turned(block_pick(me_ref, block, lanes(k_ref)), cos, sin).astype(BF)
        vo[:, cols] = block_pick(me_ref, block, lanes(v_ref)).astype(BF)
        for j in range(heads):
            rows = slice(j * hd, (j + 1) * hd)
            qo[rows, cols] = turned(block_pick(me_ref, block, lanes(q_ref, rows)), cos, sin).astype(BF)
    kt = ko[...]
    vt = vo[...]
    keys = jnp.transpose(kt.astype(F32)).astype(BF)
    pkt = features(nn(fk_ref[0], kt)).astype(BF)
    pko[...] = pkt
    pk = jnp.transpose(pkt.astype(F32)).astype(BF)
    for j in range(heads):
        qt = qo[j * hd : (j + 1) * hd, :]
        pqo[j * 2 * hd : (j + 1) * 2 * hd, :] = features(nn(fq_ref[j], qt)).astype(BF)
    for q0 in range(0, length, QB):
        n = q0 + QB
        w0 = max(q0 - WIN, 0)
        l1 = n - WIN
        qcat = side([qo[j * hd : (j + 1) * hd, q0:n] for j in range(heads)])
        pcat = side([pqo[j * 2 * hd : (j + 1) * 2 * hd, q0:n] for j in range(heads)])
        window, _ = masks(drow_ref, dcol_ref, q0, w0, n - w0, heads)
        _, linear = masks(drow_ref, dcol_ref, q0, 0, l1, heads)
        s = nn(keys[w0:n], qcat) * hd ** (-0.5)
        s = jnp.where(window > 0, s, -1e30)
        m = jnp.max(s, axis=0, keepdims=True)
        w = jnp.exp(s - m)
        kd = jnp.where(linear > 0, nn(pk[:l1], pcat) * jnp.exp(-m), 0.0)
        den = jnp.sum(w, axis=0, keepdims=True) + jnp.sum(kd, axis=0, keepdims=True)
        a = mixed_rows(w, kd, w0, l1, n).astype(BF)
        out = nn(vt[:, :n], a) / den
        for j in range(heads):
            cols = slice(j * QB, (j + 1) * QB)
            atto[j * hd : (j + 1) * hd, q0:n] = out[:, cols]
            mo[0, j : j + 1, q0:n] = m[:, cols]
            deno[0, j : j + 1, q0:n] = den[:, cols]
    for place in range(length // QB):
        ctxo[:, place * QB : (place + 1) * QB] = block_pick(me_ref, place, lanes(atto)).astype(BF)


def bwd_kernel(me_ref, q_ref, k_ref, v_ref, pq_ref, pk_ref, att_ref, m_ref, den_ref, g_ref,
               cos_ref, sin_ref, drow_ref, dcol_ref, fq_ref, fk_ref,
               dqo, dko, dvo, dfqo, dfko,
               dq_s, dpq_s, dk_s, dv_s, dpk_s):
    heads = fq_ref.shape[0]
    hd = k_ref.shape[0]
    length = k_ref.shape[1]
    cos, sin = cos_ref[...], sin_ref[...]
    kt = k_ref[...]
    pkt = pk_ref[...]
    keys = jnp.transpose(kt.astype(F32)).astype(BF)
    vals = jnp.transpose(v_ref[...].astype(F32)).astype(BF)
    pk = jnp.transpose(pkt.astype(F32)).astype(BF)

    def store(ref, rows, value):
        for place in range(length // QB):
            block = block_pick(me_ref, place, [value[:, p : p + QB] for p in range(0, length, QB)])
            ref[rows, place * QB : (place + 1) * QB] = block.astype(BF)

    dk_s[...] = jnp.zeros_like(dk_s)
    dv_s[...] = jnp.zeros_like(dv_s)
    dpk_s[...] = jnp.zeros_like(dpk_s)
    scale = hd ** (-0.5)
    for q0 in range(0, length, QB):
        n = q0 + QB
        w0 = max(q0 - WIN, 0)
        l1 = n - WIN
        qcat = side([q_ref[j * hd : (j + 1) * hd, q0:n] for j in range(heads)])
        pcat = side([pq_ref[j * 2 * hd : (j + 1) * 2 * hd, q0:n] for j in range(heads)])
        gcat = block_pick(
            me_ref, q0 // QB,
            [side([g_ref[j * hd : (j + 1) * hd, p : p + QB] for j in range(heads)]).astype(F32)
             for p in range(0, length, QB)],
        ).astype(BF)
        acat = side([att_ref[j * hd : (j + 1) * hd, q0:n] for j in range(heads)])
        m = side([m_ref[0, j : j + 1, q0:n] for j in range(heads)])
        rden = 1.0 / side([den_ref[0, j : j + 1, q0:n] for j in range(heads)])
        gf = gcat.astype(F32)
        c = jnp.sum(gf * acat, axis=0, keepdims=True)
        window, _ = masks(drow_ref, dcol_ref, q0, w0, n - w0, heads)
        _, linear = masks(drow_ref, dcol_ref, q0, 0, l1, heads)
        db = (nn(vals[:n], gcat) - c) * rden
        s = nn(keys[w0:n], qcat) * scale
        s = jnp.where(window > 0, s, -1e30)
        w = jnp.exp(s - m)
        d = jnp.exp(-m)
        kd = jnp.where(linear > 0, nn(pk[:l1], pcat) * d, 0.0)
        b = mixed_rows(w, kd, w0, l1, n)
        dv_s[0:n, :] += nt(b.astype(BF), (gf * rden).astype(BF))
        dm = -jnp.sum(b * db, axis=0, keepdims=True)
        top = jnp.where(s == m, 1.0, 0.0)
        ties = jnp.sum(top, axis=0, keepdims=True)
        ds = ((w * db[w0:] + top * (dm / ties)) * scale).astype(BF)
        dqw = tn(keys[w0:n], ds)
        dk_s[w0:n, :] += nt(ds, qcat)
        dker = jnp.where(linear > 0, db[:l1] * d, 0.0).astype(BF)
        dpq = tn(pk[:l1], dker)
        dpk_s[0:l1, :] += nt(dker, pcat)
        for j in range(heads):
            cols = slice(j * QB, (j + 1) * QB)
            dq_s[j * hd : (j + 1) * hd, q0:n] = dqw[:, cols]
            dpq_s[j * 2 * hd : (j + 1) * 2 * hd, q0:n] = dpq[:, cols]
    for j in range(heads):
        rows = slice(j * hd, (j + 1) * hd)
        wide = slice(j * 2 * hd, (j + 1) * 2 * hd)
        dz = features_back(pq_ref[wide, :].astype(F32), dpq_s[wide, :]).astype(BF)
        dfqo[j] = nt(q_ref[rows, :], dz)
        store(dqo, rows, turned(dq_s[rows, :] + nn(fq_ref[j], dz), cos, -sin))
    dz = features_back(pkt.astype(F32), jnp.transpose(dpk_s[...])).astype(BF)
    dfko[0] = nt(kt, dz)
    dk = jnp.transpose(dk_s[...]) + nn(fk_ref[0], dz)
    store(dko, slice(None), turned(dk, cos, -sin))
    store(dvo, slice(None), jnp.transpose(dv_s[...]))


def attn_specs(nq, nk, hd, length):
    heads = nq // nk
    whole = lambda shape: pl.BlockSpec(shape, lambda g: (0,) * len(shape))
    return dict(
        me=pl.BlockSpec(memory_space=pltpu.SMEM),
        q=pl.BlockSpec((heads * hd, length), lambda g: (g, 0)),
        k=pl.BlockSpec((hd, length), lambda g: (g, 0)),
        kin=pl.BlockSpec((hd, length), lambda g: (nq + g, 0)),
        vin=pl.BlockSpec((hd, length), lambda g: (nq + nk + g, 0)),
        pq=pl.BlockSpec((2 * heads * hd, length), lambda g: (g, 0)),
        pk=pl.BlockSpec((2 * hd, length), lambda g: (g, 0)),
        row=pl.BlockSpec((1, heads, length), lambda g: (g, 0, 0)),
        angle=whole((hd // 2, length)),
        drow=whole((1, length)),
        dcol=whole((length, QB)),
        fq2=pl.BlockSpec((heads, 2 * hd, hd), lambda g: (g, 0, 0)),
        fk2=pl.BlockSpec((1, 2 * hd, hd), lambda g: (g, 0, 0)),
        fq=pl.BlockSpec((heads, hd, hd), lambda g: (g, 0, 0)),
        fk=pl.BlockSpec((1, hd, hd), lambda g: (g, 0, 0)),
    )


def attn_fwd(me, proj, cos, sin, drow, dcol, fq2, fk2):
    nq, nk, hd = fq2.shape[0], fk2.shape[0], fq2.shape[2]
    length = proj.shape[1]
    heads = nq // nk
    sp = attn_specs(nq, nk, hd, length)
    sds = jax.ShapeDtypeStruct
    pairs = length * length * nq
    return pl.pallas_call(
        fwd_kernel,
        grid=(nk,),
        in_specs=[sp["me"], sp["q"], sp["kin"], sp["vin"], sp["angle"], sp["angle"], sp["drow"], sp["dcol"],
                  sp["fq2"], sp["fk2"]],
        out_specs=[sp["q"], sp["k"], sp["k"], sp["pq"], sp["pk"], sp["q"], sp["q"], sp["row"], sp["row"]],
        out_shape=[
            sds((nq * hd, length), BF), sds((nk * hd, length), BF), sds((nk * hd, length), BF),
            sds((2 * nq * hd, length), BF), sds((2 * nk * hd, length), BF),
            sds((nq * hd, length), F32), sds((nq * hd, length), BF),
            sds((nk, heads, length), F32), sds((nk, heads, length), F32),
        ],
        cost_estimate=pl.CostEstimate(flops=8 * pairs * hd, bytes_accessed=8 << 20, transcendentals=pairs),
        compiler_params=pltpu.CompilerParams(vmem_limit_bytes=48 << 20),
        name="attn_fwd",
    )(me, proj, proj, proj, cos, sin, drow, dcol, fq2, fk2)


def attn_bwd(me, saved, g, cos, sin, drow, dcol, fq, fk):
    qt, kt, vt, pq, pk, att, m, den = saved
    nq, nk, hd = fq.shape[0], fk.shape[0], fq.shape[2]
    length = qt.shape[1]
    heads = nq // nk
    sp = attn_specs(nq, nk, hd, length)
    sds = jax.ShapeDtypeStruct
    pairs = length * length * nq
    return pl.pallas_call(
        bwd_kernel,
        grid=(nk,),
        in_specs=[sp["me"], sp["q"], sp["k"], sp["k"], sp["pq"], sp["pk"], sp["q"], sp["row"], sp["row"], sp["q"],
                  sp["angle"], sp["angle"], sp["drow"], sp["dcol"], sp["fq"], sp["fk"]],
        out_specs=[sp["q"], sp["k"], sp["k"], sp["fq"], sp["fk"]],
        out_shape=[
            sds((nq * hd, length), BF), sds((nk * hd, length), BF), sds((nk * hd, length), BF),
            sds((nq, hd, hd), F32), sds((nk, hd, hd), F32),
        ],
        scratch_shapes=[
            pltpu.VMEM((heads * hd, length), F32),
            pltpu.VMEM((2 * heads * hd, length), F32),
            pltpu.VMEM((length, hd), F32),
            pltpu.VMEM((length, hd), F32),
            pltpu.VMEM((length, 2 * hd), F32),
        ],
        cost_estimate=pl.CostEstimate(flops=20 * pairs * hd, bytes_accessed=8 << 20, transcendentals=pairs),
        compiler_params=pltpu.CompilerParams(vmem_limit_bytes=48 << 20),
        name="attn_bwd",
    )(me, qt, kt, vt, pq, pk, att, m, den, g, cos, sin, drow, dcol, fq, fk)


def ffn_kernel(x_ref, g_ref, wg_ref, wu_ref, wd_ref, out_ref, back_ref, prod_ref, dgate_ref, dup_ref,
               out_acc, back_acc):
    step = pl.program_id(1)
    x = x_ref[...]
    gate = nn(x, wg_ref[...])
    up = nn(x, wu_ref[...])
    sg = jax.nn.sigmoid(gate)
    act = gate * sg
    prod = (act * up).astype(BF)
    prod_ref[...] = prod
    gp = nt(g_ref[...], wd_ref[...])
    dgate = (gp * up * (sg + act * (1.0 - sg))).astype(BF)
    dup = (gp * act).astype(BF)
    dgate_ref[...] = dgate
    dup_ref[...] = dup
    out = nn(prod, wd_ref[...])
    back = nt(dgate, wg_ref[...]) + nt(dup, wu_ref[...])

    @pl.when(step == 0)
    def _():
        out_acc[...] = out
        back_acc[...] = back

    @pl.when(step > 0)
    def _():
        out_acc[...] += out
        back_acc[...] += back

    @pl.when(step == pl.num_programs(1) - 1)
    def _():
        out_ref[...] = out_acc[...].astype(BF)
        back_ref[...] = back_acc[...].astype(BF)


def ffn_both(x, g, w_both, wd):
    length, width = x.shape
    ff = wd.shape[0]
    tm, tf = min(512, length), min(512, ff)
    rows = pl.BlockSpec((tm, width), lambda i, j: (i, 0))
    cols = pl.BlockSpec((width, tf), lambda i, j: (0, j))
    tile = pl.BlockSpec((tm, tf), lambda i, j: (i, j))
    more = pl.BlockSpec((width, tf), lambda i, j: (0, ff // tf + j))
    sds = jax.ShapeDtypeStruct
    return pl.pallas_call(
        ffn_kernel,
        grid=(length // tm, ff // tf),
        in_specs=[rows, rows, cols, more, pl.BlockSpec((tf, width), lambda i, j: (j, 0))],
        out_specs=[rows, rows, tile, tile, tile],
        out_shape=[sds((length, width), BF)] * 2 + [sds((length, ff), BF)] * 3,
        scratch_shapes=[pltpu.VMEM((tm, width), F32)] * 2,
        cost_estimate=pl.CostEstimate(
            flops=12 * length * width * ff, bytes_accessed=6 * width * ff, transcendentals=length * ff
        ),
        compiler_params=pltpu.CompilerParams(vmem_limit_bytes=56 << 20),
        name="ffn_both",
    )(x, g, w_both, w_both, wd)


def weight_grad(pairs, x_dim, y_dim, by_rows, side_index, others=None, add=None):
    x0, y0 = pairs[0]
    tokens, rows, cols = x0.shape[x_dim], x0.shape[1 - x_dim], y0.shape[1 - y_dim]
    groups = lax.axis_size("grp")
    half = groups // 2
    count = len(pairs)
    extra = 0 if add is None else 1

    def kernel(side_ref, *refs):
        out = refs[-1]

        def cut(ref, dim, size, which):
            place = slice(which * size, (which + 1) * size)
            return ref[:, place] if dim == 0 else ref[place, :]

        for which in range(2):

            @pl.when(side_ref[0] == which)
            def _(which=which):
                total = None
                for k in range(count):
                    x, y = refs[2 * k], refs[2 * k + 1]
                    x = cut(x, x_dim, tm, which) if by_rows else x[...]
                    y = y[...] if by_rows else cut(y, y_dim, tn, which)
                    part = lax.dot_general(x, y, (((x_dim,), (y_dim,)), ((), ())), preferred_element_type=F32)
                    total = part if total is None else total + part
                total = total.reshape(out.shape)
                if extra:
                    total = total + refs[2 * count][...].astype(F32)
                out[...] = total.astype(BF)

    def spec(dim, size, where):
        if dim == 0:
            return pl.BlockSpec((tokens, size), lambda i, j: (0, where(i, j)))
        return pl.BlockSpec((size, tokens), lambda i, j: (where(i, j), 0))

    if by_rows:
        shards = lax.axis_size("shard")
        part = rows // shards // groups
        tm, tn = half * part, cols
        grid = (shards, 1)
        xs = spec(x_dim, 2 * tm, lambda i, j: i)
        ys = spec(y_dim, tn, lambda i, j: j)
        shape = (half, shards, part, cols)
        block = pl.BlockSpec((half, 1, part, tn), lambda i, j: (0, i, 0, j))
    else:
        tm, tn = min(1024, rows), cols // groups
        grid = (rows // tm, half)
        xs = spec(x_dim, tm, lambda i, j: i)
        ys = spec(y_dim, 2 * tn, lambda i, j: j)
        shape = (half, rows, tn)
        block = pl.BlockSpec((1, tm, tn), lambda i, j: (j, i, 0))
    return pl.pallas_call(
        kernel,
        grid=grid,
        in_specs=[pl.BlockSpec(memory_space=pltpu.SMEM)] + [xs, ys] * count + [block] * extra,
        out_specs=block,
        out_shape=jax.ShapeDtypeStruct(shape, BF),
        cost_estimate=pl.CostEstimate(
            flops=count * tokens * rows * cols, bytes_accessed=rows * cols, transcendentals=0
        ),
        compiler_params=pltpu.CompilerParams(vmem_limit_bytes=48 << 20),
        name="weight_grad",
    )(side_index, *[a for pair in pairs for a in pair], *([add] if extra else []))


def tie(x, *others):
    return lax.optimization_barrier((x,) + others)[0] if others else x


def gather_small(x):
    SCOPE[0] = "small"
    n = lax.axis_size("shard")
    x = now(x)
    return [x] + [permute(x, "shard", [(k, (k + t) % n) for k in range(n)]) for t in range(1, n)]


SCOPE = ["start"]


def permute(x, axis, pairs):
    Clock.sent.append(x)
    with jax.named_scope(SCOPE[0]):
        return lax.ppermute(x, axis, pairs)


class Clock:
    before, here, sent = [], [], []


def now(x):
    return tie(x, *Clock.before)


def beside(x):
    return tie(x, *Clock.before, *Clock.sent)


def put(*values):
    Clock.here.extend(values)


def tick():
    Clock.before, Clock.here, Clock.sent = Clock.here, [], []


class Gather:
    def __init__(self, x, name="gather"):
        self.name = name
        self.x, self.up, self.down = x, x, x
        self.ups, self.downs = [], []

    def step(self):
        n, t = lax.axis_size("shard"), len(self.ups) + 1
        if t >= n:
            return
        SCOPE[0] = self.name + str(t)
        self.up = permute(now(self.up), "shard", [(k, k + 1) for k in range(t - 1, n - 1)])
        self.down = permute(now(self.down), "shard", [(k, k - 1) for k in range(n - t, 0, -1)])
        self.ups.append(self.up)
        self.downs.append(self.down)
        put(self.up, self.down)

    def last(self):
        while len(self.ups) + 1 < lax.axis_size("shard"):
            self.step()

    def result(self):
        n, i = lax.axis_size("shard"), lax.axis_index("shard")
        blocks = [jnp.where(i >= t, now(self.ups[t - 1]), now(self.downs[n - t - 1])) for t in range(1, n)]
        return jnp.concatenate([self.x] + blocks)


class Scatter:
    def __init__(self, x, name="scatter"):
        self.name = name
        n = lax.axis_size("shard")
        rows = x.shape[0] // n
        self.parts = [x[k * rows : (k + 1) * rows] for k in range(n)]
        self.got, self.t = {1: None, -1: None}, 0

    def step(self):
        n, t = len(self.parts), self.t + 1
        if t >= n:
            return
        SCOPE[0] = self.name + str(t)
        self.t = t
        for way in (1, -1):
            block = now(self.parts[t if way > 0 else n - t])
            if self.got[way] is not None:
                block = (block.astype(F32) + self.got[way].astype(F32)).astype(block.dtype)
            if way > 0:
                pairs = [(k, k + 1) for k in range(0, t)]
            else:
                pairs = [(k, k - 1) for k in range(n - 1, n - 1 - t, -1)]
            self.got[way] = permute(block, "shard", pairs)
            put(self.got[way])

    def last(self):
        while self.t + 1 < len(self.parts):
            self.step()

    def result(self):
        total = self.parts[0].astype(F32)
        for way in (1, -1):
            if self.got[way] is not None:
                total = total + self.got[way].astype(F32)
        return total


def gather_direct(x, name):
    SCOPE[0] = name
    n = lax.axis_size("shard")
    x = now(x)
    got = [permute(x, "shard", [(k, (k + t) % n) for k in range(n)]) for t in range(1, n)]
    put(*got)
    return [x] + got


def scatter_direct(x, name):
    SCOPE[0] = name
    n = lax.axis_size("shard")
    rows = x.shape[0] // n
    x = now(x)
    got = [
        permute(x[t * rows : (t + 1) * rows], "shard", [(k, (k - t) % n) for k in range(n)]) for t in range(1, n)
    ]
    put(*got)
    return functools.reduce(lambda a, c: a + c.astype(F32), got, x[:rows].astype(F32))


def in_order(blocks):
    n, i = lax.axis_size("shard"), lax.axis_index("shard")
    return [pick(i, [blocks[(m - j) % n] for m in range(n)]) for j in range(n)]


def pick(i, cases):
    out = cases[0]
    for m in range(1, len(cases)):
        out = jnp.where(i == m, cases[m], out)
    return out


def swap_z(parts, name="swap"):
    n, i = lax.axis_size("shard"), lax.axis_index("shard")
    SCOPE[0] = name
    parts = now(parts)
    out = [lax.dynamic_index_in_dim(parts, i, 0, False)]
    for t in range(1, n):
        block = lax.dynamic_index_in_dim(parts, (i + t) % n, 0, False)
        out.append(permute(block, "shard", [(k, (k + t) % n) for k in range(n)]))
    put(*out[1:])
    return out


def scatter_small(p):
    return functools.reduce(lambda a, c: a + c, [part.astype(F32) for part in swap_z(p)])


class SwappedRows:
    def __init__(self, name, pieces):
        self.name, self.pieces = name, pieces
        self.blocks = {0: self.part(lax.axis_index("shard"))}

    def part(self, d):
        n, size, g = lax.axis_size("shard"), lax.axis_size("grp"), lax.axis_index("grp")
        rows = self.pieces[0].shape[0] // size
        cut = []
        for w in self.pieces:
            cols = w.shape[1] // n
            cut.append(lax.dynamic_slice(w, (g * rows, d * cols), (rows, cols)))
        return jnp.concatenate(cut, axis=1) if len(cut) > 1 else cut[0]

    def step(self, *distances):
        SCOPE[0] = self.name
        n, i = lax.axis_size("shard"), lax.axis_index("shard")
        for t in distances:
            if 0 < t < n:
                block = now(self.part((i + t) % n))
                self.blocks[t] = permute(block, "shard", [(k, (k + t) % n) for k in range(n)])
                put(self.blocks[t])

    def result(self):
        n = lax.axis_size("shard")
        self.step(*[t for t in range(1, n) if t not in self.blocks])
        return jnp.stack(in_order([now(self.blocks[t]) for t in range(n)]))


def all_rows(part):
    n, rows, cols = part.shape
    return lax.all_gather(part, "grp", axis=1).reshape(n * lax.axis_size("grp") * rows, cols)


class Halves:
    def __init__(self, name, pairs, x_dim, y_dim, by_rows):
        self.name = name
        self.args = (pairs, x_dim, y_dim, by_rows)

    def half(self, which, **more):
        (x, y), *rest = self.args[0]
        which = jnp.stack([which]).astype(jnp.int32)
        return weight_grad([(beside(x), y)] + rest, *self.args[1:], which, **more)

    def send(self):
        self.sent = self.half(1 - lax.axis_index("grp") % 2)
        put(self.sent)

    def core(self):
        SCOPE[0] = self.name + "core"
        size = lax.axis_size("grp")
        self.come = permute(now(self.sent), "grp", [(k, k ^ 1) for k in range(size)])
        put(self.come)

    def keep(self):
        self.value = self.half(lax.axis_index("grp") % 2, add=self.come)
        put(self.value)

    def finish(self):
        size = lax.axis_size("grp")
        flat = now(self.value).reshape((-1,) + self.value.shape[2:])
        alike = [[k for k in range(size) if k % 2 == c] for c in range(2)]
        return lax.psum_scatter(flat, "grp", scatter_dimension=0, axis_index_groups=alike, tiled=True)


def column_grads(part, widths):
    n, size = lax.axis_size("shard"), lax.axis_size("grp")
    rows = part.shape[1]
    pieces, start = [], 0
    for group in widths:
        cols = []
        for width in group:
            cols.append(jnp.swapaxes(part[:, :, start : start + width], 0, 1).reshape(rows, n * width))
            start += width
        whole = jnp.concatenate(cols, axis=1) if len(cols) > 1 else cols[0]
        pieces.append(whole.reshape(rows, size, -1))
    moved = jnp.concatenate(pieces, axis=2) if len(pieces) > 1 else pieces[0]
    moved = lax.all_to_all(moved.reshape(rows, -1), "grp", 1, 0, tiled=True)
    moved = jnp.swapaxes(moved.reshape(size // 2, 2, rows, -1), 0, 1).reshape(size * rows, -1)
    outs, start = [], 0
    for piece in pieces:
        outs.append(moved[:, start : start + piece.shape[2]].astype(F32))
        start += piece.shape[2]
    return outs


def group_sum(x):
    SCOPE[0] = "groupsum"
    size = lax.axis_size("grp")
    step = 1
    while step < size:
        got = lax.ppermute(x, "grp", [(k, k ^ step) for k in range(size)])
        x = (x.astype(F32) + got.astype(F32)).astype(BF)
        step *= 2
    return x.astype(F32)


def norm_scale(h):
    return lax.rsqrt(jnp.mean(h * h, axis=-1, keepdims=True) + EPS)


def norm_back(h, gain, gn):
    r = norm_scale(h)
    g = gn * gain
    grad = r * g - h * (r * r * r) * jnp.mean(g * h, axis=-1, keepdims=True)
    return grad, jnp.sum(gn * h * r, axis=0)


def body(
    tokens,
    cotangent,
    sequence_lengths,
    attention_norm_gain,
    query_matrix,
    key_value_matrix,
    output_matrix,
    adapter_down_maps,
    adapter_up_query,
    adapter_up_key_value,
    adapter_down_output,
    adapter_up_output,
    query_feature_matrices,
    key_feature_matrices,
    feedforward_norm_gain,
    gate_matrix,
    up_matrix,
    down_matrix,
):
    n, shard, size = lax.axis_size("shard"), lax.axis_index("shard"), lax.axis_size("grp")
    batches, _, rows, width = tokens.shape
    length = n * rows
    share = width // n
    nq, hd = query_feature_matrices.shape[:2]
    nk = key_feature_matrices.shape[0]
    rank = adapter_up_query.shape[0]
    qw, kw = nq * hd, nk * hd
    ffq = down_matrix.shape[0]

    small = jnp.concatenate(
        [
            attention_norm_gain[None],
            feedforward_norm_gain[None],
            adapter_up_output,
            adapter_down_maps.T,
        ],
        axis=0,
    )
    half_kv = key_value_matrix.shape[1] // 2
    ends = jnp.cumsum(sequence_lengths[:, 0], axis=1)
    last = sequence_lengths.shape[2] - 2
    own = shard * rows + jnp.arange(rows, dtype=jnp.int32)
    gm_own = [jnp.where((own < ends[b, last])[:, None], cotangent[b, 0], 0) for b in range(batches)]
    me = jnp.stack([shard, jnp.int32(n), jnp.int32(rows // QB)]).astype(jnp.int32)
    Clock.before, Clock.here, Clock.sent = [], [], []
    tok = [Gather(tokens[b, 0], f"tok{b}x") for b in range(batches)]
    cot0 = Gather(gm_own[0], "cot0x")
    s_qkv = SwappedRows("sqkv", [query_matrix, key_value_matrix[:, :half_kv], key_value_matrix[:, half_kv:]])
    s_qkv.step(*range(1, n))
    tok[0].step()
    tick()
    w_qkv = all_rows(s_qkv.result())
    small_full = jnp.concatenate(in_order(gather_small(small)), axis=1)
    gain_attn = small_full[0].astype(F32)
    gain_ffn = small_full[1].astype(F32)
    up_output = small_full[2 : 2 + rank]
    down_maps_t = small_full[2 + rank :]
    tok[0].step()
    tick()
    tok[0].last()
    tick()
    tok[1].step()
    s_both = SwappedRows("sgu", [gate_matrix, up_matrix])
    s_both.step(1)
    pad = jnp.zeros((qw, -rank % 128), BF)
    out_wide = jnp.concatenate([output_matrix, adapter_down_output, pad], axis=1)
    zero = jnp.zeros
    u_all = jnp.concatenate(
        [
            jnp.concatenate([adapter_up_query, zero((rank, 2 * kw), BF)], axis=1),
            jnp.concatenate([zero((rank, qw), BF), adapter_up_key_value[0], zero((rank, kw), BF)], axis=1),
            jnp.concatenate([zero((rank, qw + kw), BF), adapter_up_key_value[1]], axis=1),
        ],
        axis=0,
    )

    begins = ends - sequence_lengths[:, 0]
    where = jnp.arange(length, dtype=jnp.int32)
    docs = jnp.sum((where[None, :, None] >= ends[:, None, :]).astype(jnp.int32), axis=2)
    relative = where[None] - jnp.max(
        jnp.where(where[None, :, None] >= begins[:, None, :], begins[:, None, :], 0), axis=2
    )
    freq = ROPE_BASE ** (-jnp.arange(hd // 2, dtype=F32) / (hd // 2))
    angles = freq[None, :, None] * relative.astype(F32)[:, None, :]
    cos_all, sin_all = jnp.cos(angles), jnp.sin(angles)

    def doubled(f):
        return jnp.swapaxes(jnp.concatenate([f, -f], axis=2), 1, 2)

    fq2, fk2 = doubled(query_feature_matrices), doubled(key_feature_matrices)

    def attention(b):
        x = beside(tok[b].result()).astype(F32)
        normed = (x * norm_scale(x) * gain_attn).astype(BF)
        mid = nt(normed, down_maps_t).astype(BF)
        proj = lax.dot_general(w_qkv, normed, (((0,), (1,)), ((), ())), preferred_element_type=F32)
        proj = proj + lax.dot_general(u_all, mid, (((0,), (1,)), ((), ())), preferred_element_type=F32)
        place = (
            cos_all[b],
            sin_all[b],
            docs[b][None],
            jnp.broadcast_to(docs[b][:, None], (length, QB)),
        )
        qt, kt, vt, pq, pk, att, ctx, m, den = attn_fwd(me, proj, *place, fq2, fk2)
        branch = tn(ctx, out_wide).astype(BF)
        put(branch)
        return dict(normed=normed, mid=mid, saved=(qt, kt, vt, pq, pk, att, m, den), ctx=ctx, place=place,
                    branch=Scatter(branch, f"br{b}x"))

    def after_attention(b):
        k = keep[b]
        branch = k["branch"].result()
        lora_own = branch[:, width : width + rank].astype(BF)
        x_own = tokens[b, 0].astype(F32)
        hidden = x_own + branch[:, :width] + nn(lora_own, up_output)
        normed_own = (hidden * norm_scale(hidden) * gain_ffn).astype(BF)
        k.update(lora=lora_own, x=x_own, hidden=hidden, send=Gather(normed_own, f"nf{b}x"))

    def ffn(b, cot):
        k = keep[b]
        nf = k["send"].result()
        out, back, product, dgate, dup = ffn_both(beside(nf), cot, w_both, down_matrix)
        put(dup)
        k.update(nf=nf, gm=cot, out=out, back=back, product=product, dgate=dgate, dup=dup)

    def after_ffn(b, gnf):
        k = keep[b]
        back, ffn_gain = norm_back(k["hidden"], gain_ffn, gnf)
        grad_hidden = gm_own[b].astype(F32) + back
        gb_own = grad_hidden.astype(BF)
        k.update(grad_hidden=grad_hidden, gb_own=gb_own, send=Gather(gb_own, f"gb{b}x"), ffn_gain=ffn_gain)

    def attention_back(b):
        k = keep[b]
        gb = beside(k["send"].result())
        glo = nt(gb, up_output)
        gctx = nt(output_matrix, gb) + nt(adapter_down_output.astype(F32), glo)
        dq, dk, dv, dfq, dfk = attn_bwd(
            me, k["saved"], gctx.astype(BF), *k["place"], query_feature_matrices, key_feature_matrices
        )
        dqkv = jnp.concatenate([dq, dk, dv], axis=0)
        glm = tn(dqkv, u_all.T)
        gn = lax.dot_general(dqkv, w_qkv, (((0,), (1,)), ((), ())), preferred_element_type=F32)
        gn = (gn + nn(glm, down_maps_t.astype(F32))).astype(BF)
        put(gn)
        k.update(gb=gb, glo=glo, dqkv=dqkv, glm=glm, dfq=dfq, dfk=dfk, gn=Scatter(gn, f"gn{b}x"))

    def pairs(one, two):
        return [(k[one], k[two]) for k in keep]

    tick()
    tok[1].step()
    s_both.step(n - 1)
    keep = [attention(0)]
    tick()
    s_both.step(*range(2, n - 1))
    keep[0]["branch"].step()
    tok[1].last()
    tick()
    w_both = all_rows(s_both.result())
    keep[0]["branch"].step()
    tick()
    keep[0]["branch"].last()
    keep.append(attention(1))
    tick()
    after_attention(0)
    keep[0]["send"].step()
    tick()
    keep[0]["send"].step()
    keep[1]["branch"].step()
    tick()
    keep[0]["send"].last()
    keep[1]["branch"].step()
    tick()
    keep[1]["branch"].last()
    cot0.step()
    tick()
    after_attention(1)
    keep[1]["send"].step()
    cot0.step()
    tick()
    keep[1]["send"].step()
    cot0.last()
    tick()
    keep[1]["send"].last()
    cot1 = gather_direct(gm_own[1], "cot1x")
    ffn(0, cot0.result())
    tick()
    gnf0 = scatter_direct(keep[0]["back"], "gnf0x")
    ffn(1, jnp.concatenate([now(c) for c in cot1]))
    tick()
    w_g = Halves("Wg", pairs("nf", "dgate"), 0, 0, True)
    w_u = Halves("Wu", pairs("nf", "dup"), 0, 0, True)
    w_d = Halves("Wd", pairs("product", "gm"), 0, 0, False)
    gnf1 = Scatter(keep[1]["back"], "gnf1x")
    out = [Scatter(k["out"], f"out{b}x") for b, k in enumerate(keep)]
    after_ffn(0, gnf0)
    keep[0]["send"].step()
    out[0].step()
    w_g.send()
    w_u.send()
    tick()
    keep[0]["send"].step()
    gnf1.step()
    w_g.core()
    w_d.send()
    tick()
    keep[0]["send"].last()
    gnf1.step()
    w_u.core()
    w_g.keep()
    tick()
    r_g = w_g.finish()
    gnf1.last()
    out[0].step()
    w_d.core()
    attention_back(0)
    tick()
    after_ffn(1, gnf1.result())
    keep[1]["send"].step()
    out[0].last()
    w_u.keep()
    tick()
    r_u = w_u.finish()
    keep[1]["send"].step()
    keep[0]["gn"].step()
    w_d.keep()
    tick()
    r_d = w_d.finish()
    keep[1]["send"].last()
    keep[0]["gn"].step()
    put(r_g)
    tick()
    keep[0]["gn"].last()
    t_g = swap_z(r_g.reshape(n, -1, ffq), "swapg")
    attention_back(1)
    w_q = Halves("Wq", pairs("normed", "dqkv"), 0, 1, True)
    w_o = Halves("Wo", pairs("ctx", "gb"), 1, 0, False)
    w_q.send()
    w_o.send()
    tick()
    keep[1]["gn"].step()
    out[1].step()
    w_q.core()
    w_o.core()
    put(r_u)
    tick()
    keep[1]["gn"].step()
    out[1].step()
    w_q.keep()
    w_o.keep()
    put(r_d)
    tick()
    r_q = w_q.finish()
    r_o = w_o.finish()
    keep[1]["gn"].last()
    t_u = swap_z(r_u.reshape(n, -1, ffq), "swapu")
    (grad_gate,) = column_grads(jnp.stack(in_order([now(t) for t in t_g])), [[ffq]])
    tick()
    (grad_up,) = column_grads(jnp.stack(in_order([now(t) for t in t_u])), [[ffq]])
    out[1].last()
    for k in keep:
        k["gn_sum"] = now(k["gn"].result())
    for k in keep:
        k["up_out"] = tn(k["lora"], k["gb_own"])
    token_grads = []
    for k in keep:
        back, attn_gain = norm_back(k["x"], gain_attn, k["gn_sum"])
        token_grads.append((k["grad_hidden"] + back).astype(BF))
        k.update(attn_gain=attn_gain)

    def both(name, axis=0):
        return jnp.concatenate([k[name] for k in keep], axis=axis)

    def added(name):
        return functools.reduce(lambda a, c: a + c, [k[name] for k in keep])

    normed = both("normed")
    ctx = both("ctx", 1)
    dqkv = both("dqkv", 1)
    glm = both("glm")
    down_maps_grad = tn(normed.astype(F32), glm)
    ups = lax.dot_general(both("mid"), dqkv, (((0,), (1,)), ((), ())), preferred_element_type=F32)
    down_out_grad = nn(ctx.astype(F32), both("glo"))
    spread = [
        added("attn_gain").reshape(n, share),
        added("ffn_gain").reshape(n, share),
        down_maps_grad.reshape(n, share * 3 * rank),
        jnp.swapaxes(added("up_out").reshape(rank, n, share), 0, 1).reshape(n, rank * share),
    ]
    lined = scatter_small(jnp.concatenate(spread, axis=1).astype(BF))
    local = [
        ups[:rank, :qw].reshape(-1),
        ups[rank : 2 * rank, qw : qw + kw].reshape(-1),
        ups[2 * rank :, qw + kw :].reshape(-1),
        down_out_grad.reshape(-1),
        added("dfq").reshape(-1),
        added("dfk").reshape(-1),
    ]
    t_q = jnp.stack(in_order(swap_z(r_q.reshape(n, -1, qw + 2 * kw), "swapq")))
    grad_query, grad_kv = column_grads(t_q, [[qw], [kw, kw]])
    grad_down = r_d.astype(F32)
    grad_output = r_o.astype(F32)
    output = [(k["hidden"] + o.result()).astype(BF) for k, o in zip(keep, out)]
    flat = group_sum(beside(jnp.concatenate([lined] + local).astype(BF)))
    shapes = [
        (share,),
        (share,),
        (share, 3 * rank),
        (rank, share),
        (rank, qw),
        (rank, kw),
        (rank, kw),
        (qw, rank),
        (nq, hd, hd),
        (nk, hd, hd),
    ]
    got, start = [], 0
    for shape in shapes:
        count = 1
        for extent in shape:
            count *= extent
        got.append(flat[start : start + count].reshape(shape))
        start += count
    g_attn, g_ffn, g_down_maps, g_up_out, g_up_q, g_up_k, g_up_v, g_down_out, g_fq, g_fk = got
    return (
        jnp.stack(output)[:, None],
        jnp.stack(token_grads)[:, None],
        g_attn,
        grad_query,
        grad_kv,
        grad_output,
        g_down_maps,
        g_up_q,
        jnp.stack([g_up_k, g_up_v]),
        g_down_out,
        g_up_out,
        g_fq,
        g_fk,
        g_ffn,
        grad_gate,
        grad_up,
        grad_down,
    )


def solution(mesh):
    placed = (
        P(None, "grp", "shard", None),
        P(None, "grp", "shard", None),
        P(None, "grp", None),
        P("shard"),
        P("shard", None),
        P("shard", None),
        P("shard", None),
        P("shard", None),
        P(None, "shard"),
        P(None, None, "shard"),
        P("shard", None),
        P(None, "shard"),
        P("shard", None, None),
        P("shard", None, None),
        P("shard"),
        P("shard", None),
        P("shard", None),
        P("shard", None),
    )
    return jax.shard_map(
        body,
        mesh=mesh,
        in_specs=placed,
        out_specs=(
            P(None, "grp", "shard", None),
            P(None, "grp", "shard", None),
            P("shard"),
            P("shard", "grp"),
            P("shard", "grp"),
            P("shard", "grp"),
            P("shard", None),
            P(None, "shard"),
            P(None, None, "shard"),
            P("shard", None),
            P(None, "shard"),
            P("shard", None, None),
            P("shard", None, None),
            P("shard"),
            P("shard", "grp"),
            P("shard", "grp"),
            P("shard", "grp"),
        ),
        check_vma=False,
    )
```
